32 devices in a mesh: dp: 16 (over z, y, x), tensor: 2 (over core).
Axes of the slice: x: 2, y: 2, z: 4, core: 2. Of those that a mesh axis runs over, the one named last changes fastest.
Arguments:
- hidden_in: bfloat16 [4096, 2048], P(('dp', 'tensor')), may hold values from -6 to 6
- segments: int32 [16, 256], P('dp'), may hold values from 0 to 3, never falling along the last dimension, each value on 1 to 128 neighbouring positions
- mix_weights: bfloat16 [2048, 4, 2048], P('dp', None, 'tensor'), may hold values from -0.125 to 0.125
- ffn_weights: bfloat16 [2048, 3, 5632], P('dp', None, 'tensor'), may hold values from -0.125 to 0.125
- norm1_gain: float32 [2048], replicated, may hold values from 0.25 to 1.75
- norm2_gain: float32 [2048], replicated, may hold values from 0.25 to 1.75
- head_gain: float32 [128], replicated, may hold values from 0.25 to 1.75
- lower_bound: float32 [2048], P('tensor'), may hold values from 0.05 to 0.97
- out_grad: bfloat16 [4096, 2048], P(('dp', 'tensor')), may hold values from -6 to 6
Outputs:
- block_out: bfloat16 [4096, 2048], P(('dp', 'tensor'))
- input_grad: float32 [4096, 2048], P(('dp', 'tensor'))
- mix_weights_grad: float32 [2048, 4, 2048], P('dp', None, 'tensor')
- ffn_weights_grad: float32 [2048, 3, 5632], P('dp', None, 'tensor')
- norm1_gain_grad: float32 [2048], replicated
- norm2_gain_grad: float32 [2048], replicated
- head_gain_grad: float32 [128], replicated
- lower_bound_grad: float32 [2048], replicated
The draws below stay inside these ranges and needn't reach their ends.
Inputs may be any that keep to these rules, and one draw needn't show every extreme that they name: `segments`: along each sequence the numbers never fall; each of the 4 documents of a sequence is a run of 1 to 128 tokens, and one run is exactly 128 long.
All inputs are finite; a program needn't handle non-finite values.
Results may differ from the reference program's by a relative error of at most 0.0085.
Values may be sent and summed in bfloat16 or wider, within the bound.
No kernel may reach another device: no remote copies, remote signals or barrier semaphores. Data moves between devices by JAX's collectives and lax.ppermute only.
A program may use at most 320 MiB of HBM per device.

```python
import math
import jax
import jax.numpy as jnp
import numpy as np
from jax import lax

D = 2048
HEAD_DIM = 128
FF = 5632
LEN = 256
SPAN = 64
HK = 2048
SEQS = 16
TOKENS = 4096
DOCS = 4
DOC_MOST = 128


def spiked(entries, rng, source, target, parts, factor):
    owner, partner = [(jnp.arange(entries.shape[dim]) // (entries.shape[dim] // parts)).reshape([-1 if axis == dim else 1 for axis in range(entries.ndim)]) for dim in (source, target)]
    chosen = jax.random.permutation(rng, parts)[partner]
    strong = (owner == chosen) | (owner == (partner + parts // 2) % parts)
    return jnp.where(strong, factor * entries, entries)


def level_of(stream_key, shape, pieces, smallest, top_value):
    loudness = 1.0
    for dim, shards_of in pieces:
        draws = jax.random.uniform(jax.random.fold_in(jax.random.fold_in(stream_key, 6), dim), (shards_of,), jnp.float32, smallest / len(pieces), top_value / len(pieces))
        loudness = loudness * jnp.repeat(jnp.exp(draws), shape[dim] // shards_of).reshape((-1,) + (1,) * (len(shape) - 1 - dim))
    return loudness


def split_up(amount, total, reach, slope):
    loads = [(1 << 20) // math.isqrt(standing ** slope) + 1 for standing in range(2, amount + 1)]
    spare, given = total - reach - (amount - 1), [1] * (amount - 1)
    while spare > 0:
        free = [i for i in range(amount - 1) if given[i] < reach]
        pool, remaining = sum([loads[i] for i in free]), spare
        for i in free:
            extra = min(reach - given[i], max(1, remaining * loads[i] // pool), spare)
            given[i] = given[i] + extra
            spare = spare - extra
    return np.array([reach] + given)


def uneven(key, count, total, reach, skew):
    if count == 2:
        one = jax.random.randint(key, (), max(1, total - reach), min(reach, total - 1) + 1)
        return jnp.stack([one, total - one])
    sizes = jnp.asarray(split_up(count, total, reach, skew), jnp.int32)
    couples = (count - 1) // 2
    giver, taker = sizes[1:1 + 2 * couples:2], sizes[2:2 + 2 * couples:2]
    room = jnp.minimum(giver - 1, reach - taker)
    moved = jax.random.randint(jax.random.fold_in(key, 1), (couples,), 0, 1 << 20) % (room + 1)
    sizes = sizes.at[1:1 + 2 * couples:2].set(giver - moved).at[2:2 + 2 * couples:2].set(taker + moved)
    return sizes[jax.random.permutation(jax.random.fold_in(key, 2), count)]


def centred(key, dims, deviation, limit, shards=(), kind=jnp.bfloat16):
    factor_of = level_of(key, dims, shards, -0.22, 0.18) if shards else 1.0
    values = jax.random.normal(key, dims, jnp.float32) * deviation * factor_of
    return jnp.minimum(jnp.maximum(values, -limit), limit).astype(kind)


def bell_draw_with(key, dims, width, bound, cuts, heavy, kind=jnp.bfloat16):
    values = width * jax.random.normal(key, dims, jnp.float32)
    if cuts:
        values = values * level_of(key, dims, cuts, -0.22, 0.18)
    return jnp.clip(spiked(values, jax.random.fold_in(key, 3), *heavy), -bound, bound).astype(kind)


def setup_inputs(seed: int = 0) -> dict:
    keys = jax.random.split(jax.random.key(seed), 10)
    hidden_in = bell_draw_with(keys[0], (TOKENS, D), 1.0, 6.0, ((0, 32),), (0, 1, 32, 2.75))
    segments = jax.vmap(lambda own: jnp.searchsorted(jnp.cumsum(uneven(own, DOCS, LEN, DOC_MOST, 1)), jnp.arange(LEN), side="right"))(jax.random.split(keys[1], SEQS)).reshape((SEQS, LEN)).astype(jnp.int32)
    mix_weights = centred(keys[2], (D, 4, HK), D ** -0.5, 0.125, ((0, 16), (2, 2)))
    ffn_weights = centred(keys[3], (D, 3, FF), D ** -0.5, 0.125, ((0, 16), (2, 2)))
    norm1_gain = jnp.clip(1.0 + 0.15 * jax.random.normal(keys[4], (D,), jnp.float32), 0.25, 1.75)
    norm2_gain = jnp.clip(1.0 + 0.15 * jax.random.normal(keys[5], (D,), jnp.float32), 0.25, 1.75)
    head_gain = jnp.clip(1.0 + 0.15 * jax.random.normal(keys[6], (HEAD_DIM,), jnp.float32), 0.25, 1.75)
    lower_bound = jnp.clip(0.05 + 0.92 * jax.random.uniform(keys[7], (HK,), jnp.float32) ** level_of(keys[7], (HK,), ((0, 2),), -0.2, 0.2), 0.05, 0.97)
    out_grad = bell_draw_with(keys[8], (TOKENS, D), 1.0, 6.0, ((0, 32),), (0, 1, 32, 2.75))
    return {"hidden_in": hidden_in, "segments": segments, "mix_weights": mix_weights, "ffn_weights": ffn_weights, "norm1_gain": norm1_gain, "norm2_gain": norm2_gain, "head_gain": head_gain, "lower_bound": lower_bound, "out_grad": out_grad}


@jax.custom_vjp
def low(v):
    return lax.optimization_barrier(v.astype(jnp.bfloat16)).astype(jnp.float32)

@jax.custom_vjp
def low_back(v):
    return v

def low_keep(v):
    return (low(v), None)

def low_pass(kept, grad):
    return (grad,)

def back_keep(v):
    return (v, None)

def back_low(kept, grad):
    return (low(grad),)
low.defvjp(low_keep, low_pass)
low_back.defvjp(back_keep, back_low)
epsilon = 1e-06
peak_value = lax.Precision.HIGHEST

def rms_norm(values, scales):
    return values * lax.rsqrt(lax.optimization_barrier(jnp.mean(values * values, axis=-1, keepdims=True)) + epsilon) * scales

def block_step(carried, inputs):
    running_state, last_seen = carried
    query_rows, incoming_keys, incoming_values, log_decay, labels = inputs
    float_kind = query_rows.dtype
    block_len = labels.shape[0]
    grand_totals = jnp.cumsum(log_decay, axis=1)
    position = jnp.arange(block_len, dtype=jnp.int32)
    allowed = (labels[:, None] == labels[None, :]) & (position[:, None] >= position[None, :])
    allowed_full = allowed[None, :, :, None]
    spread_log = grand_totals[:, :, None, :] - grand_totals[:, None, :, :]
    weights_in = jnp.exp(jnp.where(allowed_full, spread_log, 0.0)) * allowed_full.astype(float_kind)
    scores = lax.optimization_barrier(jnp.sum(query_rows[:, :, None, :] * incoming_keys[:, None, :, :] * weights_in, axis=-1))
    inside = jnp.einsum('hts,hsv->htv', scores, incoming_values, precision=peak_value)
    joined_rows = (labels == last_seen).astype(float_kind)
    external_part = jnp.einsum('ewy,eyi->ewi', query_rows * jnp.exp(grand_totals), running_state, precision=peak_value) * joined_rows[None, :, None]
    final_log = grand_totals[:, -1:, :]
    same_last = (labels == labels[-1])[None, :, None]
    toward_final = jnp.exp(jnp.where(same_last, final_log - grand_totals, 0.0)) * same_last.astype(float_kind)
    renewed_sum = jnp.einsum('rfj,rfe->rje', incoming_keys * toward_final, incoming_values, precision=peak_value)
    survive = (labels[-1] == last_seen).astype(float_kind)
    running_state = running_state * jnp.exp(final_log[:, 0, :])[:, :, None] * survive + renewed_sum
    return ((running_state, labels[-1]), inside + external_part)

def mixer_core(projected, floor_gate, head_scale, labels):
    labels = labels.astype(jnp.int32)
    length = projected.shape[0]
    size_head = head_scale.shape[0]
    count_heads = projected.shape[2] // size_head
    query_rows = jax.nn.silu(projected[:, 0])
    forget = floor_gate + (1.0 - floor_gate) * jax.nn.sigmoid(projected[:, 1])
    incoming_keys = 1.0 - forget
    log_decay = jnp.log(forget)
    incoming_values = projected[:, 2]
    blocks_count = length // SPAN

    def arrange(source):
        return source.reshape(blocks_count, SPAN, count_heads, size_head).transpose(0, 2, 1, 3)
    inputs = (arrange(query_rows), arrange(incoming_keys), arrange(incoming_values), arrange(log_decay), labels.reshape(blocks_count, SPAN))
    initial = (jnp.zeros((count_heads, size_head, size_head), projected.dtype), jnp.asarray(-1, jnp.int32))
    _, produced = lax.scan(jax.checkpoint(block_step), initial, inputs)
    recurrent = produced.transpose(0, 2, 1, 3).reshape(length, count_heads, size_head)
    return rms_norm(recurrent, head_scale).reshape(length, count_heads * size_head)

def reference(hidden_in, segments, mix_weights, ffn_weights, norm1_gain, norm2_gain, head_gain, lower_bound, out_grad):
    labels_all = segments.astype(jnp.int32)

    def forward(hidden, mixing, feeding, gain_first, gain_second, gain_head, floor_gate):
        normed = low(rms_norm(hidden, gain_first))
        projected = low_back(jnp.einsum('td,dkx->tkx', normed, mixing[:, :3], precision=peak_value))
        grouped = projected.reshape(SEQS, LEN, 3, HK)

        def per_sequence(sequence_item):
            return mixer_core(sequence_item[0], floor_gate, gain_head, sequence_item[1])
        mixed_out = lax.map(jax.checkpoint(per_sequence), (grouped, labels_all))
        mixed_out = low(mixed_out.reshape(TOKENS, HK))
        branch = low_back(jnp.einsum('tx,dx->td', mixed_out, mixing[:, 3], precision=peak_value))
        middle = hidden + branch
        normed_two = low(rms_norm(middle, gain_second))
        gate_up = low_back(jnp.einsum('td,dkx->tkx', normed_two, feeding[:, :2], precision=peak_value))
        active = low(jax.nn.silu(gate_up[:, 0]) * gate_up[:, 1])
        branch_two = low_back(jnp.einsum('tx,dx->td', active, feeding[:, 2], precision=peak_value))
        return middle + branch_two
    result, pullback = jax.vjp(forward, hidden_in.astype(jnp.float32), mix_weights.astype(jnp.float32), ffn_weights.astype(jnp.float32), norm1_gain, norm2_gain, head_gain, lower_bound)
    gradients = pullback(out_grad.astype(jnp.float32))
    return (result.astype(jnp.bfloat16), gradients[0], gradients[1], gradients[2], gradients[3], gradients[4], gradients[5], gradients[6])
```

```python
import jax
import jax.numpy as jnp
from jax import lax
from jax.experimental import pallas as pl
from jax.experimental.pallas import tpu as pltpu
from jax.sharding import PartitionSpec as P

HEAD = 128
STRIP = 32
CAP = 50.0
epsilon = 1e-06


def dot(a, b, dims):
    return lax.dot_general(a, b, (dims, ((), ())), preferred_element_type=jnp.float32)


def exact_dot(ones, values):
    high = values.astype(jnp.bfloat16)
    rest = values - high.astype(jnp.float32)
    mid = rest.astype(jnp.bfloat16)
    tail = (rest - mid.astype(jnp.float32)).astype(jnp.bfloat16)
    dims = ((1,), (0,))
    return dot(ones, high, dims) + dot(ones, mid, dims) + dot(ones, tail, dims)


def gates(p0, p1, floor):
    swish = jax.nn.sigmoid(p0)
    gate = jax.nn.sigmoid(p1)
    forget = floor + (1.0 - floor) * gate
    return swish, gate, forget


def masks(seg_col, seg_row, length):
    row = lax.broadcasted_iota(jnp.int32, (length, length), 0)
    col = lax.broadcasted_iota(jnp.int32, (length, length), 1)
    same = seg_col == seg_row
    return same, row, col


def strips(length):
    out = []
    for start in range(0, length, STRIP):
        out.append((start, -(-(start + STRIP) // 128) * 128))
    return out


def fill_scores(length, query, key, totals, allowed, scores, keep=None):
    for start, wide in strips(length):
        rows = slice(start, start + STRIP)
        ref = totals[start + STRIP // 2 - 1 : start + STRIP // 2]
        lead = (query[rows] * jnp.exp(totals[rows] - ref)).astype(jnp.bfloat16)
        trail = (key[:wide] * jnp.exp(jnp.minimum(ref - totals[:wide], CAP))).astype(jnp.bfloat16)
        part = dot(lead, trail, ((1,), (1,)))
        part = jnp.where(allowed[rows, :wide], part, 0.0)
        scores[rows, :wide] = part.astype(jnp.bfloat16)
        if wide < length:
            scores[rows, wide:] = jnp.zeros((STRIP, length - wide), jnp.bfloat16)


def forward_kernel(p0_ref, p1_ref, p2_ref, col_ref, row_ref, floor_ref, gain_ref, out_ref, scores):
    length = p0_ref.shape[0]
    p0 = p0_ref[...]
    swish, gate, forget = gates(p0, p1_ref[...], floor_ref[...])
    same, row, col = masks(col_ref[0], row_ref[0], length)
    tri = (col <= row).astype(jnp.bfloat16)
    totals = exact_dot(tri, jnp.log(forget))
    fill_scores(length, p0 * swish, 1.0 - forget, totals, same & (col <= row), scores)
    rec = dot(scores[...], p2_ref[...].astype(jnp.bfloat16), ((1,), (0,)))
    rms = lax.rsqrt(jnp.mean(rec * rec, axis=-1, keepdims=True) + epsilon)
    out_ref[...] = (rec * rms * gain_ref[...]).astype(jnp.bfloat16)


def backward_kernel(
    p0_ref, p1_ref, p2_ref, grad_ref, col_ref, row_ref, floor_ref, gain_ref,
    g0_ref, g1_ref, g2_ref, floor_grad_ref, gain_grad_ref,
    scores, key_grad, decay_grad, query_grad,
):
    length = p0_ref.shape[0]
    bf = jnp.bfloat16
    p0 = p0_ref[...]
    floor = floor_ref[...]
    swish, gate, forget = gates(p0, p1_ref[...], floor)
    query = p0 * swish
    key = 1.0 - forget
    same, row, col = masks(col_ref[0], row_ref[0], length)
    allowed = same & (col <= row)
    tri = (col <= row).astype(bf)
    totals = exact_dot(tri, jnp.log(forget))
    fill_scores(length, query, key, totals, allowed, scores)
    value = p2_ref[...].astype(bf)
    rec = dot(scores[...], value, ((1,), (0,)))
    rms = lax.rsqrt(jnp.mean(rec * rec, axis=-1, keepdims=True) + epsilon)
    mixed_grad = grad_ref[...]
    unit = rec * rms
    scaled = mixed_grad * gain_ref[...]
    rec_grad = rms * (scaled - unit * jnp.mean(scaled * unit, axis=-1, keepdims=True))
    rec_low = rec_grad.astype(bf)
    g2_ref[...] = dot(scores[...], rec_low, ((0,), (0,))).astype(bf)
    score_grad = jnp.where(allowed, dot(rec_low, value, ((1,), (1,))), 0.0).astype(bf)
    key_grad[...] = jnp.zeros_like(key_grad)
    decay_grad[...] = jnp.zeros_like(decay_grad)
    for start, wide in strips(length):
        rows = slice(start, start + STRIP)
        ref = totals[start + STRIP // 2 - 1 : start + STRIP // 2]
        lead_scale = jnp.exp(totals[rows] - ref)
        trail_scale = jnp.exp(jnp.minimum(ref - totals[:wide], CAP))
        lead = (query[rows] * lead_scale).astype(bf)
        trail = (key[:wide] * trail_scale).astype(bf)
        part = score_grad[rows, :wide]
        lead_grad = dot(part, trail, ((1,), (0,)))
        trail_grad = dot(part, lead, ((0,), (0,)))
        query_grad[rows, :] = lead_grad * lead_scale
        key_grad[:wide, :] += trail_grad * trail_scale
        decay_grad[:wide, :] -= trail_grad * trail.astype(jnp.float32)
        decay_grad[rows, :] += lead_grad * lead.astype(jnp.float32)
    joined = (row > 0) & same & (col >= row)
    seg_col = col_ref[0]
    before = jnp.concatenate([seg_col[:1] - 1, seg_col[:-1]], axis=0)
    carry = (seg_col == before).astype(jnp.float32)
    later = (same & (col >= row)).astype(bf)
    forget_grad = exact_dot(later, decay_grad[...]) * carry / forget
    joint = forget_grad - key_grad[...]
    floor_grad_ref[0] = jnp.broadcast_to(jnp.sum(joint * (1.0 - gate), axis=0, keepdims=True), (8, HEAD)) * 0.125
    gain_grad_ref[0] = jnp.broadcast_to(jnp.sum(mixed_grad * unit, axis=0, keepdims=True), (8, HEAD)) * 0.125
    g0_ref[...] = (query_grad[...] * swish * (1.0 + p0 * (1.0 - swish))).astype(bf)
    g1_ref[...] = (joint * (1.0 - floor) * gate * (1.0 - gate)).astype(bf)


def specs(length):
    tile = pl.BlockSpec((length, HEAD), lambda s, h: (s, h))
    col = pl.BlockSpec((1, length, 1), lambda s, h: (s, 0, 0))
    row = pl.BlockSpec((1, 1, length), lambda s, h: (s, 0, 0))
    floor = pl.BlockSpec((1, HEAD), lambda s, h: (0, h))
    gain = pl.BlockSpec((1, HEAD), lambda s, h: (0, 0))
    return tile, col, row, floor, gain


PARAMS = dict(vmem_limit_bytes=32 * 1024 * 1024)


def mixer_forward(p0, p1, p2, segments, floor, gain):
    count, length = segments.shape
    tile, col, row, floor_spec, gain_spec = specs(length)
    heads = p0.shape[1] // HEAD
    return pl.pallas_call(
        forward_kernel,
        grid=(count, heads),
        in_specs=[tile, tile, tile, col, row, floor_spec, gain_spec],
        out_specs=tile,
        out_shape=jax.ShapeDtypeStruct(p0.shape, jnp.bfloat16),
        scratch_shapes=[pltpu.VMEM((length, length), jnp.bfloat16)],
        compiler_params=pltpu.CompilerParams(**PARAMS),
        name="mixer_forward",
    )(p0, p1, p2, segments[:, :, None], segments[:, None, :], floor[None], gain[None])


def mixer_backward(p0, p1, p2, grad, segments, floor, gain):
    count, length = segments.shape
    tile, col, row, floor_spec, gain_spec = specs(length)
    heads = p0.shape[1] // HEAD
    small = pl.BlockSpec((1, 8, HEAD), lambda s, h: (s, 0, h))
    low = jax.ShapeDtypeStruct(p0.shape, jnp.bfloat16)
    sums = jax.ShapeDtypeStruct((count, 8, p0.shape[1]), jnp.float32)
    return pl.pallas_call(
        backward_kernel,
        grid=(count, heads),
        in_specs=[tile, tile, tile, tile, col, row, floor_spec, gain_spec],
        out_specs=[tile, tile, tile, small, small],
        out_shape=[low, low, low, sums, sums],
        scratch_shapes=[
            pltpu.VMEM((length, length), jnp.bfloat16),
            pltpu.VMEM((length, HEAD), jnp.float32),
            pltpu.VMEM((length, HEAD), jnp.float32),
            pltpu.VMEM((length, HEAD), jnp.float32),
        ],
        compiler_params=pltpu.CompilerParams(**PARAMS),
        name="mixer_backward",
    )(p0, p1, p2, grad, segments[:, :, None], segments[:, None, :], floor[None], gain[None])


MEMBERS = ((1, 1), (4, 2), (5, 3))
BF = jnp.bfloat16


def swap(values, bits):
    total = lax.axis_size("dp")
    return lax.ppermute(values, "dp", [(s, s ^ bits) for s in range(total)])


def shift(values, steps):
    total = lax.axis_size("dp")
    return lax.ppermute(values, "dp", [(s, (s + 8 * steps) % total) for s in range(total)])


def other_core(values):
    return lax.ppermute(values, "tensor", [(0, 1), (1, 0)])


def pick(values, index, axis=0):
    return lax.dynamic_index_in_dim(values, index, axis, keepdims=False)


def put(values, part, index, axis=0):
    return lax.dynamic_update_index_in_dim(values, part, index, axis)


def place():
    me = lax.axis_index("dp")
    x, y, z, high = me & 1, (me >> 1) & 1, (me >> 2) & 1, me >> 3
    return x, y, z, high, z * 2 + x


def gather_weight(local):
    _, y, _, high, member = place()
    highs = lax.axis_size("dp") // 8
    rows = local.shape[0]
    slices = local.reshape(rows, 4, -1).transpose(1, 0, 2)
    width = slices.shape[2]
    block = slices
    for bits, flip in MEMBERS:
        block = put(block, swap(pick(slices, member ^ flip), bits), member ^ flip)
    full = jnp.zeros((highs, 2, 2, 2, rows, width), local.dtype)

    def store(full, part, h, yy):
        return lax.dynamic_update_slice(
            full, part.reshape(1, 2, 1, 2, rows, width), (h, 0, yy, 0, 0, 0)
        )

    full = store(full, block, high, y)
    full = store(full, swap(block, 2), high, 1 - y)
    for k in range(1, highs):
        far = shift(block, k)
        full = store(full, far, (high - k) % highs, y)
        full = store(full, swap(far, 2), (high - k) % highs, 1 - y)
    return full.reshape(highs * 8 * rows, width)


def scatter_grad(tokens, grads):
    _, y, _, high, member = place()
    highs = lax.axis_size("dp") // 8
    rows = tokens.shape[1] // (8 * highs)
    width = grads.shape[1]
    split = tokens.reshape(tokens.shape[0], highs * 2, 2, 2 * rows)

    def half(yy):
        return jnp.einsum(
            "tad,tx->adx", pick(split, yy, 2), grads, preferred_element_type=jnp.float32
        ).reshape(highs, 4, rows, width)

    came = swap(half(1 - y).astype(BF), 2)
    total = half(y) + came.astype(jnp.float32)
    mine = pick(total, high)
    for k in range(1, highs):
        sent = pick(total, (high + k) % highs).astype(BF)
        mine = mine + shift(sent, k).astype(jnp.float32)
    out = mine
    for bits, flip in MEMBERS:
        got = swap(pick(mine, member ^ flip).astype(BF), bits)
        out = put(out, got.astype(jnp.float32), member ^ flip)
    return out.transpose(1, 0, 2).reshape(rows, 4 * width)


def gather_rows(rows):
    core = lax.axis_index("tensor")
    member = place()[4]
    column = jnp.zeros((4,) + rows.shape, rows.dtype)
    column = put(column, rows, member)
    for bits, flip in MEMBERS:
        column = put(column, swap(rows, bits), member ^ flip)
    full = jnp.zeros((4, 2) + rows.shape, rows.dtype)
    full = put(full, column, core, 1)
    return put(full, other_core(column), 1 - core, 1)


def scatter_rows(count, product, *sources):
    core = lax.axis_index("tensor")
    member = place()[4]
    split = [s.reshape(4, 2, count, s.shape[-1]) for s in sources]

    def half(which):
        return product(*[pick(s, which, 1).reshape(4 * count, -1) for s in split])

    came = other_core(half(1 - core).astype(BF))
    total = (half(core) + came.astype(jnp.float32)).reshape(4, count, -1)
    mine = pick(total, member)
    for bits, flip in MEMBERS:
        got = swap(pick(total, member ^ flip).astype(BF), bits)
        mine = mine + got.astype(jnp.float32)
    return mine


def sum_all(values):
    bits = 1
    while bits < lax.axis_size("dp"):
        values = values + swap(values, bits)
        bits *= 2
    return values + other_core(values)


def rms_of(values):
    return lax.rsqrt(jnp.mean(values * values, axis=-1, keepdims=True) + epsilon)


def norm_back(values, scale, gain, grad):
    unit = values * scale
    wide = grad * gain
    out = scale * (wide - unit * jnp.mean(wide * unit, axis=-1, keepdims=True))
    return out, jnp.sum(grad * unit, axis=0)


def mul(left, right):
    return lax.dot_general(left, right, (((1,), (0,)), ((), ())), preferred_element_type=jnp.float32)


def mul_back(left, right):
    return lax.dot_general(left, right, (((1,), (1,)), ((), ())), preferred_element_type=jnp.float32)


def body(
    hidden_in,
    segments,
    mix_weights,
    ffn_weights,
    norm1_gain,
    norm2_gain,
    head_gain,
    lower_bound,
    out_grad,
):
    core = lax.axis_index("tensor")
    member = place()[4]
    count, model = hidden_in.shape
    hidden = hidden_in.astype(jnp.float32)
    scale_one = rms_of(hidden)
    normed = (hidden * scale_one * norm1_gain).astype(BF)
    normed_full = gather_rows(normed).reshape(-1, model)
    labels = segments
    group_labels = jnp.zeros((4,) + labels.shape, labels.dtype)
    group_labels = put(group_labels, labels, member)
    for bits, flip in MEMBERS:
        group_labels = put(group_labels, swap(labels, bits), member ^ flip)
    group_labels = group_labels.reshape(-1, labels.shape[-1])
    quarter = lower_bound.shape[0] // 4
    floor = lax.dynamic_slice_in_dim(lower_bound, member * quarter, quarter)

    mix = [gather_weight(mix_weights[:, j]) for j in range(4)]
    projected = [mul(normed_full, mix[j]) for j in range(3)]
    mixed = mixer_forward(*projected, group_labels, floor, head_gain)
    middle = hidden + scatter_rows(count, lambda m: mul_back(m, mix[3]), mixed)

    ffn = [gather_weight(ffn_weights[:, j]) for j in range(3)]
    scale_two = rms_of(middle)
    normed_two = (middle * scale_two * norm2_gain).astype(BF)
    normed_two_full = gather_rows(normed_two).reshape(-1, model)
    out_grad_full = gather_rows(out_grad).reshape(-1, model)
    gate = mul(normed_two_full, ffn[0])
    up = mul(normed_two_full, ffn[1])
    active_grad = mul(out_grad_full, ffn[2])
    squash = jax.nn.sigmoid(gate)
    swish = gate * squash
    active = (swish * up).astype(BF)
    gate_grad = (active_grad * up * squash * (1.0 + gate * (1.0 - squash))).astype(BF)
    up_grad = (active_grad * swish).astype(BF)
    normed_two_grad = scatter_rows(
        count, lambda g, u: mul_back(g, ffn[0]) + mul_back(u, ffn[1]), gate_grad, up_grad
    )
    extra_two, gain_two_grad = norm_back(middle, scale_two, norm2_gain, normed_two_grad)
    middle_grad = out_grad.astype(jnp.float32) + extra_two
    middle_grad_full = gather_rows(middle_grad.astype(BF)).reshape(-1, model)
    ffn_grad = [
        scatter_grad(normed_two_full, gate_grad),
        scatter_grad(normed_two_full, up_grad),
        scatter_grad(out_grad_full, active),
    ]
    block_out = (middle + scatter_rows(count, lambda a: mul_back(a, ffn[2]), active)).astype(BF)

    mixed_grad = mul(middle_grad_full, mix[3])
    *projected_grad, floor_sums, gain_sums = mixer_backward(
        *projected, mixed_grad, group_labels, floor, head_gain
    )
    normed_grad = scatter_rows(
        count,
        lambda a, b, c: mul_back(a, mix[0]) + mul_back(b, mix[1]) + mul_back(c, mix[2]),
        *projected_grad,
    )
    extra_one, gain_one_grad = norm_back(hidden, scale_one, norm1_gain, normed_grad)
    input_grad = middle_grad + extra_one
    mix_grad = [scatter_grad(normed_full, g) for g in projected_grad]
    mix_grad.append(scatter_grad(middle_grad_full, mixed))

    head_grad = jnp.sum(gain_sums.reshape(-1, HEAD), axis=0)
    lower_grad = jnp.zeros((2, 4, quarter), jnp.float32)
    lower_grad = lax.dynamic_update_slice(
        lower_grad, jnp.sum(floor_sums, axis=(0, 1)).reshape(1, 1, quarter), (core, member, 0)
    )
    sums = jnp.concatenate([gain_one_grad, gain_two_grad, head_grad, lower_grad.reshape(-1)])
    sums = sum_all(sums.reshape(-1, HEAD)).reshape(-1)
    edges = [model, 2 * model, 2 * model + HEAD]
    one, two, head, lower = jnp.split(sums, edges)
    return (
        block_out,
        input_grad,
        jnp.stack(mix_grad, axis=1),
        jnp.stack(ffn_grad, axis=1),
        one,
        two,
        head,
        lower,
    )


def solution(mesh):
    rows = P(("dp", "tensor"), None)
    weights = P("dp", None, "tensor")
    return jax.shard_map(
        body,
        mesh=mesh,
        in_specs=(rows, P("dp", None), weights, weights, P(), P(), P(), P("tensor"), rows),
        out_specs=(rows, rows, weights, weights, P(), P(), P(), P()),
        check_vma=False,
    )
```

```python
import functools

import jax
import jax.numpy as jnp
from jax import lax
from jax.experimental import pallas as pl
from jax.experimental.pallas import tpu as pltpu
from jax.sharding import Mesh, PartitionSpec as P

HEAD = 128
STRIP = 32
CAP = 50.0
BF = jnp.bfloat16
epsilon = 1e-06
PARAMS = pltpu.CompilerParams(vmem_limit_bytes=56 * 1024 * 1024)


def cost(us):
    return pl.CostEstimate(flops=int(us * 1e9), bytes_accessed=1, transcendentals=0)


NN, NT, TN = ((1,), (0,)), ((1,), (1,)), ((0,), (0,))


def dot(a, b, dims=NN):
    return lax.dot_general(a, b, (dims, ((), ())), preferred_element_type=jnp.float32)


def exact_dot(ones, values):
    high = values.astype(BF)
    rest = values - high.astype(jnp.float32)
    mid = rest.astype(BF)
    tail = (rest - mid.astype(jnp.float32)).astype(BF)
    return dot(ones, high) + dot(ones, mid) + dot(ones, tail)


def gates(p0, p1, floor):
    swish = jax.nn.sigmoid(p0)
    gate = jax.nn.sigmoid(p1)
    return swish, gate, floor + (1.0 - floor) * gate


def masks(seg_col, seg_row):
    length = seg_col.shape[0]
    row = lax.broadcasted_iota(jnp.int32, (length, length), 0)
    col = lax.broadcasted_iota(jnp.int32, (length, length), 1)
    return seg_col == seg_row, row, col


def strips(length):
    return [(s, -(-(s + STRIP) // 128) * 128) for s in range(0, length, STRIP)]


def fill_scores(query, key, totals, allowed, scores):
    length = query.shape[0]
    for start, wide in strips(length):
        rows = slice(start, start + STRIP)
        ref = totals[start + STRIP // 2 - 1 : start + STRIP // 2]
        lead = (query[rows] * jnp.exp(totals[rows] - ref)).astype(BF)
        trail = (key[:wide] * jnp.exp(jnp.minimum(ref - totals[:wide], CAP))).astype(BF)
        part = jnp.where(allowed[rows, :wide], dot(lead, trail, NT), 0.0)
        scores[rows, :wide] = part.astype(BF)
        if wide < length:
            scores[rows, wide:] = jnp.zeros((STRIP, length - wide), BF)


def head_forward(p0, p1, p2, seg_col, seg_row, floor, gain, scores):
    swish, gate, forget = gates(p0, p1, floor)
    same, row, col = masks(seg_col, seg_row)
    totals = exact_dot((col <= row).astype(BF), jnp.log(forget))
    fill_scores(p0 * swish, 1.0 - forget, totals, same & (col <= row), scores)
    rec = dot(scores[...], p2.astype(BF))
    rms = lax.rsqrt(jnp.mean(rec * rec, axis=-1, keepdims=True) + epsilon)
    return (rec * rms * gain).astype(BF)


def head_backward(
    p0, p1, p2, mixed_grad, seg_col, seg_row, floor, gain, scores, key_grad, decay_grad, query_grad
):
    length = p0.shape[0]
    swish, gate, forget = gates(p0, p1, floor)
    query = p0 * swish
    key = 1.0 - forget
    same, row, col = masks(seg_col, seg_row)
    allowed = same & (col <= row)
    totals = exact_dot((col <= row).astype(BF), jnp.log(forget))
    fill_scores(query, key, totals, allowed, scores)
    value = p2.astype(BF)
    rec = dot(scores[...], value)
    rms = lax.rsqrt(jnp.mean(rec * rec, axis=-1, keepdims=True) + epsilon)
    unit = rec * rms
    scaled = mixed_grad * gain
    rec_grad = rms * (scaled - unit * jnp.mean(scaled * unit, axis=-1, keepdims=True))
    rec_low = rec_grad.astype(BF)
    value_grad = dot(scores[...], rec_low, TN).astype(BF)
    score_grad = jnp.where(allowed, dot(rec_low, value, NT), 0.0).astype(BF)
    key_grad[...] = jnp.zeros_like(key_grad)
    decay_grad[...] = jnp.zeros_like(decay_grad)
    for start, wide in strips(length):
        rows = slice(start, start + STRIP)
        ref = totals[start + STRIP // 2 - 1 : start + STRIP // 2]
        lead_scale = jnp.exp(totals[rows] - ref)
        trail_scale = jnp.exp(jnp.minimum(ref - totals[:wide], CAP))
        lead = (query[rows] * lead_scale).astype(BF)
        trail = (key[:wide] * trail_scale).astype(BF)
        part = score_grad[rows, :wide]
        lead_grad = dot(part, trail)
        trail_grad = dot(part, lead, TN)
        query_grad[rows, :] = lead_grad * lead_scale
        key_grad[:wide, :] += trail_grad * trail_scale
        decay_grad[:wide, :] -= trail_grad * trail.astype(jnp.float32)
        decay_grad[rows, :] += lead_grad * lead.astype(jnp.float32)
    before = jnp.concatenate([seg_col[:1] - 1, seg_col[:-1]], axis=0)
    carry = (seg_col == before).astype(jnp.float32)
    later = (same & (col >= row)).astype(BF)
    forget_grad = exact_dot(later, decay_grad[...]) * carry / forget
    joint = forget_grad - key_grad[...]
    floor_sum = jnp.sum(joint * (1.0 - gate), axis=0, keepdims=True)
    gain_sum = jnp.sum(mixed_grad * unit, axis=0, keepdims=True)
    g0 = (query_grad[...] * swish * (1.0 + p0 * (1.0 - swish))).astype(BF)
    g1 = (joint * (1.0 - floor) * gate * (1.0 - gate)).astype(BF)
    return g0, g1, value_grad, floor_sum, gain_sum


def load_weight(offsets_ref, sources, refs, whole, sems, begin=0):
    end = begin + whole.shape[1]
    copies = []
    for (piece, low), ref in zip(sources, refs):
        rows, lanes = ref.shape[1:]
        first, last = max(low, begin), min(low + lanes, end)
        if first >= last:
            continue
        for m in range(4):
            at = pl.multiple_of(offsets_ref[4 * piece + m], rows)
            copies.append(
                pltpu.make_async_copy(
                    ref.at[m, :, pl.ds(first - low, last - first)],
                    whole.at[pl.ds(at, rows), pl.ds(first - begin, last - first)],
                    sems.at[len(copies)],
                )
            )
    for copy in copies:
        copy.start()
    for copy in copies:
        copy.wait()


def mixer_forward_kernel(core_ref, offsets_ref, rows_ref, *refs, sources):
    (col_ref, row_ref, floor_ref, gain_ref, p_ref, mixed_ref, send_ref, keep_ref, scores, whole,
     weight, sems) = refs[len(sources) :]

    @pl.when(pl.program_id(0) == 0)
    def _():
        load_weight(offsets_ref, sources, refs, weight, sems)

    count = rows_ref.shape[1] // 2
    width = whole.shape[1]
    mine = pl.multiple_of(core_ref[0] * count, count)
    theirs = pl.multiple_of((1 - core_ref[0]) * count, count)
    p_ref[0] = dot(rows_ref[0], weight[:, : 3 * width])
    for h in range(width // HEAD):
        p0, p1, p2 = [p_ref[0, :, pl.ds(j * width + h * HEAD, HEAD)] for j in range(3)]
        lanes = slice(h * HEAD, (h + 1) * HEAD)
        whole[:, lanes] = head_forward(
            p0, p1, p2, col_ref[0], row_ref[0], floor_ref[:, lanes], gain_ref[...], scores.at[h]
        )
    mixed_ref[0] = whole[...]
    send_ref[0] = dot(whole[pl.ds(theirs, count), :], weight[:, 3 * width :], NT).astype(BF)
    keep_ref[0] = dot(whole[pl.ds(mine, count), :], weight[:, 3 * width :], NT)


def mixer_backward_kernel(core_ref, offsets_ref, rows_ref, *refs, sources):
    (p_ref, col_ref, row_ref, floor_ref, gain_ref, g_one_ref, g_two_ref, send_ref, keep_ref,
     floor_sum_ref, gain_sum_ref, scores, key_grad, decay_grad, query_grad, mixed_grad, parts,
     weight, sems) = refs[len(sources) :]

    @pl.when(pl.program_id(0) == 0)
    def _():
        load_weight(offsets_ref, sources, refs, weight, sems)

    count = rows_ref.shape[1] // 2
    width = mixed_grad.shape[1]
    mine = pl.multiple_of(core_ref[0] * count, count)
    theirs = pl.multiple_of((1 - core_ref[0]) * count, count)
    mixed_grad[...] = dot(rows_ref[0], weight[:, 3 * width :])
    for h in range(width // HEAD):
        p0, p1, p2 = [p_ref[0, :, pl.ds(j * width + h * HEAD, HEAD)] for j in range(3)]
        lanes = slice(h * HEAD, (h + 1) * HEAD)
        g0, g1, g2, floor_sum, gain_sum = head_backward(
            p0, p1, p2, mixed_grad[:, lanes], col_ref[0], row_ref[0], floor_ref[:, lanes],
            gain_ref[...], scores.at[h], key_grad.at[h], decay_grad.at[h], query_grad.at[h],
        )
        for j, g in enumerate((g0, g1, g2)):
            parts[:, pl.ds(j * width + h * HEAD, HEAD)] = g
        floor_sum_ref[0, :, lanes] = jnp.broadcast_to(floor_sum, (8, HEAD)) * 0.125
        gain_sum_ref[0, :, lanes] = jnp.broadcast_to(gain_sum, (8, HEAD)) * 0.125

    def back(at):
        return dot(parts[pl.ds(at, count), :], weight[:, : 3 * width], NT)

    g_one_ref[0] = parts[:, : 2 * width]
    g_two_ref[0] = parts[:, 2 * width :]
    send_ref[0] = back(theirs).astype(BF)
    keep_ref[0] = back(mine)


def mixer_specs(count, model, width, length):
    def at(shape, index):
        return pl.BlockSpec(shape, lambda s, c, o: index(s))

    rows = at((1, length, model), lambda s: (s, 0, 0))
    side = at((1, count, model), lambda s: (s, 0, 0))
    col = at((1, length, 1), lambda s: (s, 0, 0))
    row = at((1, 1, length), lambda s: (s, 0, 0))
    floor = at((1, width), lambda s: (0, 0))
    gain = at((1, HEAD), lambda s: (0, 0))
    wide = at((1, length, 3 * width), lambda s: (s, 0, 0))
    pairs = [at((1, length, k * width), lambda s: (s, 0, 0)) for k in (1, 2)]
    return at, rows, side, wide, pairs, [col, row, floor, gain]


def weight_scratch(model, lanes, sources):
    return [pltpu.VMEM((model, lanes), BF), pltpu.SemaphoreType.DMA((4 * len(sources),))]


def layout_of(sources):
    return tuple((piece, low) for piece, low, _ in sources), [part for _, _, part in sources]


def mixer_forward(core, offsets, tokens, sources, segments, floor, gain):
    groups, length, model = tokens.shape
    width, count = floor.shape[0], length // 2
    half = (groups, count, model)
    at, rows, side, wide, pairs, small = mixer_specs(count, model, width, length)
    layout, parts = layout_of(sources)
    shape = jax.ShapeDtypeStruct
    return pl.pallas_call(
        functools.partial(mixer_forward_kernel, sources=layout),
        grid_spec=pltpu.PrefetchScalarGridSpec(
            num_scalar_prefetch=2,
            grid=(groups,),
            in_specs=[rows] + [pl.BlockSpec(memory_space=pl.ANY)] * len(parts) + small,
            out_specs=[wide, pairs[0], side, side],
            scratch_shapes=[
                pltpu.VMEM((width // HEAD, length, length), BF),
                pltpu.VMEM((length, width), BF),
            ]
            + weight_scratch(model, 4 * width, parts),
        ),
        out_shape=[
            shape((groups, length, 3 * width), jnp.float32),
            shape((groups, length, width), BF),
            shape(half, BF),
            shape(half, jnp.float32),
        ],
        compiler_params=PARAMS,
        cost_estimate=cost(17),
        name="mixer_forward",
    )(
        core, offsets, tokens, *parts, segments[:, :, None],
        segments[:, None, :], floor[None], gain[None],
    )


def mixer_backward(core, offsets, tokens, sources, projected, segments, floor, gain):
    groups, length, model = tokens.shape
    width, count = floor.shape[0], length // 2
    half = (groups, count, model)
    at, rows, side, wide, pairs, small = mixer_specs(count, model, width, length)
    layout, parts = layout_of(sources)
    heads = width // HEAD
    sums = at((1, 8, width), lambda s: (s, 0, 0))
    shape = jax.ShapeDtypeStruct
    return pl.pallas_call(
        functools.partial(mixer_backward_kernel, sources=layout),
        grid_spec=pltpu.PrefetchScalarGridSpec(
            num_scalar_prefetch=2,
            grid=(groups,),
            in_specs=[rows]
            + [pl.BlockSpec(memory_space=pl.ANY)] * len(parts)
            + [wide]
            + small,
            out_specs=[pairs[1], pairs[0], side, side, sums, sums],
            scratch_shapes=[pltpu.VMEM((heads, length, length), BF)]
            + [pltpu.VMEM((heads, length, HEAD), jnp.float32)] * 3
            + [pltpu.VMEM((length, width), jnp.float32), pltpu.VMEM((length, 3 * width), BF)]
            + weight_scratch(model, 4 * width, parts),
        ),
        out_shape=[
            shape((groups, length, 2 * width), BF),
            shape((groups, length, width), BF),
            shape(half, BF),
            shape(half, jnp.float32),
        ]
        + [shape((groups, 8, width), jnp.float32)] * 2,
        compiler_params=PARAMS,
        cost_estimate=cost(27),
        name="mixer_backward",
    )(
        core, offsets, tokens, *parts, projected, segments[:, :, None],
        segments[:, None, :], floor[None], gain[None],
    )


def ffn_kernel(core_ref, offsets_ref, rows_ref, top_ref, *refs, sources):
    (active_one_ref, active_two_ref, one_ref, two_ref, send_ref, keep_ref, grads, weight,
     sems) = refs[len(sources) :]

    @pl.when(pl.program_id(0) == 0)
    def _():
        load_weight(offsets_ref, sources, refs, weight, sems)

    width, cut = grads.shape[1] // 2, one_ref.shape[2]
    count = rows_ref.shape[1] // 2
    mine = pl.multiple_of(core_ref[0] * count, count)
    theirs = pl.multiple_of((1 - core_ref[0]) * count, count)
    both = dot(rows_ref[0], weight[:, : 2 * width])
    gate, up = both[:, :width], both[:, width:]
    active_grad = dot(top_ref[0], weight[:, 2 * width : 3 * width])
    squash = jax.nn.sigmoid(gate)
    swish = gate * squash
    half = active_one_ref.shape[2]
    spare = jnp.zeros((2 * count, 2 * half - width), BF)
    active = (swish * up).astype(BF)
    active_one_ref[0] = active[:, :half]
    active_two_ref[0] = jnp.concatenate([active[:, half:], spare], axis=1)
    gate_grad = active_grad * up * squash * (1.0 + gate * (1.0 - squash))
    grads[...] = jnp.concatenate([gate_grad, active_grad * swish], axis=1).astype(BF)
    one_ref[0] = grads[:, :cut]
    two_ref[0] = grads[:, cut:]
    send_ref[0] = dot(grads[pl.ds(theirs, count), :], weight[:, : 2 * width], NT).astype(BF)
    keep_ref[0] = dot(grads[pl.ds(mine, count), :], weight[:, : 2 * width], NT)


def ffn(core, offsets, tokens, tops, sources, width, total):
    groups, length, model = tokens.shape
    cut = width // 128 * 128
    widths = [(total - 2 * width) // 2] * 2 + [cut, 2 * width - cut]
    layout, parts = layout_of(sources)

    def at(rows, lanes):
        return pl.BlockSpec((1, rows, lanes), lambda s, c, o: (s, 0, 0))

    shape = jax.ShapeDtypeStruct
    return pl.pallas_call(
        functools.partial(ffn_kernel, sources=layout),
        grid_spec=pltpu.PrefetchScalarGridSpec(
            num_scalar_prefetch=2,
            grid=(groups,),
            in_specs=[at(length, model)] * 2 + [pl.BlockSpec(memory_space=pl.ANY)] * len(parts),
            out_specs=[at(length, n) for n in widths] + [at(length // 2, model)] * 2,
            scratch_shapes=[pltpu.VMEM((length, 2 * width), BF)]
            + weight_scratch(model, total, parts),
        ),
        out_shape=[
            *[shape((groups, length, n), BF) for n in widths],
            shape((groups, length // 2, model), BF),
            shape((groups, length // 2, model), jnp.float32),
        ],
        compiler_params=PARAMS,
        cost_estimate=cost(36),
        name="ffn",
    )(core, offsets, tokens, tops, *parts)


def rows_kernel(core_ref, offsets_ref, one_ref, two_ref, *refs, sources, begin):
    send_ref, keep_ref, whole, sems = refs[len(sources) :]

    @pl.when(pl.program_id(0) == 0)
    def _():
        load_weight(offsets_ref, sources, refs, whole, sems, begin)

    count = one_ref.shape[1] // 2
    mine = pl.multiple_of(core_ref[0] * count, count)
    theirs = pl.multiple_of((1 - core_ref[0]) * count, count)

    def product(at):
        parts = [one_ref[0, pl.ds(at, count), :], two_ref[0, pl.ds(at, count), :]]
        return dot(jnp.concatenate(parts, axis=1), whole[...], NT)

    send_ref[0] = product(theirs).astype(BF)
    keep_ref[0] = product(mine)


def rows_product(core, offsets, one, two, sources, begin, model):
    groups, length, width = one.shape
    layout, parts = layout_of(sources)

    def at(rows, lanes):
        return pl.BlockSpec((1, rows, lanes), lambda s, c, o: (s, 0, 0))

    shape = jax.ShapeDtypeStruct
    return pl.pallas_call(
        functools.partial(rows_kernel, sources=layout, begin=begin),
        grid_spec=pltpu.PrefetchScalarGridSpec(
            num_scalar_prefetch=2,
            grid=(groups,),
            in_specs=[at(length, width)] * 2 + [pl.BlockSpec(memory_space=pl.ANY)] * len(parts),
            out_specs=[at(length // 2, model)] * 2,
            scratch_shapes=weight_scratch(model, 2 * width, parts),
        ),
        out_shape=[
            shape((groups, length // 2, model), BF),
            shape((groups, length // 2, model), jnp.float32),
        ],
        compiler_params=PARAMS,
        cost_estimate=cost(13),
        name="rows_product",
    )(core, offsets, one, two, *parts)


def grad_kernel(blocks_ref, rows_ref, *refs):
    half = len(refs) // 2
    for grad_ref, out_ref in zip(refs[:half], refs[half:]):
        out_ref[0] = dot(rows_ref[...], grad_ref[...], TN).astype(out_ref.dtype)


def grad_product(tokens, grads, blocks, wide, kind):
    count, model = tokens.shape
    side = pl.BlockSpec((count, wide), lambda i, b: (0, b[i]))
    number = blocks.shape[0]
    return pl.pallas_call(
        grad_kernel,
        grid_spec=pltpu.PrefetchScalarGridSpec(
            num_scalar_prefetch=1,
            grid=(number,),
            in_specs=[side] + [pl.BlockSpec(g.shape, lambda i, b: (0, 0)) for g in grads],
            out_specs=[pl.BlockSpec((1, wide, g.shape[1]), lambda i, b: (i, 0, 0)) for g in grads],
        ),
        out_shape=[jax.ShapeDtypeStruct((number, wide, g.shape[1]), kind) for g in grads],
        compiler_params=PARAMS,
        cost_estimate=cost(6),
        name="grad_product",
    )(blocks, tokens, *grads)


GROUP = ("l", "x")


def swap(values, axes):
    total = 2 ** len(axes)
    return lax.ppermute(values, axes, [(s, total - 1 - s) for s in range(total)])


def shift(values, steps):
    total = lax.axis_size("h")
    return lax.ppermute(values, "h", [(s, (s + steps) % total) for s in range(total)])


def own_member():
    return lax.axis_index("l") * 2 + lax.axis_index("x")


def source_rows(rows):
    y, high = lax.axis_index("y"), lax.axis_index("h")
    highs = lax.axis_size("h")
    starts = []
    for k in range(highs):
        for side in (y, 1 - y):
            for member in range(4):
                block = ((high - k) % highs) * 8 + (member >> 1) * 4 + side * 2 + (member & 1)
                starts.append(block * rows)
    return jnp.stack(starts).astype(jnp.int32)


def trade(slices):
    return lax.all_to_all(slices, GROUP, 0, 0, tiled=True)


def after(values, *others):
    return lax.optimization_barrier((values, others))[0]


def far(block):
    return [shift(block, k) for k in range(1, lax.axis_size("h"))]


def near(parts):
    return [swap(part, ("y",)) for part in parts]


def pieces(low, straight, crossed):
    out = []
    for k, (one, two) in enumerate(zip(straight, crossed), 1):
        out += [(2 * k, low, one), (2 * k + 1, low, two)]
    return out


def half_grads(tokens, grads, yy, kind):
    highs, high = lax.axis_size("h"), lax.axis_index("h")
    wide = tokens.shape[1] // (4 * highs)
    order = [(high + k) % highs for k in range(1, highs)] + [high]
    blocks = jnp.stack([(h * 2 + z) * 2 + yy for h in order for z in range(2)]).astype(jnp.int32)
    if wide % 128 == 0:
        return grad_product(tokens, grads, blocks, wide, kind)
    split = jnp.take(tokens.reshape(tokens.shape[0], -1, wide), blocks, axis=1)
    return [
        jnp.einsum("tad,tx->adx", split, g, preferred_element_type=jnp.float32).astype(kind)
        for g in grads
    ]


def grad_sends(tokens, grads):
    return half_grads(flat(tokens), [flat(g) for g in grads], 1 - lax.axis_index("y"), BF)


def grad_keeps(tokens, grads):
    return half_grads(flat(tokens), [flat(g) for g in grads], lax.axis_index("y"), jnp.float32)


def add_near(keep, came):
    highs = lax.axis_size("h")
    total = keep + came.astype(jnp.float32)
    cuts = [2 * k for k in range(1, highs)]
    *away, home = jnp.split(total, cuts)
    return home, [part.astype(BF) for part in away]


def send_far(away):
    return [shift(part, k) for k, part in enumerate(away, 1)]


def add_far(home, fars):
    for far in fars:
        home = home + far.astype(jnp.float32)
    return home.reshape(4, -1, home.shape[-1]).astype(BF)


def flat(values):
    return values.reshape(-1, values.shape[-1])


def gather_rows(rows):
    full = lax.all_gather(rows, GROUP + ("tensor",), axis=0, tiled=True)
    return full.reshape(4, -1, rows.shape[1])


def add_cores(keep, came):
    return (keep + came.astype(jnp.float32)).astype(BF)


def add_members(parts):
    return jnp.sum(parts.astype(jnp.float32), axis=0)


def sum_all(values):
    for axis in ("x", "y", "l", "tensor"):
        values = values + swap(values, (axis,))
    size, bits = lax.axis_size("h"), 1
    while bits < size:
        values = values + lax.ppermute(values, "h", [(s, s ^ bits) for s in range(size)])
        bits *= 2
    return values


def rms_of(values):
    return lax.rsqrt(jnp.mean(values * values, axis=-1, keepdims=True) + epsilon)


def norm_back(values, scale, gain, grad):
    unit = values * scale
    wide = grad * gain
    out = scale * (wide - unit * jnp.mean(wide * unit, axis=-1, keepdims=True))
    return out, jnp.sum(grad * unit, axis=0)


def body(
    hidden_in,
    segments,
    mix_weights,
    ffn_weights,
    norm1_gain,
    norm2_gain,
    head_gain,
    lower_bound,
    out_grad,
):
    core, member = lax.axis_index("tensor"), own_member()
    core_at = core.astype(jnp.int32).reshape(1)
    rows = mix_weights.shape[0]
    offsets = source_rows(rows)
    quarter, units = lower_bound.shape[0] // 4, ffn_weights.shape[2] // 4
    model = hidden_in.shape[1]
    channels = 4 * quarter
    lanes = -(-3 * units // 128) * 128

    def slices(weights, width):
        split = weights.reshape(rows, weights.shape[1], 4, -1).transpose(2, 0, 1, 3)
        split = split.reshape(4, rows, -1)
        return jnp.pad(split, ((0, 0), (0, 0), (0, width - split.shape[2])))

    length = segments.shape[1]
    labels = jnp.pad(segments.astype(BF), ((0, 15), (0, channels - length)))
    labels = jnp.broadcast_to(labels, (4,) + labels.shape)
    hidden = hidden_in.astype(jnp.float32)
    scale_one = rms_of(hidden)
    normed = (hidden * scale_one * norm1_gain).astype(BF)
    floor = lax.dynamic_slice_in_dim(lower_bound, member * quarter, quarter)
    feed = slices(ffn_weights, lanes)
    mix = trade(jnp.concatenate([slices(mix_weights, channels), labels], axis=1))

    gate = (mix, normed, feed)
    mix, normed, feed = lax.optimization_barrier(gate)
    labels = mix[:, rows, :length].astype(jnp.int32)
    mix = mix[:, :rows]
    cut = 640
    mix_far_a = far(mix[..., :cut])
    mix_near = swap(mix, ("y",))
    feed = trade(feed)

    gate = (mix_far_a, mix_near, feed)
    mix_far_b = far(after(mix[..., cut:], gate))
    mix_cross_a = near(after(mix_far_a, gate))
    normed = gather_rows(after(normed, gate))

    gate = (mix_far_b, mix_cross_a)
    cuts = [0, 384, 768, 1024, 1664, lanes]
    feeds = [feed[..., low:high] for low, high in zip(cuts[:-1], cuts[1:])]
    far_a = far(after(feeds[0], gate))
    mix_cross_b = near(after(mix_far_b, gate))
    mix_sources = [(0, 0, mix), (1, 0, mix_near)]
    mix_sources += pieces(0, mix_far_a, mix_cross_a) + pieces(cut, mix_far_b, mix_cross_b)

    gate = (far_a, mix_cross_b, normed)
    far_b = far(after(feeds[1], gate))
    near_a = swap(after(feed[..., :768], gate), ("y",))
    tops = gather_rows(after(out_grad, gate))
    projected, mixed, send, keep = mixer_forward(
        core_at, offsets, after(normed, gate), mix_sources, labels, floor, head_gain
    )

    gate = (send, far_b, near_a)
    came = swap(after(send, gate), ("tensor",))
    far_c = far(after(feeds[2], gate))
    near_b = swap(after(feed[..., 768:1280], gate), ("y",))
    total = add_cores(keep, came)

    gate = (total, far_c, near_b)
    parts = trade(after(total, gate))
    far_d = far(after(feeds[3], gate))
    near_c = swap(after(feed[..., 1280:], gate), ("y",))
    cross_a = near(after(far_a, near_c))

    gate = (parts, far_d, near_c, cross_a)
    far_e = far(after(feeds[4], gate))
    cross_b = near(after(far_b, gate))
    cross_c = near(after(far_c, cross_b))
    middle = hidden + add_members(after(parts, gate))
    scale_two = rms_of(middle)
    normed_two = gather_rows((middle * scale_two * norm2_gain).astype(BF))

    gate = (far_e, cross_c)
    cross_d = near(after(far_d, gate))
    cross_e = near(after(far_e, gate))
    feed_sources = [(0, 0, feed), (1, 0, near_a), (1, 768, near_b), (1, 1280, near_c)]
    crosses = [cross_a, cross_b, cross_c, cross_d, cross_e]
    for low, straight, crossed in zip(cuts, [far_a, far_b, far_c, far_d, far_e], crosses):
        feed_sources += pieces(low, straight, crossed)

    active_one, active_two, grad_one, grad_two, send, keep = ffn(
        core_at, offsets, normed_two, tops, feed_sources, units, lanes
    )
    came = swap(send, ("tensor",))
    down_send, down_send_two = grad_sends(after(tops, send), [active_one, active_two])
    down_came = swap(down_send, ("y",))
    total = add_cores(keep, after(came, down_send))

    gate = (total,)
    parts = trade(total)
    one_send, two_send = grad_sends(after(normed_two, gate), [grad_one, grad_two])
    down_keep, down_keep_two = grad_keeps(after(tops, one_send), [active_one, active_two])

    gate = (down_came, down_keep)
    down_home, down_away = add_near(down_keep, after(down_came, gate))
    down_fars = send_far(down_away)
    down_came_two = swap(after(down_send_two, gate), ("y",))

    gate = (parts, down_fars, down_came_two)
    normed_two_grad = add_members(after(parts, gate))
    extra_two, gain_two_grad = norm_back(middle, scale_two, norm2_gain, normed_two_grad)
    middle_grad = out_grad.astype(jnp.float32) + extra_two
    middle_low = middle_grad.astype(BF)
    middle_full = gather_rows(middle_low)
    one_came = swap(after(one_send, gate), ("y",))
    down_home_two, down_away_two = add_near(down_keep_two, after(down_came_two, gate))
    down_fars_two = send_far(down_away_two)
    one_keep, two_keep = grad_keeps(
        after(normed_two, middle_low, down_away_two), [grad_one, grad_two]
    )
    away_send, away_keep = rows_product(
        core_at, offsets, after(active_one, one_keep), active_two, feed_sources, 2 * units, model
    )

    gate = (down_fars_two, one_came, away_send)
    one_home, one_away = add_near(one_keep, after(one_came, gate))
    one_fars = send_far(one_away)
    two_came = swap(after(two_send, gate), ("y",))
    away_total = add_cores(away_keep, swap(after(away_send, gate), ("tensor",)))

    gate = (middle_full, away_total, one_away)
    middle_full = after(middle_full, gate)
    (last_send,) = grad_sends(middle_full, [mixed])
    block_parts = trade(after(away_total, gate))
    g_one, g_two, send, keep, floor_sums, gain_sums = mixer_backward(
        core_at, offsets, after(middle_full, last_send), mix_sources, projected, labels, floor,
        head_gain,
    )

    gate = (send, one_fars, two_came, block_parts)
    two_home, two_away = add_near(two_keep, after(two_came, gate))
    two_fars = send_far(two_away)
    last_came = swap(after(last_send, gate), ("y",))
    came = swap(after(send, gate), ("tensor",))
    (g_two_send,) = grad_sends(after(normed, gate), [g_two])
    total = add_cores(keep, after(came, g_two_send, two_away))

    gate = (total, last_came)
    parts = trade(after(total, gate))
    g_two_came = swap(after(g_two_send, gate), ("y",))
    (g_one_send,) = grad_sends(after(normed, gate), [g_one])
    (last_keep,) = grad_keeps(after(middle_full, g_one_send), [mixed])
    (g_two_keep,) = grad_keeps(after(normed, last_keep), [g_two])

    gate = (g_two_came, g_two_keep)
    g_one_came = swap(after(g_one_send, gate), ("y",))
    last_home, last_away = add_near(last_keep, after(last_came, gate))
    g_two_home, g_two_away = add_near(g_two_keep, after(g_two_came, gate))
    near_away = [jnp.concatenate(pair, axis=-1) for pair in zip(g_two_away, last_away)]
    near_home = jnp.concatenate([g_two_home, last_home], axis=-1)
    (g_one_keep,) = grad_keeps(after(normed, near_away), [g_one])

    gate = (parts, two_fars, g_one_keep)
    near_fars = send_far(after(near_away, gate))
    sums = [add_far(one_home, after(one_fars, gate)), add_far(two_home, after(two_fars, gate))]
    input_parts = trade(jnp.concatenate(sums, axis=-1))
    normed_grad = add_members(after(parts, gate))
    extra_one, gain_one_grad = norm_back(hidden, scale_one, norm1_gain, normed_grad)
    input_grad = middle_grad + extra_one
    block_out = (middle + add_members(after(block_parts, gate))).astype(BF)
    g_one_home, g_one_away = add_near(g_one_keep, after(g_one_came, normed_grad))

    gate = (near_fars, input_parts, g_one_away)
    g_one_fars = send_far(after(g_one_away, gate))
    sums = [
        add_far(near_home, after(near_fars, gate)),
        add_far(down_home, after(down_fars, gate)),
        add_far(down_home_two, after(down_fars_two, gate)),
    ]
    near_parts = trade(jnp.concatenate(sums, axis=-1))
    down_parts = near_parts[..., 2 * quarter :]
    g_one_parts = trade(add_far(g_one_home, after(g_one_fars, near_parts)))

    head_grad = jnp.sum(gain_sums.reshape(-1, HEAD), axis=0)
    lower_grad = jnp.zeros((2, 4, quarter), jnp.float32)
    lower_grad = lax.dynamic_update_slice(
        lower_grad, jnp.sum(floor_sums, axis=(0, 1)).reshape(1, 1, quarter), (core, member, 0)
    )
    sums = jnp.concatenate([gain_one_grad, gain_two_grad, head_grad, lower_grad.reshape(-1)])
    sums = sum_all(sums.reshape(-1, HEAD)).reshape(-1)
    gain_one, gain_two, head, lower = jnp.split(sums, [model, 2 * model, 2 * model + HEAD])

    def stacked(*parts):
        joined = [p.transpose(1, 0, 2).reshape(rows, -1) for p in parts]
        return jnp.stack(joined, axis=1).astype(jnp.float32)

    mix_grad = stacked(
        g_one_parts[..., :quarter],
        g_one_parts[..., quarter:],
        near_parts[..., :quarter],
        near_parts[..., quarter : 2 * quarter],
    )
    ffn_grad = stacked(input_parts[..., :units], input_parts[..., units:], down_parts[..., :units])
    return (block_out, input_grad, mix_grad, ffn_grad, gain_one, gain_two, head, lower)


def solution(mesh):
    total, cores = mesh.shape["dp"], mesh.shape["tensor"]
    fine = Mesh(mesh.devices.reshape(total // 8, 2, 2, 2, cores), ("h", "l", "y", "x", "tensor"))
    dp = ("h", "l", "y", "x")
    rows = P(dp + ("tensor",), None)
    weights = P(dp, None, "tensor")
    return jax.shard_map(
        body,
        mesh=fine,
        in_specs=(rows, P(dp, None), weights, weights, P(), P(), P(), P("tensor"), rows),
        out_specs=(rows, rows, weights, weights, P(), P(), P(), P()),
        check_vma=False,
    )
```

```python
import functools

import jax
import jax.numpy as jnp
from jax import lax
from jax.experimental import pallas as pl
from jax.experimental.pallas import tpu as pltpu
from jax.sharding import Mesh, PartitionSpec as P

HEAD = 128
STRIP = 32
CAP = 50.0
BF = jnp.bfloat16
epsilon = 1e-06
PARAMS = pltpu.CompilerParams(vmem_limit_bytes=56 * 1024 * 1024)


LONG, SHORT = [pl.CostEstimate(flops=f, bytes_accessed=1, transcendentals=0) for f in (5 * 10**10, 1)]


NN, NT, TN = ((1,), (0,)), ((1,), (1,)), ((0,), (0,))


def dot(a, b, dims=NN):
    return lax.dot_general(a, b, (dims, ((), ())), preferred_element_type=jnp.float32)


def exact_dot(ones, values):
    high = values.astype(BF)
    rest = values - high.astype(jnp.float32)
    mid = rest.astype(BF)
    tail = (rest - mid.astype(jnp.float32)).astype(BF)
    return dot(ones, high) + dot(ones, mid) + dot(ones, tail)


def gates(p0, p1, floor):
    swish = jax.nn.sigmoid(p0)
    gate = jax.nn.sigmoid(p1)
    return swish, gate, floor + (1.0 - floor) * gate


def masks(seg_col, seg_row):
    length = seg_col.shape[0]
    row = lax.broadcasted_iota(jnp.int32, (length, length), 0)
    col = lax.broadcasted_iota(jnp.int32, (length, length), 1)
    return seg_col == seg_row, row, col


def strips(length):
    return [(s, -(-(s + STRIP) // 128) * 128) for s in range(0, length, STRIP)]


def fill_scores(query, key, totals, allowed, scores):
    length = query.shape[0]
    for start, wide in strips(length):
        rows = slice(start, start + STRIP)
        ref = totals[start + STRIP // 2 - 1 : start + STRIP // 2]
        lead = (query[rows] * jnp.exp(totals[rows] - ref)).astype(BF)
        trail = (key[:wide] * jnp.exp(jnp.minimum(ref - totals[:wide], CAP))).astype(BF)
        part = jnp.where(allowed[rows, :wide], dot(lead, trail, NT), 0.0)
        scores[rows, :wide] = part.astype(BF)
        if wide < length:
            scores[rows, wide:] = jnp.zeros((STRIP, length - wide), BF)


def head_forward(p0, p1, p2, seg_col, seg_row, floor, gain, scores):
    swish, gate, forget = gates(p0, p1, floor)
    same, row, col = masks(seg_col, seg_row)
    totals = exact_dot((col <= row).astype(BF), jnp.log(forget))
    fill_scores(p0 * swish, 1.0 - forget, totals, same & (col <= row), scores)
    rec = dot(scores[...], p2.astype(BF))
    rms = lax.rsqrt(jnp.mean(rec * rec, axis=-1, keepdims=True) + epsilon)
    return (rec * rms * gain).astype(BF)


def head_backward(
    p0, p1, p2, mixed_grad, seg_col, seg_row, floor, gain, scores, key_grad, decay_grad, query_grad
):
    length = p0.shape[0]
    swish, gate, forget = gates(p0, p1, floor)
    query = p0 * swish
    key = 1.0 - forget
    same, row, col = masks(seg_col, seg_row)
    allowed = same & (col <= row)
    totals = exact_dot((col <= row).astype(BF), jnp.log(forget))
    fill_scores(query, key, totals, allowed, scores)
    value = p2.astype(BF)
    rec = dot(scores[...], value)
    rms = lax.rsqrt(jnp.mean(rec * rec, axis=-1, keepdims=True) + epsilon)
    unit = rec * rms
    scaled = mixed_grad * gain
    rec_grad = rms * (scaled - unit * jnp.mean(scaled * unit, axis=-1, keepdims=True))
    rec_low = rec_grad.astype(BF)
    value_grad = dot(scores[...], rec_low, TN).astype(BF)
    score_grad = jnp.where(allowed, dot(rec_low, value, NT), 0.0).astype(BF)
    key_grad[...] = jnp.zeros_like(key_grad)
    decay_grad[...] = jnp.zeros_like(decay_grad)
    for start, wide in strips(length):
        rows = slice(start, start + STRIP)
        ref = totals[start + STRIP // 2 - 1 : start + STRIP // 2]
        lead_scale = jnp.exp(totals[rows] - ref)
        trail_scale = jnp.exp(jnp.minimum(ref - totals[:wide], CAP))
        lead = (query[rows] * lead_scale).astype(BF)
        trail = (key[:wide] * trail_scale).astype(BF)
        part = score_grad[rows, :wide]
        lead_grad = dot(part, trail)
        trail_grad = dot(part, lead, TN)
        query_grad[rows, :] = lead_grad * lead_scale
        key_grad[:wide, :] += trail_grad * trail_scale
        decay_grad[:wide, :] -= trail_grad * trail.astype(jnp.float32)
        decay_grad[rows, :] += lead_grad * lead.astype(jnp.float32)
    before = jnp.concatenate([seg_col[:1] - 1, seg_col[:-1]], axis=0)
    carry = (seg_col == before).astype(jnp.float32)
    later = (same & (col >= row)).astype(BF)
    forget_grad = exact_dot(later, decay_grad[...]) * carry / forget
    joint = forget_grad - key_grad[...]
    floor_sum = jnp.sum(joint * (1.0 - gate), axis=0, keepdims=True)
    gain_sum = jnp.sum(mixed_grad * unit, axis=0, keepdims=True)
    g0 = (query_grad[...] * swish * (1.0 + p0 * (1.0 - swish))).astype(BF)
    g1 = (joint * (1.0 - floor) * gate * (1.0 - gate)).astype(BF)
    return g0, g1, value_grad, floor_sum, gain_sum


def load_weight(offsets_ref, sources, refs, whole, sems, begin=0):
    end = begin + whole.shape[1]
    copies = []
    for (piece, low), ref in zip(sources, refs):
        rows, lanes = ref.shape[1:]
        first, last = max(low, begin), min(low + lanes, end)
        if first >= last:
            continue
        for m in range(4):
            at = pl.multiple_of(offsets_ref[4 * piece + m], rows)
            copies.append(
                pltpu.make_async_copy(
                    ref.at[m, :, pl.ds(first - low, last - first)],
                    whole.at[pl.ds(at, rows), pl.ds(first - begin, last - first)],
                    sems.at[len(copies)],
                )
            )
    for copy in copies:
        copy.start()
    for copy in copies:
        copy.wait()


def row_copies(core, refs, whole, sems):
    count = refs[0].shape[0]
    for side in range(2):
        at = pl.multiple_of((core if side == 0 else 1 - core) * count, count)
        for m in range(4):
            ref = refs[m] if side == 0 else refs[4].at[m] if m < 3 else refs[5]
            yield m, pltpu.make_async_copy(
                ref, whole.at[m, pl.ds(at, count), :], sems.at[side, m]
            )


def start_rows(core, refs, whole, sems):
    for _, copy in row_copies(core, refs, whole, sems):
        copy.start()


def wait_rows(core, refs, whole, sems, sequence):
    for m, copy in row_copies(core, refs, whole, sems):

        @pl.when(sequence == m)
        def _():
            copy.wait()


def row_scratch(count, model):
    return [pltpu.VMEM((4, 2 * count, model), BF), pltpu.SemaphoreType.DMA((2, 4))]


def mixer_forward_kernel(core_ref, offsets_ref, *refs, sources):
    rows, refs = refs[:6], refs[6:]
    (col_ref, row_ref, floor_ref, gain_ref, p_ref, mixed_ref, send_ref, keep_ref, scores, whole,
     back, tokens, token_sems, weight, sems) = refs[len(sources) :]

    sequence = pl.program_id(0)

    @pl.when(sequence == 0)
    def _():
        start_rows(core_ref[0], rows, tokens, token_sems)
        load_weight(offsets_ref, sources, refs, weight, sems)

    wait_rows(core_ref[0], rows, tokens, token_sems, sequence)

    count = rows[0].shape[0]
    width = whole.shape[1]
    mine = pl.multiple_of(core_ref[0] * count, count)
    theirs = pl.multiple_of((1 - core_ref[0]) * count, count)
    p_ref[0] = dot(tokens[sequence], weight[:, : 3 * width])
    for h in range(width // HEAD):
        p0, p1, p2 = [p_ref[0, :, pl.ds(j * width + h * HEAD, HEAD)] for j in range(3)]
        lanes = slice(h * HEAD, (h + 1) * HEAD)
        whole[:, lanes] = head_forward(
            p0, p1, p2, col_ref[0], row_ref[0], floor_ref[:, lanes], gain_ref[...], scores.at[h]
        )
    mixed_ref[0] = whole[...]
    back[...] = dot(whole[...], weight[:, 3 * width :], NT)
    send_ref[0] = back[pl.ds(theirs, count), :].astype(BF)
    keep_ref[0] = back[pl.ds(mine, count), :]


def mixer_backward_kernel(core_ref, offsets_ref, *refs, sources):
    rows, refs = refs[:6], refs[6:]
    (p_ref, col_ref, row_ref, floor_ref, gain_ref, g_one_ref, g_two_ref, send_ref, keep_ref,
     floor_sum_ref, gain_sum_ref, scores, key_grad, decay_grad, query_grad, mixed_grad, parts,
     back, tokens, token_sems, weight, sems) = refs[len(sources) :]

    sequence = pl.program_id(0)

    @pl.when(sequence == 0)
    def _():
        start_rows(core_ref[0], rows, tokens, token_sems)
        load_weight(offsets_ref, sources, refs, weight, sems)

    wait_rows(core_ref[0], rows, tokens, token_sems, sequence)

    count = rows[0].shape[0]
    width = mixed_grad.shape[1]
    mine = pl.multiple_of(core_ref[0] * count, count)
    theirs = pl.multiple_of((1 - core_ref[0]) * count, count)
    mixed_grad[...] = dot(tokens[sequence], weight[:, 3 * width :])
    for h in range(width // HEAD):
        p0, p1, p2 = [p_ref[0, :, pl.ds(j * width + h * HEAD, HEAD)] for j in range(3)]
        lanes = slice(h * HEAD, (h + 1) * HEAD)
        g0, g1, g2, floor_sum, gain_sum = head_backward(
            p0, p1, p2, mixed_grad[:, lanes], col_ref[0], row_ref[0], floor_ref[:, lanes],
            gain_ref[...], scores.at[h], key_grad.at[h], decay_grad.at[h], query_grad.at[h],
        )
        for j, g in enumerate((g0, g1, g2)):
            parts[:, pl.ds(j * width + h * HEAD, HEAD)] = g
        floor_sum_ref[0, :, lanes] = jnp.broadcast_to(floor_sum, (8, HEAD)) * 0.125
        gain_sum_ref[0, :, lanes] = jnp.broadcast_to(gain_sum, (8, HEAD)) * 0.125

    g_one_ref[0] = parts[:, : 2 * width]
    g_two_ref[0] = parts[:, 2 * width :]
    back[...] = dot(parts[...], weight[:, : 3 * width], NT)
    send_ref[0] = back[pl.ds(theirs, count), :].astype(BF)
    keep_ref[0] = back[pl.ds(mine, count), :]


def mixer_specs(count, model, width, length):
    def at(shape, index):
        return pl.BlockSpec(shape, lambda s, c, o: index(s))

    side = at((1, count, model), lambda s: (s, 0, 0))
    col = at((1, length, 1), lambda s: (s, 0, 0))
    row = at((1, 1, length), lambda s: (s, 0, 0))
    floor = at((1, width), lambda s: (0, 0))
    gain = at((1, HEAD), lambda s: (0, 0))
    wide = at((1, length, 3 * width), lambda s: (s, 0, 0))
    pairs = [at((1, length, k * width), lambda s: (s, 0, 0)) for k in (1, 2)]
    return at, side, wide, pairs, [col, row, floor, gain]


def weight_scratch(model, lanes, sources):
    return [pltpu.VMEM((model, lanes), BF), pltpu.SemaphoreType.DMA((4 * len(sources),))]


def layout_of(sources):
    return tuple((piece, low) for piece, low, _ in sources), [part for _, _, part in sources]


def mixer_forward(core, offsets, tokens, sources, segments, floor, gain):
    groups, length = segments.shape
    count, model = tokens[0].shape
    width = floor.shape[0]
    half = (groups, count, model)
    at, side, wide, pairs, small = mixer_specs(count, model, width, length)
    layout, parts = layout_of(sources)
    shape = jax.ShapeDtypeStruct
    return pl.pallas_call(
        functools.partial(mixer_forward_kernel, sources=layout),
        grid_spec=pltpu.PrefetchScalarGridSpec(
            num_scalar_prefetch=2,
            grid=(groups,),
            in_specs=[pl.BlockSpec(memory_space=pl.ANY)] * (6 + len(parts)) + small,
            out_specs=[wide, pairs[0], side, side],
            scratch_shapes=[
                pltpu.VMEM((width // HEAD, length, length), BF),
                pltpu.VMEM((length, width), BF),
                pltpu.VMEM((length, model), jnp.float32),
            ]
            + row_scratch(count, model)
            + weight_scratch(model, 4 * width, parts),
        ),
        out_shape=[
            shape((groups, length, 3 * width), jnp.float32),
            shape((groups, length, width), BF),
            shape(half, BF),
            shape(half, jnp.float32),
        ],
        compiler_params=PARAMS,
        cost_estimate=LONG,
        name="mixer_forward",
    )(
        core, offsets, *tokens, *parts, segments[:, :, None],
        segments[:, None, :], floor[None], gain[None],
    )


def mixer_backward(core, offsets, tokens, sources, projected, segments, floor, gain):
    groups, length = segments.shape
    count, model = tokens[0].shape
    width = floor.shape[0]
    half = (groups, count, model)
    at, side, wide, pairs, small = mixer_specs(count, model, width, length)
    layout, parts = layout_of(sources)
    heads = width // HEAD
    sums = at((1, 8, width), lambda s: (s, 0, 0))
    shape = jax.ShapeDtypeStruct
    return pl.pallas_call(
        functools.partial(mixer_backward_kernel, sources=layout),
        grid_spec=pltpu.PrefetchScalarGridSpec(
            num_scalar_prefetch=2,
            grid=(groups,),
            in_specs=[pl.BlockSpec(memory_space=pl.ANY)] * (6 + len(parts))
            + [wide]
            + small,
            out_specs=[pairs[1], pairs[0], side, side, sums, sums],
            scratch_shapes=[pltpu.VMEM((heads, length, length), BF)]
            + [pltpu.VMEM((heads, length, HEAD), jnp.float32)] * 3
            + [pltpu.VMEM((length, width), jnp.float32), pltpu.VMEM((length, 3 * width), BF)]
            + [pltpu.VMEM((length, model), jnp.float32)]
            + row_scratch(count, model)
            + weight_scratch(model, 4 * width, parts),
        ),
        out_shape=[
            shape((groups, length, 2 * width), BF),
            shape((groups, length, width), BF),
            shape(half, BF),
            shape(half, jnp.float32),
        ]
        + [shape((groups, 8, width), jnp.float32)] * 2,
        compiler_params=PARAMS,
        cost_estimate=LONG,
        name="mixer_backward",
    )(
        core, offsets, *tokens, *parts, projected, segments[:, :, None],
        segments[:, None, :], floor[None], gain[None],
    )


def ffn_kernel(core_ref, offsets_ref, *refs, sources, units):
    rows, tops, refs = refs[:6], refs[6:12], refs[12:]
    (*parts, send_ref, keep_ref, grads, back,
     tokens, token_sems, top_tokens, top_sems, weight, sems) = refs[len(sources) :]

    sequence = pl.program_id(0)

    @pl.when(sequence == 0)
    def _():
        start_rows(core_ref[0], rows, tokens, token_sems)
        start_rows(core_ref[0], tops, top_tokens, top_sems)
        load_weight(offsets_ref, sources, refs, weight, sems)

    wait_rows(core_ref[0], rows, tokens, token_sems, sequence)
    wait_rows(core_ref[0], tops, top_tokens, top_sems, sequence)

    width = units
    count = rows[0].shape[0]
    mine = pl.multiple_of(core_ref[0] * count, count)
    theirs = pl.multiple_of((1 - core_ref[0]) * count, count)
    both = dot(tokens[sequence], weight[:, : 2 * width])
    gate, up = both[:, :width], both[:, width:]
    active_grad = dot(top_tokens[sequence], weight[:, 2 * width : 3 * width])
    squash = jax.nn.sigmoid(gate)
    swish = gate * squash
    gate_grad = active_grad * up * squash * (1.0 + gate * (1.0 - squash))
    grads[:, : 2 * width] = jnp.concatenate([gate_grad, active_grad * swish], axis=1).astype(BF)
    spare = jnp.zeros((2 * count, grads.shape[1] - 3 * width), BF)
    grads[:, 2 * width :] = jnp.concatenate([(swish * up).astype(BF), spare], axis=1)
    low = 0
    for part_ref in parts:
        part_ref[0] = grads[:, low : low + part_ref.shape[2]]
        low += part_ref.shape[2]
    back[...] = dot(grads[:, : 2 * width], weight[:, : 2 * width], NT)
    send_ref[0] = back[pl.ds(theirs, count), :].astype(BF)
    keep_ref[0] = back[pl.ds(mine, count), :]


def ffn(core, offsets, tokens, tops, sources, width, widths):
    count, model = tokens[0].shape
    groups, length = 4, 2 * count
    total = sum(widths)
    layout, parts = layout_of(sources)

    def at(rows, lanes):
        return pl.BlockSpec((1, rows, lanes), lambda s, c, o: (s, 0, 0))

    shape = jax.ShapeDtypeStruct
    return pl.pallas_call(
        functools.partial(ffn_kernel, sources=layout, units=width),
        grid_spec=pltpu.PrefetchScalarGridSpec(
            num_scalar_prefetch=2,
            grid=(groups,),
            in_specs=[pl.BlockSpec(memory_space=pl.ANY)] * (12 + len(parts)),
            out_specs=[at(length, n) for n in widths] + [at(length // 2, model)] * 2,
            scratch_shapes=[
                pltpu.VMEM((length, total), BF),
                pltpu.VMEM((length, model), jnp.float32),
            ]
            + row_scratch(count, model) * 2
            + weight_scratch(model, total, parts),
        ),
        out_shape=[
            *[shape((groups, length, n), BF) for n in widths],
            shape((groups, length // 2, model), BF),
            shape((groups, length // 2, model), jnp.float32),
        ],
        compiler_params=PARAMS,
        cost_estimate=LONG,
        name="ffn",
    )(core, offsets, *tokens, *tops, *parts)


def rows_kernel(core_ref, offsets_ref, *refs, sources, begin, number):
    own, refs = refs[:number], refs[number:]
    out_ref, whole, sems = refs[len(sources) :]

    @pl.when(pl.program_id(0) == 0)
    def _():
        load_weight(offsets_ref, sources, refs, whole, sems, begin)

    out_ref[0] = dot(jnp.concatenate([r[0] for r in own], axis=1), whole[...], NT).astype(BF)


def rows_product(core, offsets, own, sources, begin, model, estimate=SHORT):
    groups, length, _ = own[0].shape
    width = sum(o.shape[2] for o in own)
    layout, parts = layout_of(sources)

    def at(rows, lanes):
        return pl.BlockSpec((1, rows, lanes), lambda s, c, o: (s, 0, 0))

    shape = jax.ShapeDtypeStruct
    return pl.pallas_call(
        functools.partial(rows_kernel, sources=layout, begin=begin, number=len(own)),
        grid_spec=pltpu.PrefetchScalarGridSpec(
            num_scalar_prefetch=2,
            grid=(groups,),
            in_specs=[at(length, o.shape[2]) for o in own] + [pl.BlockSpec(memory_space=pl.ANY)] * len(parts),
            out_specs=pl.BlockSpec((1, length, model), lambda s, c, o: (s ^ c[1], 0, 0)),
            scratch_shapes=weight_scratch(model, width, parts),
        ),
        out_shape=shape((groups, length, model), BF),
        compiler_params=PARAMS,
        cost_estimate=estimate,
        name="rows_product",
    )(core, offsets, *own, *parts)


def grad_kernel(core_ref, blocks_ref, *refs, number):
    rows, grads, outs, tokens = refs[:6], refs[6 : 6 + number], refs[6 + number : -1], refs[-1]
    count = rows[0].shape[0]
    for side in range(2):
        at = core_ref[0] if side == 0 else 1 - core_ref[0]
        for m in range(4):
            first = pl.multiple_of((2 * m + at) * count, count)
            part = rows[m][...] if side == 0 else rows[4][m] if m < 3 else rows[5][...]
            tokens[pl.ds(first, count), :] = part
    for grad_ref, out_ref in zip(grads, outs):
        out_ref[0] = dot(tokens[...], grad_ref[...], TN).astype(out_ref.dtype)


def grad_product(core, tokens, grads, blocks, wide, kind, estimate):
    count, model = tokens[0].shape
    side = pl.BlockSpec((count, wide), lambda i, c, b: (0, b[i]))
    three = pl.BlockSpec((3, count, wide), lambda i, c, b: (0, 0, b[i]))
    number = blocks.shape[0]
    return pl.pallas_call(
        functools.partial(grad_kernel, number=len(grads)),
        grid_spec=pltpu.PrefetchScalarGridSpec(
            num_scalar_prefetch=2,
            grid=(number,),
            in_specs=[side] * 4
            + [three, side]
            + [pl.BlockSpec(g.shape, lambda i, c, b: (0, 0)) for g in grads],
            out_specs=[pl.BlockSpec((1, wide, g.shape[1]), lambda i, c, b: (i, 0, 0)) for g in grads],
            scratch_shapes=[pltpu.VMEM((8 * count, wide), BF)],
        ),
        out_shape=[jax.ShapeDtypeStruct((number, wide, g.shape[1]), kind) for g in grads],
        compiler_params=PARAMS,
        cost_estimate=estimate,
        name="grad_product",
    )(core, blocks, *tokens, *grads)


def rms_of(values):
    return lax.rsqrt(jnp.mean(values * values, axis=-1, keepdims=True) + epsilon)


def cores_kernel(keep_ref, came_ref, own_ref, x_ref, z_ref, xz_ref):
    own_ref[...] = keep_ref[0] + came_ref[0].astype(jnp.float32)
    for m, out_ref in enumerate((x_ref, z_ref, xz_ref), 1):
        out_ref[...] = (keep_ref[m] + came_ref[m].astype(jnp.float32)).astype(BF)


def add_cores(keep, came, estimate=SHORT):
    count, model = keep.shape[1:]
    block = count // 4
    both = pl.BlockSpec((4, block, model), lambda i: (0, i, 0))
    one = pl.BlockSpec((block, model), lambda i: (i, 0))
    shape = jax.ShapeDtypeStruct
    return pl.pallas_call(
        cores_kernel,
        grid=(4,),
        in_specs=[both, both],
        out_specs=[one] * 4,
        out_shape=[shape((count, model), jnp.float32)] + [shape((count, model), BF)] * 3,
        compiler_params=PARAMS,
        cost_estimate=estimate,
        name="add_cores",
    )(keep, came)


def middle_kernel(own_ref, x_ref, z_ref, hidden_ref, gain_ref, middle_ref, normed_ref):
    branch = own_ref[...] + x_ref[...].astype(jnp.float32) + z_ref[...].astype(jnp.float32)
    middle = hidden_ref[...].astype(jnp.float32) + branch
    middle_ref[...] = middle
    normed_ref[...] = (middle * rms_of(middle) * gain_ref[...]).astype(BF)


def back_kernel(own_ref, x_ref, z_ref, values_ref, add_ref, gain_ref, out_ref, low_ref, sum_ref):
    grad = own_ref[...] + x_ref[...].astype(jnp.float32) + z_ref[...].astype(jnp.float32)
    values = values_ref[...].astype(jnp.float32)
    scale = rms_of(values)
    unit = values * scale
    wide = grad * gain_ref[...]
    inner = wide - unit * jnp.mean(wide * unit, axis=-1, keepdims=True)
    out = add_ref[...].astype(jnp.float32) + scale * inner
    out_ref[...] = out
    low_ref[...] = out.astype(BF)

    @pl.when(pl.program_id(0) == 0)
    def _():
        sum_ref[...] = jnp.zeros_like(sum_ref)

    sum_ref[...] += jnp.sum(grad * unit, axis=0, keepdims=True)


def row_call(kernel, name, kinds, *args):
    count, model = args[0].shape
    block = count // 4

    def spec(one):
        if one:
            return pl.BlockSpec((1, model), lambda i: (0, 0))
        return pl.BlockSpec((block, model), lambda i: (i, 0))

    shapes = [jax.ShapeDtypeStruct((1 if k is None else count, model), k or jnp.float32) for k in kinds]
    return pl.pallas_call(
        kernel,
        grid=(4,),
        in_specs=[spec(a.shape[0] == 1) for a in args],
        out_specs=[spec(k is None) for k in kinds],
        out_shape=shapes,
        compiler_params=PARAMS,
        cost_estimate=LONG,
        name=name,
    )(*args)


def mix_grad_kernel(parts_ref, out_ref):
    quarter = parts_ref.shape[2] // 4
    for j, at in enumerate((2, 3, 0, 1)):
        for m in range(4):
            part = parts_ref[m, :, at * quarter : (at + 1) * quarter]
            out_ref[:, j, m * quarter : (m + 1) * quarter] = part.astype(jnp.float32)


def mix_grad_of(parts):
    _, rows, wide = parts.shape
    block = min(rows, 32)
    return pl.pallas_call(
        mix_grad_kernel,
        grid=(rows // block,),
        in_specs=[pl.BlockSpec((4, block, wide), lambda i: (0, i, 0))],
        out_specs=pl.BlockSpec((block, 4, wide), lambda i: (i, 0, 0)),
        out_shape=jax.ShapeDtypeStruct((rows, 4, wide), jnp.float32),
        compiler_params=PARAMS,
        cost_estimate=SHORT,
        name="mix_grad",
    )(parts)


DOWN_FIRST = 384


def ffn_grad_kernel(first_ref, second_ref, out_ref):
    units = out_ref.shape[2] // 4
    for j in range(3):
        parts = []
        for m in range(4):
            down = first_ref.shape[2] - DOWN_FIRST
            gates = jnp.concatenate([first_ref[m, :, down:], second_ref[m]], axis=1)
            parts.append(first_ref[m, :, :units] if j == 2 else gates[:, j * units : (j + 1) * units])
        out_ref[j] = jnp.concatenate(parts, axis=1).astype(jnp.float32)


def ffn_grad_of(parts, units):
    rows = parts[0].shape[1]
    block = min(rows, 32)
    out = pl.pallas_call(
        ffn_grad_kernel,
        grid=(rows // block,),
        in_specs=[pl.BlockSpec((4, block, p.shape[2]), lambda i: (0, i, 0)) for p in parts],
        out_specs=pl.BlockSpec((3, block, 4 * units), lambda i: (0, i, 0)),
        out_shape=jax.ShapeDtypeStruct((3, rows, 4 * units), jnp.float32),
        compiler_params=PARAMS,
        cost_estimate=LONG,
        name="ffn_grad",
    )(*parts)
    return out.transpose(1, 0, 2)


def near_kernel(*refs, number, ends):
    home_ref, away_ref = refs[2 * number :]
    block = pl.program_id(0)
    last = pl.num_programs(0) // ends
    for k in range(number):
        keep_ref, came_ref = refs[2 * k], refs[2 * k + 1]
        low = sum(refs[2 * j].shape[2] for j in range(k))
        total = keep_ref[0] + came_ref[0].astype(jnp.float32)
        lanes = slice(low, low + keep_ref.shape[2])

        @pl.when(block < pl.num_programs(0) - last)
        def _():
            away_ref[0, :, lanes] = total.astype(BF)

        @pl.when(block >= pl.num_programs(0) - last)
        def _():
            home_ref[0, :, lanes] = total


def near_sums(pairs, estimate=SHORT):
    highs = lax.axis_size("h")
    blocks, rows, _ = pairs[0][0].shape
    away_count = blocks - 2
    wide = sum(keep.shape[2] for keep, _ in pairs)
    specs, args = [], []
    for pair in pairs:
        specs += [pl.BlockSpec((1,) + pair[0].shape[1:], lambda i: (i, 0, 0))] * 2
        args += list(pair)
    home, away = pl.pallas_call(
        functools.partial(near_kernel, number=len(pairs), ends=highs),
        grid=(blocks,),
        in_specs=specs,
        out_specs=[
            pl.BlockSpec((1, rows, wide), lambda i: (jnp.maximum(i - away_count, 0), 0, 0)),
            pl.BlockSpec((1, rows, wide), lambda i: (jnp.minimum(i, away_count - 1), 0, 0)),
        ],
        out_shape=[
            jax.ShapeDtypeStruct((2, rows, wide), jnp.float32),
            jax.ShapeDtypeStruct((away_count, rows, wide), BF),
        ],
        compiler_params=PARAMS,
        cost_estimate=estimate,
        name="near_sums",
    )(*args)
    return home, [away[2 * k : 2 * k + 2] for k in range(highs - 1)]


def far_kernel(*refs, counts):
    out_ref = refs[-1]
    low, at = 0, 0
    for count in counts:
        total = refs[at][0]
        for ref in refs[at + 1 : at + 1 + count]:
            total = total + ref[0].astype(jnp.float32)
        out_ref[0, :, low : low + total.shape[1]] = total.astype(BF)
        low, at = low + total.shape[1], at + 1 + count


def far_sums(pairs, estimate=SHORT):
    _, rows, _ = pairs[0][0].shape
    wide = sum(home.shape[2] for home, _ in pairs)
    args = [part for home, fars in pairs for part in (home, *fars)]
    out = pl.pallas_call(
        functools.partial(far_kernel, counts=[len(fars) for _, fars in pairs]),
        grid=(2,),
        in_specs=[pl.BlockSpec((1,) + a.shape[1:], lambda i: (i, 0, 0)) for a in args],
        out_specs=pl.BlockSpec((1, rows, wide), lambda i: (i, 0, 0)),
        out_shape=jax.ShapeDtypeStruct((2, rows, wide), BF),
        compiler_params=PARAMS,
        cost_estimate=estimate,
        name="far_sums",
    )(*args)
    return out.reshape(4, rows // 2, wide)


GROUP = ("l", "x")


def swap(values, axes):
    total = 2 ** len(axes)
    return lax.ppermute(values, axes, [(s, total - 1 - s) for s in range(total)])


def shift(values, steps):
    total = lax.axis_size("h")
    return lax.ppermute(values, "h", [(s, (s + steps) % total) for s in range(total)])


def pick(values, index):
    return lax.dynamic_index_in_dim(values, index, 0, keepdims=False)


def over_c(values):
    return swap(values, ("tensor",))


def over_x(values):
    return swap(values, ("x",))


def over_y(values):
    return swap(values, ("y",))


def over_z(values):
    return swap(values, ("l",))


def own_member():
    return lax.axis_index("l") * 2 + lax.axis_index("x")


def source_rows(rows):
    y, high = lax.axis_index("y"), lax.axis_index("h")
    highs = lax.axis_size("h")
    starts = []
    for k in range(highs):
        for side in (y, 1 - y):
            for member in range(4):
                block = ((high - k) % highs) * 8 + (member >> 1) * 4 + side * 2 + (member & 1)
                starts.append(block * rows)
    return jnp.stack(starts).astype(jnp.int32)


def trade(slices):
    return lax.all_to_all(slices, GROUP, 0, 0, tiled=True)


def after(values, *others):
    return lax.optimization_barrier((values, others))[0]


def far(block):
    return [shift(block, k) for k in range(1, lax.axis_size("h"))]


def near(parts):
    return [over_y(part) for part in parts]


def pieces(low, straight, crossed):
    out = []
    for k, (one, two) in enumerate(zip(straight, crossed), 1):
        out += [(2 * k, low, one), (2 * k + 1, low, two)]
    return out


def half_grads(core, tokens, grads, yy, kind, estimate):
    highs, high = lax.axis_size("h"), lax.axis_index("h")
    wide = tokens[0].shape[1] // (4 * highs)
    order = [(high + k) % highs for k in range(1, highs)] + [high]
    blocks = jnp.stack([(h * 2 + z) * 2 + yy for h in order for z in range(2)]).astype(jnp.int32)
    grads = [flat(g) for g in grads]
    if wide % 128 == 0:
        return grad_product(core, tokens, grads, blocks, wide, kind, estimate)
    sides = [jnp.stack(tokens[:4]), jnp.concatenate([tokens[4], tokens[5][None]])]
    ordered = [jnp.where(core[0] == 0, a, b) for a, b in (sides, sides[::-1])]
    whole = jnp.stack(ordered, axis=1)
    split = jnp.take(whole.reshape(grads[0].shape[0], -1, wide), blocks, axis=1)
    return [
        jnp.einsum("tad,tx->adx", split, g, preferred_element_type=jnp.float32).astype(kind)
        for g in grads
    ]


def grad_sends(core, tokens, grads, estimate=SHORT):
    return half_grads(core, tokens, grads, 1 - lax.axis_index("y"), BF, estimate)


def grad_keeps(core, tokens, grads, estimate=SHORT):
    return half_grads(core, tokens, grads, lax.axis_index("y"), jnp.float32, estimate)


def send_far(away):
    return [shift(part, k) for k, part in enumerate(away, 1)]


def flat(values):
    return values.reshape(-1, values.shape[-1])


def add_low(keep, came):
    return (keep.astype(jnp.float32) + came.astype(jnp.float32)).astype(BF)


def sum_highs(values):
    size, bits = lax.axis_size("h"), 1
    while bits < size:
        values = values + lax.ppermute(values, "h", [(s, s ^ bits) for s in range(size)])
        bits *= 2
    return values


def body(
    hidden_in,
    segments,
    mix_weights,
    ffn_weights,
    norm1_gain,
    norm2_gain,
    head_gain,
    lower_bound,
    out_grad,
):
    core, member = lax.axis_index("tensor"), own_member()
    core_at = jnp.stack([core, member]).astype(jnp.int32)
    rows = mix_weights.shape[0]
    offsets = source_rows(rows)
    quarter, units = lower_bound.shape[0] // 4, ffn_weights.shape[2] // 4
    model = hidden_in.shape[1]
    channels = 4 * quarter
    lanes = -(-3 * units // 128) * 128

    def slices(weights, width):
        split = weights.reshape(rows, weights.shape[1], 4, -1).transpose(2, 0, 1, 3)
        split = split.reshape(4, rows, -1)
        return jnp.pad(split, ((0, 0), (0, 0), (0, width - split.shape[2])))

    length = segments.shape[1]
    labels = jnp.pad(segments.astype(BF), ((0, 15), (0, channels - length)))
    labels = jnp.broadcast_to(labels, (4,) + labels.shape)
    hidden = hidden_in.astype(jnp.float32)
    scale_one = rms_of(hidden)
    normed = (hidden * scale_one * norm1_gain).astype(BF)
    floor = lax.dynamic_slice_in_dim(lower_bound, member * quarter, quarter)
    feed = slices(ffn_weights, lanes)
    mix = slices(mix_weights, channels)

    mix = trade(jnp.concatenate([slices(mix_weights, channels), labels], axis=1))

    gate = (mix, normed, feed)
    mix, normed, feed = lax.optimization_barrier(gate)
    labels = mix[:, rows, :length].astype(jnp.int32)
    labels = jnp.stack([pick(labels, member ^ m) for m in range(4)])
    mix = mix[:, :rows]
    cuts = [0, 384, 768, 1024, 1408, 1664, 1920, lanes]
    feed_cut = cuts[4]
    mix_far = far(mix)
    mix_near = over_y(mix)
    feed_one = trade(feed[..., :feed_cut])
    feed_rest = after(feed[..., feed_cut:], gate)
    normed_x, normed_z = over_x(normed), over_z(normed)
    top_x = over_x(after(out_grad, gate))

    gate = (mix_far, mix_near, feed_one, feed_rest, normed_x, normed_z, top_x)
    mix_cross = near(after(mix_far, gate))
    ones = [feed_one[..., low:high] for low, high in zip(cuts[:4], cuts[1:5])]
    far_a = far(after(ones[0], gate))
    normed_xz = over_x(after(normed_z, gate))
    normed_three = jnp.stack(after([normed, normed_x, normed_z], gate))
    top_z = over_z(after(out_grad, gate))

    gate = (mix_cross, far_a, normed_xz, normed_three, top_z, ones)
    normed_c, normed_cxz = over_c(after(normed_three, gate)), over_c(after(normed_xz, gate))
    top_three = jnp.stack(after([out_grad, top_x, top_z], gate))
    normed = [normed, normed_x, normed_z, normed_xz, normed_c, normed_cxz]
    mix_sources = [(0, 0, mix), (1, 0, mix_near)] + pieces(0, mix_far, mix_cross)

    gate = (normed_c, normed_cxz, top_three)
    far_b = far(after(ones[1], gate))
    near_a = over_y(after(feed_one[..., :640], gate))
    cross_a = near(after(far_a, gate))
    top_xz = over_x(after(top_z, gate))
    projected, mixed, send, keep = mixer_forward(
        core_at, offsets, after(normed, gate), mix_sources, labels, floor, head_gain
    )

    gate = (send, far_b, near_a, cross_a, top_xz)
    came = over_c(after(send, gate))
    far_c = far(after(ones[2], gate))
    near_b = over_y(after(feed_one[..., 640:1024], gate))
    feed_two = trade(after(feed_rest, gate))
    top_c = over_c(after(top_three, gate))
    own, to_x, to_z, to_xz = add_cores(keep, came)

    gate = (own, far_c, near_b, top_c)
    from_x = over_x(after(to_xz, gate))
    far_d = far(after(ones[3], gate))
    near_c = over_y(after(feed_one[..., 1024:], gate))
    cross_b = near(after(far_b, gate))
    top_cxz = over_c(after(top_xz, gate))
    tops = [out_grad, top_x, top_z, top_xz, top_c, top_cxz]

    gate = (from_x, far_d, near_c, cross_b, top_cxz, feed_two)
    to_z = add_low(to_z, after(from_x, gate))
    of_x = over_x(after(to_x, gate))
    of_z = over_z(to_z)
    far_e = far(after(feed_two[..., : cuts[5] - feed_cut], gate))
    near_d = over_y(after(feed_two, gate))

    gate = (of_x, of_z, far_e, near_d)
    far_f = far(after(feed_two[..., cuts[5] - feed_cut : cuts[6] - feed_cut], gate))
    cross_c, cross_d = near(after(far_c, gate)), near(after(far_d, gate))
    middle, normed_two = row_call(
        middle_kernel, "middle", [jnp.float32, BF], *after((own, of_x, of_z), gate), hidden_in,
        norm2_gain[None],
    )
    two_x, two_z = over_x(normed_two), over_z(normed_two)

    gate = (far_f, cross_c, cross_d, two_x, two_z)
    far_g = far(after(feed_two[..., cuts[6] - feed_cut :], gate))
    cross_e, cross_f = near(after(far_e, gate)), near(after(far_f, gate))
    two_xz = over_x(after(two_z, gate))
    two_three = jnp.stack(after([normed_two, two_x, two_z], gate))

    gate = (far_g, cross_e, cross_f, two_xz, two_three)
    cross_g = near(after(far_g, gate))
    two_c, two_cxz = over_c(after(two_three, gate)), over_c(after(two_xz, gate))
    normed_two = [normed_two, two_x, two_z, two_xz, two_c, two_cxz]
    feed_sources = [(0, 0, feed_one), (0, feed_cut, feed_two)]
    feed_sources += [(1, 0, near_a), (1, 640, near_b), (1, 1024, near_c), (1, feed_cut, near_d)]
    fars = [far_a, far_b, far_c, far_d, far_e, far_f, far_g]
    crosses = [cross_a, cross_b, cross_c, cross_d, cross_e, cross_f, cross_g]
    for low, straight, crossed in zip(cuts, fars, crosses):
        feed_sources += pieces(low, straight, crossed)

    widths = [128, 256, 384, 256, 384, 256, 256, lanes - 1920]
    *grads, send, keep = ffn(core_at, offsets, normed_two, tops, feed_sources, units, widths)
    gates, downs = grads[:5], grads[5:]
    came = over_c(send)
    down_sends = grad_sends(core_at, after(tops, send), downs, LONG)
    own, to_x, to_z, to_xz = add_cores(keep, after(came, down_sends))

    gate = (own,)
    from_x = over_x(after(to_xz, gate))
    down_one = over_y(after(down_sends[0], gate))
    gate_sends = grad_sends(core_at, after(normed_two, gate), gates, LONG)

    gate = (from_x, down_one, gate_sends)
    to_z = add_low(to_z, after(from_x, gate))
    of_x = over_x(after(to_x, gate))
    of_z = over_z(to_z)
    down_two = over_y(after(down_sends[1], gate))
    down_keeps = grad_keeps(core_at, after(tops, gate), downs, LONG)
    down_home, down_away = near_sums([(down_keeps[0], after(down_one, gate))])

    gate = (of_x, of_z, down_two, down_away)
    down_fars = send_far(after(down_away, gate))
    down_three = over_y(after(down_sends[2], gate))
    one_came = over_y(after(gate_sends[0], gate))
    middle_grad, middle_low, gain_two_grad = row_call(
        back_kernel, "middle_grad", [jnp.float32, BF, None], *after((own, of_x, of_z), gate),
        middle, out_grad, norm2_gain[None],
    )
    grad_x, grad_z = over_x(middle_low), over_z(middle_low)
    gate_keeps = grad_keeps(core_at, after(normed_two, middle_low), gates, LONG)
    down_home_two, down_away_two = near_sums(
        [(after(down_keeps[1], gate_keeps), after(down_two, gate))]
    )

    gate = (grad_x, grad_z, down_three, one_came, down_away_two, down_fars)
    down_fars_two = send_far(after(down_away_two, gate))
    two_came = over_y(after(gate_sends[1], gate))
    grad_xz = over_x(after(grad_z, gate))
    grad_three = jnp.stack(after([middle_low, grad_x, grad_z], gate))
    branch = rows_product(
        core_at, offsets, after(downs, gate), feed_sources, 2 * units, model, LONG
    )

    gate = (grad_xz, grad_three, branch, down_fars_two, two_came)
    grad_c, grad_cxz = over_c(after(grad_three, gate)), over_c(after(grad_xz, gate))
    one_home, one_away = near_sums(
        [
            (down_keeps[2], after(down_three, gate)),
            (gate_keeps[0], after(one_came, gate)),
            (gate_keeps[1], after(two_came, gate)),
        ],
        LONG,
    )
    middle_full = [middle_low, grad_x, grad_z, grad_xz, grad_c, grad_cxz]

    gate = (grad_c, grad_cxz, one_away)
    one_fars = send_far(after(one_away, gate))
    three_came, four_came = [over_y(after(part, gate)) for part in gate_sends[2:4]]
    branch = lax.psum_scatter(
        after(branch, gate).reshape(-1, model), GROUP + ("tensor",), scatter_dimension=0, tiled=True
    )
    middle_full = after(middle_full, gate)
    g_one, g_two, send, keep, floor_sums, gain_sums = mixer_backward(
        core_at, offsets, middle_full, mix_sources, projected, labels, floor, head_gain
    )

    gate = (send, one_fars, three_came, four_came)
    came = over_c(after(send, gate))
    five_came = over_y(after(gate_sends[4], gate))
    three_home, three_away = near_sums([(gate_keeps[2], after(three_came, gate))], LONG)
    own, to_x, to_z, to_xz = add_cores(keep, after(came, three_away))

    gate = (own,)
    three_fars = send_far(after(three_away, gate))
    from_x = over_x(after(to_xz, gate))
    value_send, pair_send = grad_sends(core_at, after(normed, gate), [g_two, g_one], LONG)
    (last_send,) = grad_sends(core_at, after(middle_full, value_send), [mixed])
    four_home, four_away = near_sums([(gate_keeps[3], after(four_came, last_send))])

    gate = (from_x, three_fars, four_away, five_came)
    four_fars = send_far(after(four_away, gate))
    to_z = add_low(to_z, after(from_x, gate))
    of_x = over_x(after(to_x, gate))
    of_z = over_z(to_z)
    value_came, last_came = over_y(after(value_send, gate)), over_y(after(last_send, gate))
    value_keep, pair_keep = grad_keeps(core_at, after(normed, gate), [g_two, g_one], LONG)
    five_home, five_away = near_sums([(gate_keeps[4], after(five_came, value_keep))])
    (last_keep,) = grad_keeps(core_at, after(middle_full, five_away), [mixed])

    gate = (of_x, of_z, four_fars, value_came, last_came, last_keep)
    five_fars = send_far(after(five_away, gate))
    query_came = over_y(after(pair_send[..., :quarter], gate))
    input_grad, _, gain_one_grad = row_call(
        back_kernel, "input_grad", [jnp.float32, BF, None], *after((own, of_x, of_z), gate),
        hidden_in, middle_grad, norm1_gain[None],
    )
    near_home, near_away = near_sums(
        [(value_keep, after(value_came, input_grad)), (last_keep, last_came)]
    )
    down_parts = [(down_home, down_fars), (down_home_two, down_fars_two), (one_home, one_fars)]
    down_parts = far_sums(after(down_parts, near_away))
    head_grad = jnp.sum(after(gain_sums, gate).reshape(-1, HEAD), axis=0)
    lower_grad = jnp.zeros((2, 4, quarter), jnp.float32)
    lower_grad = lax.dynamic_update_slice(
        lower_grad,
        jnp.sum(after(floor_sums, gate), axis=(0, 1)).reshape(1, 1, quarter),
        (core, member, 0),
    )
    sums = [gain_one_grad[0], gain_two_grad[0], head_grad, lower_grad.reshape(-1)]
    sums = jnp.concatenate(sums).reshape(-1, HEAD)

    gate = (five_fars, query_came, near_away, down_parts, sums)
    near_fars = send_far(after(near_away, gate))
    forget_came = over_y(after(pair_send[..., quarter:], gate))
    down_parts = trade(after(down_parts, gate))
    sums_x = over_x(after(sums, gate))
    block_out = (middle + after(branch, gate).astype(jnp.float32)).astype(BF)
    gate_parts = [(three_home, three_fars), (four_home, four_fars), (five_home, five_fars)]
    gate_parts = far_sums(after(gate_parts, gate))
    pair_came = jnp.concatenate([query_came, after(forget_came, gate_parts)], axis=-1)
    pair_home, pair_away = near_sums([(pair_keep, pair_came)])

    gate = (near_fars, down_parts, sums_x, pair_away, gate_parts, block_out)
    pair_fars = send_far(after(pair_away, gate))
    gate_parts = trade(after(gate_parts, gate))
    sums = sums + sums_x
    sums_z = over_z(after(sums, gate))

    gate = (pair_fars, gate_parts, sums_z)
    mix_parts = trade(far_sums(after([(near_home, near_fars), (pair_home, pair_fars)], gate)))
    ffn_grad = ffn_grad_of(after([down_parts, gate_parts], gate), units)
    sums = sums + sums_z
    sums = sums + over_y(after(sums, gate))
    sums = sums + swap(sums, ("tensor",))
    sums = sum_highs(sums).reshape(-1)
    gain_one, gain_two, head, lower = jnp.split(sums, [model, 2 * model, 2 * model + HEAD])
    mix_grad = mix_grad_of(mix_parts)
    return (block_out, input_grad, mix_grad, ffn_grad, gain_one, gain_two, head, lower)


def solution(mesh):
    total, cores = mesh.shape["dp"], mesh.shape["tensor"]
    fine = Mesh(mesh.devices.reshape(total // 8, 2, 2, 2, cores), ("h", "l", "y", "x", "tensor"))
    dp = ("h", "l", "y", "x")
    rows = P(dp + ("tensor",), None)
    weights = P(dp, None, "tensor")
    return jax.shard_map(
        body,
        mesh=fine,
        in_specs=(rows, P(dp, None), weights, weights, P(), P(), P(), P("tensor"), rows),
        out_specs=(rows, rows, weights, weights, P(), P(), P(), P()),
        check_vma=False,
    )
```

```python
import functools

import jax
import jax.numpy as jnp
from jax import lax
from jax.experimental import pallas as pl
from jax.experimental.pallas import tpu as pltpu
from jax.sharding import Mesh, PartitionSpec as P

HEAD = 128
STRIP = 32
CAP = 50.0
BF = jnp.bfloat16
epsilon = 1e-06
PARAMS = pltpu.CompilerParams(vmem_limit_bytes=56 * 1024 * 1024)


LONG, SHORT = [pl.CostEstimate(flops=f, bytes_accessed=1, transcendentals=0) for f in (5 * 10**10, 1)]


NN, NT, TN = ((1,), (0,)), ((1,), (1,)), ((0,), (0,))


def dot(a, b, dims=NN):
    return lax.dot_general(a, b, (dims, ((), ())), preferred_element_type=jnp.float32)


def exact_dot(ones, values):
    high = values.astype(BF)
    rest = values - high.astype(jnp.float32)
    mid = rest.astype(BF)
    tail = (rest - mid.astype(jnp.float32)).astype(BF)
    return dot(ones, high) + dot(ones, mid) + dot(ones, tail)


def gates(p0, p1, floor):
    swish = jax.nn.sigmoid(p0)
    gate = jax.nn.sigmoid(p1)
    return swish, gate, floor + (1.0 - floor) * gate


def masks(seg_col, seg_row):
    length = seg_col.shape[0]
    row = lax.broadcasted_iota(jnp.int32, (length, length), 0)
    col = lax.broadcasted_iota(jnp.int32, (length, length), 1)
    same = seg_col == seg_row
    return same & (col <= row), (col <= row).astype(BF), (same & (col >= row)).astype(BF)


def strips(length):
    return [(s, -(-(s + STRIP) // 128) * 128) for s in range(0, length, STRIP)]


def fill_scores(query, key, totals, allowed, scores, kept=None):
    length = query.shape[0]
    for k, (start, wide) in enumerate(strips(length)):
        rows = slice(start, start + STRIP)
        ref = totals[start + STRIP // 2 - 1 : start + STRIP // 2]
        lead_scale = jnp.exp(totals[rows] - ref)
        trail_scale = jnp.exp(jnp.minimum(ref - totals[:wide], CAP))
        lead = (query[rows] * lead_scale).astype(BF)
        trail = (key[:wide] * trail_scale).astype(BF)
        if kept is not None:
            leads, lead_scales, trails, trail_scales = kept
            leads[rows, :], lead_scales[rows, :] = lead, lead_scale
            trails[k, :wide, :], trail_scales[k, :wide, :] = trail, trail_scale
        part = jnp.where(allowed[rows, :wide], dot(lead, trail, NT), 0.0)
        scores[rows, :wide] = part.astype(BF)
        if wide < length:
            scores[rows, wide:] = jnp.zeros((STRIP, length - wide), BF)


def head_forward(p0, p1, p2, seen, floor, gain, scores):
    swish, gate, forget = gates(p0, p1, floor)
    allowed, tri, _ = seen
    totals = exact_dot(tri, jnp.log(forget))
    fill_scores(p0 * swish, 1.0 - forget, totals, allowed, scores)
    rec = dot(scores[...], p2.astype(BF))
    rms = lax.rsqrt(jnp.mean(rec * rec, axis=-1, keepdims=True) + epsilon)
    return (rec * rms * gain).astype(BF)


def head_backward(
    p0, p1, p2, mixed_grad, seen, carry, floor, gain, scores, key_grad, decay_grad, query_grad, *kept
):
    length = p0.shape[0]
    swish, gate, forget = gates(p0, p1, floor)
    query = p0 * swish
    key = 1.0 - forget
    allowed, tri, later = seen
    totals = exact_dot(tri, jnp.log(forget))
    fill_scores(query, key, totals, allowed, scores, kept)
    value = p2.astype(BF)
    rec = dot(scores[...], value)
    rms = lax.rsqrt(jnp.mean(rec * rec, axis=-1, keepdims=True) + epsilon)
    unit = rec * rms
    scaled = mixed_grad * gain
    rec_grad = rms * (scaled - unit * jnp.mean(scaled * unit, axis=-1, keepdims=True))
    rec_low = rec_grad.astype(BF)
    value_grad = dot(scores[...], rec_low, TN).astype(BF)
    score_grad = jnp.where(allowed, dot(rec_low, value, NT), 0.0).astype(BF)
    key_grad[...] = jnp.zeros_like(key_grad)
    decay_grad[...] = jnp.zeros_like(decay_grad)
    leads, lead_scales, trails, trail_scales = kept
    for k, (start, wide) in enumerate(strips(length)):
        rows = slice(start, start + STRIP)
        lead, lead_scale = leads[rows, :], lead_scales[rows, :]
        trail, trail_scale = trails[k, :wide, :], trail_scales[k, :wide, :]
        part = score_grad[rows, :wide]
        lead_grad = dot(part, trail)
        trail_grad = dot(part, lead, TN)
        query_grad[rows, :] = lead_grad * lead_scale
        key_grad[:wide, :] += trail_grad * trail_scale
        decay_grad[:wide, :] -= trail_grad * trail.astype(jnp.float32)
        decay_grad[rows, :] += lead_grad * lead.astype(jnp.float32)
    forget_grad = exact_dot(later, decay_grad[...]) * carry / forget
    joint = forget_grad - key_grad[...]
    floor_sum = jnp.sum(joint * (1.0 - gate), axis=0, keepdims=True)
    gain_sum = jnp.sum(mixed_grad * unit, axis=0, keepdims=True)
    g0 = (query_grad[...] * swish * (1.0 + p0 * (1.0 - swish))).astype(BF)
    g1 = (joint * (1.0 - floor) * gate * (1.0 - gate)).astype(BF)
    return g0, g1, value_grad, floor_sum, gain_sum


def load_weight(offsets_ref, sources, refs, whole, sems, begin=0):
    end = begin + whole.shape[1]
    copies = []
    for (piece, low), ref in zip(sources, refs):
        rows, lanes = ref.shape[1:]
        first, last = max(low, begin), min(low + lanes, end)
        if first >= last:
            continue
        for m in range(4):
            at = pl.multiple_of(offsets_ref[4 * piece + m], rows)
            copies.append(
                pltpu.make_async_copy(
                    ref.at[m, :, pl.ds(first - low, last - first)],
                    whole.at[pl.ds(at, rows), pl.ds(first - begin, last - first)],
                    sems.at[len(copies)],
                )
            )
    for copy in copies:
        copy.start()
    for copy in copies:
        copy.wait()


def row_copies(core, refs, whole, sems):
    count = refs[0].shape[0]
    for side in range(2):
        at = pl.multiple_of((core if side == 0 else 1 - core) * count, count)
        for m in range(4):
            ref = refs[m] if side == 0 else refs[4].at[m] if m < 3 else refs[5]
            yield m, pltpu.make_async_copy(
                ref, whole.at[m, pl.ds(at, count), :], sems.at[side, m]
            )


def start_rows(core, refs, whole, sems):
    for _, copy in row_copies(core, refs, whole, sems):
        copy.start()


def wait_rows(core, refs, whole, sems, sequence):
    for m, copy in row_copies(core, refs, whole, sems):

        @pl.when(sequence == m)
        def _():
            copy.wait()


def row_scratch(count, model):
    return [pltpu.VMEM((4, 2 * count, model), BF), pltpu.SemaphoreType.DMA((2, 4))]


def store_sends(values, send_ref, last_ref):
    sequence = pl.program_id(0)

    @pl.when(sequence < 3)
    def _():
        send_ref[0] = values.astype(BF)

    @pl.when(sequence == 3)
    def _():
        last_ref[...] = values.astype(BF)


def mixer_forward_kernel(core_ref, offsets_ref, *refs, sources):
    rows, refs = refs[:6], refs[6:]
    (col_ref, row_ref, floor_ref, gain_ref, p_ref, mixed_ref, send_ref, last_ref, keep_ref, scores, whole,
     back, tokens, token_sems, weight, sems) = refs[len(sources) :]

    sequence = pl.program_id(0)

    @pl.when(sequence == 0)
    def _():
        start_rows(core_ref[0], rows, tokens, token_sems)
        load_weight(offsets_ref, sources, refs, weight, sems)

    wait_rows(core_ref[0], rows, tokens, token_sems, sequence)

    count = rows[0].shape[0]
    width = whole.shape[1]
    mine = pl.multiple_of(core_ref[0] * count, count)
    theirs = pl.multiple_of((1 - core_ref[0]) * count, count)
    p_ref[0] = dot(tokens[sequence], weight[:, : 3 * width])
    seen = masks(col_ref[0], row_ref[0])
    for h in range(width // HEAD):
        p0, p1, p2 = [p_ref[0, :, pl.ds(j * width + h * HEAD, HEAD)] for j in range(3)]
        lanes = slice(h * HEAD, (h + 1) * HEAD)
        whole[:, lanes] = head_forward(
            p0, p1, p2, seen, floor_ref[:, lanes], gain_ref[...], scores.at[h]
        )
    mixed_ref[0] = whole[...]
    back[...] = dot(whole[...], weight[:, 3 * width :], NT)
    store_sends(back[pl.ds(theirs, count), :], send_ref, last_ref)
    keep_ref[0] = back[pl.ds(mine, count), :]


def mixer_backward_kernel(core_ref, offsets_ref, *refs, sources):
    rows, refs = refs[:6], refs[6:]
    (p_ref, col_ref, row_ref, floor_ref, gain_ref, g0_ref, g1_ref, g2_ref, send_ref, last_ref, keep_ref,
     floor_sum_ref, gain_sum_ref, scores, key_grad, decay_grad, query_grad, *kept, mixed_grad, parts,
     back, tokens, token_sems, weight, sems) = refs[len(sources) :]

    sequence = pl.program_id(0)

    @pl.when(sequence == 0)
    def _():
        start_rows(core_ref[0], rows, tokens, token_sems)
        load_weight(offsets_ref, sources, refs, weight, sems)

    wait_rows(core_ref[0], rows, tokens, token_sems, sequence)

    count = rows[0].shape[0]
    width = mixed_grad.shape[1]
    mine = pl.multiple_of(core_ref[0] * count, count)
    theirs = pl.multiple_of((1 - core_ref[0]) * count, count)
    seg_col = col_ref[0]
    before = jnp.concatenate([seg_col[:1] - 1, seg_col[:-1]], axis=0)
    carry = (seg_col == before).astype(jnp.float32)
    mixed_grad[...] = dot(tokens[sequence], weight[:, 3 * width :])
    seen = masks(col_ref[0], row_ref[0])
    for h in range(width // HEAD):
        p0, p1, p2 = [p_ref[0, :, pl.ds(j * width + h * HEAD, HEAD)] for j in range(3)]
        lanes = slice(h * HEAD, (h + 1) * HEAD)
        g0, g1, g2, floor_sum, gain_sum = head_backward(
            p0, p1, p2, mixed_grad[:, lanes], seen, carry, floor_ref[:, lanes],
            gain_ref[...], scores.at[h], key_grad.at[h], decay_grad.at[h], query_grad.at[h],
            *[ref.at[h] for ref in kept],
        )
        for j, g in enumerate((g0, g1, g2)):
            parts[:, pl.ds(j * width + h * HEAD, HEAD)] = g
        floor_sum_ref[0, :, lanes] = jnp.broadcast_to(floor_sum, (8, HEAD)) * 0.125
        gain_sum_ref[0, :, lanes] = jnp.broadcast_to(gain_sum, (8, HEAD)) * 0.125

    for j, g_ref in enumerate((g0_ref, g1_ref, g2_ref)):
        g_ref[0] = parts[:, j * width : (j + 1) * width]
    back[...] = dot(parts[...], weight[:, : 3 * width], NT)
    store_sends(back[pl.ds(theirs, count), :], send_ref, last_ref)
    keep_ref[0] = back[pl.ds(mine, count), :]


def mixer_specs(count, model, width, length):
    def at(shape, index):
        return pl.BlockSpec(shape, lambda s, c, o: index(s))

    side = [
        at((1, count, model), lambda s: (jnp.minimum(s, 2), 0, 0)),
        at((count, model), lambda s: (0, 0)),
        at((1, count, model), lambda s: (s, 0, 0)),
    ]
    col = at((1, length, 1), lambda s: (s, 0, 0))
    row = at((1, 1, length), lambda s: (s, 0, 0))
    floor = at((1, width), lambda s: (0, 0))
    gain = at((1, HEAD), lambda s: (0, 0))
    wide = at((1, length, 3 * width), lambda s: (s, 0, 0))
    pair = at((1, length, width), lambda s: (s, 0, 0))
    return at, side, wide, pair, [col, row, floor, gain]


def weight_scratch(model, lanes, sources):
    return [pltpu.VMEM((model, lanes), BF), pltpu.SemaphoreType.DMA((4 * len(sources),))]


def layout_of(sources):
    return tuple((piece, low) for piece, low, _ in sources), [part for _, _, part in sources]


def mixer_forward(core, offsets, tokens, sources, segments, floor, gain):
    groups, length, _ = segments[0].shape
    count, model = tokens[0].shape
    width = floor.shape[0]
    at, side, wide, pair, small = mixer_specs(count, model, width, length)
    layout, parts = layout_of(sources)
    shape = jax.ShapeDtypeStruct
    return pl.pallas_call(
        functools.partial(mixer_forward_kernel, sources=layout),
        grid_spec=pltpu.PrefetchScalarGridSpec(
            num_scalar_prefetch=2,
            grid=(groups,),
            in_specs=[pl.BlockSpec(memory_space=pl.ANY)] * (6 + len(parts)) + small,
            out_specs=[wide, pair] + side,
            scratch_shapes=[
                pltpu.VMEM((width // HEAD, length, length), BF),
                pltpu.VMEM((length, width), BF),
                pltpu.VMEM((length, model), jnp.float32),
            ]
            + row_scratch(count, model)
            + weight_scratch(model, 4 * width, parts),
        ),
        out_shape=[
            shape((groups, length, 3 * width), jnp.float32),
            shape((groups, length, width), BF),
            shape((groups - 1, count, model), BF),
            shape((count, model), BF),
            shape((groups, count, model), jnp.float32),
        ],
        compiler_params=PARAMS,
        cost_estimate=LONG,
        name="mixer_forward",
    )(
        core, offsets, *tokens, *parts, segments[0],
        segments[1], floor[None], gain[None],
    )


def mixer_backward(core, offsets, tokens, sources, projected, segments, floor, gain):
    groups, length, _ = segments[0].shape
    count, model = tokens[0].shape
    width = floor.shape[0]
    at, side, wide, pair, small = mixer_specs(count, model, width, length)
    layout, parts = layout_of(sources)
    heads = width // HEAD
    sums = at((1, 8, width), lambda s: (s, 0, 0))
    shape = jax.ShapeDtypeStruct
    return pl.pallas_call(
        functools.partial(mixer_backward_kernel, sources=layout),
        grid_spec=pltpu.PrefetchScalarGridSpec(
            num_scalar_prefetch=2,
            grid=(groups,),
            in_specs=[pl.BlockSpec(memory_space=pl.ANY)] * (6 + len(parts))
            + [wide]
            + small,
            out_specs=[pair] * 3 + side + [sums, sums],
            scratch_shapes=[pltpu.VMEM((heads, length, length), BF)]
            + [pltpu.VMEM((heads, length, HEAD), jnp.float32)] * 3
            + [pltpu.VMEM((heads, length, HEAD), kind) for kind in (BF, jnp.float32)]
            + [
                pltpu.VMEM((heads, length // STRIP, length, HEAD), kind)
                for kind in (BF, jnp.float32)
            ]
            + [pltpu.VMEM((length, width), jnp.float32), pltpu.VMEM((length, 3 * width), BF)]
            + [pltpu.VMEM((length, model), jnp.float32)]
            + row_scratch(count, model)
            + weight_scratch(model, 4 * width, parts),
        ),
        out_shape=[
            shape((groups, length, width), BF),
            shape((groups, length, width), BF),
            shape((groups, length, width), BF),
            shape((groups - 1, count, model), BF),
            shape((count, model), BF),
            shape((groups, count, model), jnp.float32),
        ]
        + [shape((groups, 8, width), jnp.float32)] * 2,
        compiler_params=PARAMS,
        cost_estimate=LONG,
        name="mixer_backward",
    )(
        core, offsets, *tokens, *parts, projected, segments[0],
        segments[1], floor[None], gain[None],
    )


def ffn_kernel(core_ref, offsets_ref, *refs, sources, units):
    rows, tops, refs = refs[:6], refs[6:12], refs[12:]
    (*parts, send_ref, last_ref, keep_ref, grads, back,
     tokens, token_sems, top_tokens, top_sems, weight, sems) = refs[len(sources) :]

    sequence = pl.program_id(0)

    @pl.when(sequence == 0)
    def _():
        start_rows(core_ref[0], rows, tokens, token_sems)
        start_rows(core_ref[0], tops, top_tokens, top_sems)
        load_weight(offsets_ref, sources, refs, weight, sems)

    wait_rows(core_ref[0], rows, tokens, token_sems, sequence)
    wait_rows(core_ref[0], tops, top_tokens, top_sems, sequence)

    width = units
    count = rows[0].shape[0]
    mine = pl.multiple_of(core_ref[0] * count, count)
    theirs = pl.multiple_of((1 - core_ref[0]) * count, count)
    both = dot(tokens[sequence], weight[:, : 2 * width])
    gate, up = both[:, :width], both[:, width:]
    active_grad = dot(top_tokens[sequence], weight[:, 2 * width : 3 * width])
    squash = jax.nn.sigmoid(gate)
    swish = gate * squash
    gate_grad = active_grad * up * squash * (1.0 + gate * (1.0 - squash))
    grads[:, : 2 * width] = jnp.concatenate([gate_grad, active_grad * swish], axis=1).astype(BF)
    spare = jnp.zeros((2 * count, grads.shape[1] - 3 * width), BF)
    grads[:, 2 * width :] = jnp.concatenate([(swish * up).astype(BF), spare], axis=1)
    low = 0
    for part_ref in parts:
        part_ref[0] = grads[:, low : low + part_ref.shape[2]]
        low += part_ref.shape[2]
    back[...] = dot(grads[:, : 2 * width], weight[:, : 2 * width], NT)
    store_sends(back[pl.ds(theirs, count), :], send_ref, last_ref)
    keep_ref[0] = back[pl.ds(mine, count), :]


def ffn(core, offsets, tokens, tops, sources, width, widths):
    count, model = tokens[0].shape
    groups, length = 4, 2 * count
    total = sum(widths)
    layout, parts = layout_of(sources)

    def at(rows, lanes):
        return pl.BlockSpec((1, rows, lanes), lambda s, c, o: (s, 0, 0))

    shape = jax.ShapeDtypeStruct
    return pl.pallas_call(
        functools.partial(ffn_kernel, sources=layout, units=width),
        grid_spec=pltpu.PrefetchScalarGridSpec(
            num_scalar_prefetch=2,
            grid=(groups,),
            in_specs=[pl.BlockSpec(memory_space=pl.ANY)] * (12 + len(parts)),
            out_specs=[at(length, n) for n in widths]
            + [
                pl.BlockSpec((1, count, model), lambda s, c, o: (jnp.minimum(s, 2), 0, 0)),
                pl.BlockSpec((count, model), lambda s, c, o: (0, 0)),
                at(count, model),
            ],
            scratch_shapes=[
                pltpu.VMEM((length, total), BF),
                pltpu.VMEM((length, model), jnp.float32),
            ]
            + row_scratch(count, model) * 2
            + weight_scratch(model, total, parts),
        ),
        out_shape=[
            *[shape((groups, length, n), BF) for n in widths],
            shape((groups - 1, count, model), BF),
            shape((count, model), BF),
            shape((groups, count, model), jnp.float32),
        ],
        compiler_params=PARAMS,
        cost_estimate=LONG,
        name="ffn",
    )(core, offsets, *tokens, *tops, *parts)


def rows_kernel(core_ref, offsets_ref, *refs, sources, begin, number):
    own, refs = refs[:number], refs[number:]
    out_ref, whole, sems = refs[len(sources) :]

    @pl.when(pl.program_id(0) == 0)
    def _():
        load_weight(offsets_ref, sources, refs, whole, sems, begin)

    out_ref[0] = dot(jnp.concatenate([r[0] for r in own], axis=1), whole[...], NT).astype(BF)


def rows_product(core, offsets, own, sources, begin, model, estimate=SHORT):
    groups, length, _ = own[0].shape
    width = sum(o.shape[2] for o in own)
    layout, parts = layout_of(sources)

    def at(rows, lanes):
        return pl.BlockSpec((1, rows, lanes), lambda s, c, o: (s, 0, 0))

    shape = jax.ShapeDtypeStruct
    return pl.pallas_call(
        functools.partial(rows_kernel, sources=layout, begin=begin, number=len(own)),
        grid_spec=pltpu.PrefetchScalarGridSpec(
            num_scalar_prefetch=2,
            grid=(groups,),
            in_specs=[at(length, o.shape[2]) for o in own] + [pl.BlockSpec(memory_space=pl.ANY)] * len(parts),
            out_specs=pl.BlockSpec((1, length, model), lambda s, c, o: (s ^ c[1], 0, 0)),
            scratch_shapes=weight_scratch(model, width, parts),
        ),
        out_shape=shape((groups, length, model), BF),
        compiler_params=PARAMS,
        cost_estimate=estimate,
        name="rows_product",
    )(core, offsets, *own, *parts)


def grad_kernel(core_ref, blocks_ref, *refs, number):
    rows, grads, outs, tokens = refs[:6], refs[6 : 6 + number], refs[6 + number : -1], refs[-1]
    count = rows[0].shape[0]
    for side in range(2):
        at = core_ref[0] if side == 0 else 1 - core_ref[0]
        for m in range(4):
            first = pl.multiple_of((2 * m + at) * count, count)
            part = rows[m][...] if side == 0 else rows[4][m] if m < 3 else rows[5][...]
            tokens[pl.ds(first, count), :] = part
    for grad_ref, out_ref in zip(grads, outs):
        out_ref[0] = dot(tokens[...], grad_ref[...], TN).astype(out_ref.dtype)


def grad_product(core, tokens, grads, blocks, wide, kind, estimate):
    count, model = tokens[0].shape
    side = pl.BlockSpec((count, wide), lambda i, c, b: (0, b[i]))
    three = pl.BlockSpec((3, count, wide), lambda i, c, b: (0, 0, b[i]))
    number = blocks.shape[0]
    return pl.pallas_call(
        functools.partial(grad_kernel, number=len(grads)),
        grid_spec=pltpu.PrefetchScalarGridSpec(
            num_scalar_prefetch=2,
            grid=(number,),
            in_specs=[side] * 4
            + [three, side]
            + [pl.BlockSpec(g.shape, lambda i, c, b: (0, 0)) for g in grads],
            out_specs=[pl.BlockSpec((1, wide, g.shape[1]), lambda i, c, b: (i, 0, 0)) for g in grads],
            scratch_shapes=[pltpu.VMEM((8 * count, wide), BF)],
        ),
        out_shape=[jax.ShapeDtypeStruct((number, wide, g.shape[1]), kind) for g in grads],
        compiler_params=PARAMS,
        cost_estimate=estimate,
        name="grad_product",
    )(core, blocks, *tokens, *grads)


def rms_of(values):
    return lax.rsqrt(jnp.mean(values * values, axis=-1, keepdims=True) + epsilon)


def last_kernel(keep_ref, came_ref, out_ref):
    out_ref[...] = (keep_ref[0] + came_ref[...].astype(jnp.float32)).astype(BF)


def add_last(keep, came):
    count, model = came.shape
    block = count // 2
    return pl.pallas_call(
        last_kernel,
        grid=(2,),
        in_specs=[
            pl.BlockSpec((1, block, model), lambda i: (3, i, 0)),
            pl.BlockSpec((block, model), lambda i: (i, 0)),
        ],
        out_specs=pl.BlockSpec((block, model), lambda i: (i, 0)),
        out_shape=jax.ShapeDtypeStruct(came.shape, BF),
        compiler_params=PARAMS,
        cost_estimate=SHORT,
        name="add_last",
    )(keep, came)


def cores_kernel(keep_ref, came_ref, own_ref, x_ref, z_ref):
    own_ref[...] = keep_ref[0] + came_ref[0].astype(jnp.float32)
    for m, out_ref in enumerate((x_ref, z_ref), 1):
        out_ref[...] = (keep_ref[m] + came_ref[m].astype(jnp.float32)).astype(BF)


def add_cores(keep, came):
    count, model = keep.shape[1:]
    block = count // 2
    three = pl.BlockSpec((3, block, model), lambda i: (0, i, 0))
    one = pl.BlockSpec((block, model), lambda i: (i, 0))
    shape = jax.ShapeDtypeStruct
    return pl.pallas_call(
        cores_kernel,
        grid=(2,),
        in_specs=[three, three],
        out_specs=[one] * 3,
        out_shape=[shape((count, model), jnp.float32)] + [shape((count, model), BF)] * 2,
        compiler_params=PARAMS,
        cost_estimate=SHORT,
        name="add_cores",
    )(keep, came)


def middle_kernel(own_ref, x_ref, z_ref, hidden_ref, gain_ref, middle_ref, normed_ref):
    branch = own_ref[...] + x_ref[...].astype(jnp.float32) + z_ref[...].astype(jnp.float32)
    middle = hidden_ref[...].astype(jnp.float32) + branch
    middle_ref[...] = middle
    normed_ref[...] = (middle * rms_of(middle) * gain_ref[...]).astype(BF)


def back_kernel(own_ref, x_ref, z_ref, values_ref, add_ref, gain_ref, out_ref, low_ref, sum_ref):
    grad = own_ref[...] + x_ref[...].astype(jnp.float32) + z_ref[...].astype(jnp.float32)
    values = values_ref[...].astype(jnp.float32)
    scale = rms_of(values)
    unit = values * scale
    wide = grad * gain_ref[...]
    inner = wide - unit * jnp.mean(wide * unit, axis=-1, keepdims=True)
    out = add_ref[...].astype(jnp.float32) + scale * inner
    out_ref[...] = out
    low_ref[...] = out.astype(BF)

    @pl.when(pl.program_id(0) == 0)
    def _():
        sum_ref[...] = jnp.zeros_like(sum_ref)

    sum_ref[...] += jnp.sum(grad * unit, axis=0, keepdims=True)


def row_call(kernel, name, kinds, *args):
    count, model = args[0].shape
    block = count // 4

    def spec(one):
        if one:
            return pl.BlockSpec((1, model), lambda i: (0, 0))
        return pl.BlockSpec((block, model), lambda i: (i, 0))

    shapes = [jax.ShapeDtypeStruct((1 if k is None else count, model), k or jnp.float32) for k in kinds]
    return pl.pallas_call(
        kernel,
        grid=(4,),
        in_specs=[spec(a.shape[0] == 1) for a in args],
        out_specs=[spec(k is None) for k in kinds],
        out_shape=shapes,
        compiler_params=PARAMS,
        cost_estimate=LONG,
        name=name,
    )(*args)


def mix_grad_kernel(parts_ref, out_ref):
    quarter = parts_ref.shape[2] // 4
    for j, at in enumerate((1, 3, 0, 2)):
        for m in range(4):
            part = parts_ref[m, :, at * quarter : (at + 1) * quarter]
            out_ref[:, j, m * quarter : (m + 1) * quarter] = part.astype(jnp.float32)


def mix_grad_of(parts):
    _, rows, wide = parts.shape
    block = min(rows, 64)
    return pl.pallas_call(
        mix_grad_kernel,
        grid=(rows // block,),
        in_specs=[pl.BlockSpec((4, block, wide), lambda i: (0, i, 0))],
        out_specs=pl.BlockSpec((block, 4, wide), lambda i: (i, 0, 0)),
        out_shape=jax.ShapeDtypeStruct((rows, 4, wide), jnp.float32),
        compiler_params=PARAMS,
        cost_estimate=SHORT,
        name="mix_grad",
    )(parts)


DOWN_FIRST = 384


def ffn_grad_kernel(first_ref, second_ref, out_ref):
    units = out_ref.shape[2] // 4
    for j in range(3):
        parts = []
        for m in range(4):
            down = first_ref.shape[2] - DOWN_FIRST
            gates = jnp.concatenate([first_ref[m, :, down:], second_ref[m]], axis=1)
            parts.append(first_ref[m, :, :units] if j == 2 else gates[:, j * units : (j + 1) * units])
        out_ref[j] = jnp.concatenate(parts, axis=1).astype(jnp.float32)


def ffn_grad_of(parts, units):
    rows = parts[0].shape[1]
    block = min(rows, 32)
    out = pl.pallas_call(
        ffn_grad_kernel,
        grid=(rows // block,),
        in_specs=[pl.BlockSpec((4, block, p.shape[2]), lambda i: (0, i, 0)) for p in parts],
        out_specs=pl.BlockSpec((3, block, 4 * units), lambda i: (0, i, 0)),
        out_shape=jax.ShapeDtypeStruct((3, rows, 4 * units), jnp.float32),
        compiler_params=PARAMS,
        cost_estimate=LONG,
        name="ffn_grad",
    )(*parts)
    return out.transpose(1, 0, 2)


def near_kernel(*refs, number, ends):
    home_ref, away_ref = refs[2 * number :]
    block = pl.program_id(0)
    last = pl.num_programs(0) // ends
    for k in range(number):
        keep_ref, came_ref = refs[2 * k], refs[2 * k + 1]
        low = sum(refs[2 * j].shape[2] for j in range(k))
        total = keep_ref[0] + came_ref[0].astype(jnp.float32)
        lanes = slice(low, low + keep_ref.shape[2])

        @pl.when(block < pl.num_programs(0) - last)
        def _():
            away_ref[0, :, lanes] = total.astype(BF)

        @pl.when(block >= pl.num_programs(0) - last)
        def _():
            home_ref[0, :, lanes] = total


def near_sums(pairs, estimate=SHORT):
    highs = lax.axis_size("h")
    blocks, rows, _ = pairs[0][0].shape
    away_count = blocks - 2
    wide = sum(keep.shape[2] for keep, _ in pairs)
    specs, args = [], []
    for pair in pairs:
        specs += [pl.BlockSpec((1,) + pair[0].shape[1:], lambda i: (i, 0, 0))] * 2
        args += list(pair)
    home, away = pl.pallas_call(
        functools.partial(near_kernel, number=len(pairs), ends=highs),
        grid=(blocks,),
        in_specs=specs,
        out_specs=[
            pl.BlockSpec((1, rows, wide), lambda i: (jnp.maximum(i - away_count, 0), 0, 0)),
            pl.BlockSpec((1, rows, wide), lambda i: (jnp.minimum(i, away_count - 1), 0, 0)),
        ],
        out_shape=[
            jax.ShapeDtypeStruct((2, rows, wide), jnp.float32),
            jax.ShapeDtypeStruct((away_count, rows, wide), BF),
        ],
        compiler_params=PARAMS,
        cost_estimate=estimate,
        name="near_sums",
    )(*args)
    return home, [away[2 * k : 2 * k + 2] for k in range(highs - 1)]


def far_kernel(*refs, counts):
    out_ref = refs[-1]
    low, at = 0, 0
    for count in counts:
        total = refs[at][0]
        for ref in refs[at + 1 : at + 1 + count]:
            total = total + ref[0].astype(jnp.float32)
        out_ref[0, :, low : low + total.shape[1]] = total.astype(BF)
        low, at = low + total.shape[1], at + 1 + count


def far_sums(pairs, estimate=SHORT):
    _, rows, _ = pairs[0][0].shape
    wide = sum(home.shape[2] for home, _ in pairs)
    args = [part for home, fars in pairs for part in (home, *fars)]
    out = pl.pallas_call(
        functools.partial(far_kernel, counts=[len(fars) for _, fars in pairs]),
        grid=(2,),
        in_specs=[pl.BlockSpec((1,) + a.shape[1:], lambda i: (i, 0, 0)) for a in args],
        out_specs=pl.BlockSpec((1, rows, wide), lambda i: (i, 0, 0)),
        out_shape=jax.ShapeDtypeStruct((2, rows, wide), BF),
        compiler_params=PARAMS,
        cost_estimate=estimate,
        name="far_sums",
    )(*args)
    return out.reshape(4, rows // 2, wide)


GROUP = ("l", "x")


def swap(values, axes):
    total = 2 ** len(axes)
    return lax.ppermute(values, axes, [(s, total - 1 - s) for s in range(total)])


def shift(values, steps):
    total = lax.axis_size("h")
    return lax.ppermute(values, "h", [(s, (s + steps) % total) for s in range(total)])


def pick(values, index):
    return lax.dynamic_index_in_dim(values, index, 0, keepdims=False)


def over_c(values):
    return swap(values, ("tensor",))


def over_x(values):
    return swap(values, ("x",))


def over_y(values):
    return swap(values, ("y",))


def over_z(values):
    return swap(values, ("l",))


def own_member():
    return lax.axis_index("l") * 2 + lax.axis_index("x")


def source_rows(rows):
    y, high = lax.axis_index("y"), lax.axis_index("h")
    highs = lax.axis_size("h")
    starts = []
    for k in range(highs):
        for side in (y, 1 - y):
            for member in range(4):
                block = ((high - k) % highs) * 8 + (member >> 1) * 4 + side * 2 + (member & 1)
                starts.append(block * rows)
    return jnp.stack(starts).astype(jnp.int32)


def trade(slices):
    return lax.all_to_all(slices, GROUP, 0, 0, tiled=True)


def after(values, *others):
    return lax.optimization_barrier((values, others))[0]


def far(block):
    return [shift(block, k) for k in range(1, lax.axis_size("h"))]


def near(parts):
    return [over_y(part) for part in parts]


def pieces(low, straight, crossed):
    out = []
    for k, (one, two) in enumerate(zip(straight, crossed), 1):
        out += [(2 * k, low, one), (2 * k + 1, low, two)]
    return out


def half_grads(core, tokens, grads, yy, kind, estimate):
    highs, high = lax.axis_size("h"), lax.axis_index("h")
    wide = tokens[0].shape[1] // (4 * highs)
    order = [(high + k) % highs for k in range(1, highs)] + [high]
    blocks = jnp.stack([(h * 2 + z) * 2 + yy for h in order for z in range(2)]).astype(jnp.int32)
    grads = [flat(g) for g in grads]
    if wide % 128 == 0:
        return grad_product(core, tokens, grads, blocks, wide, kind, estimate)
    sides = [jnp.stack(tokens[:4]), jnp.concatenate([tokens[4], tokens[5][None]])]
    ordered = [jnp.where(core[0] == 0, a, b) for a, b in (sides, sides[::-1])]
    whole = jnp.stack(ordered, axis=1)
    split = jnp.take(whole.reshape(grads[0].shape[0], -1, wide), blocks, axis=1)
    return [
        jnp.einsum("tad,tx->adx", split, g, preferred_element_type=jnp.float32).astype(kind)
        for g in grads
    ]


def grad_sends(core, tokens, grads, estimate=SHORT):
    return half_grads(core, tokens, grads, 1 - lax.axis_index("y"), BF, estimate)


def grad_keeps(core, tokens, grads, estimate=SHORT):
    return half_grads(core, tokens, grads, lax.axis_index("y"), jnp.float32, estimate)


def send_far(away):
    return [shift(part, k) for k, part in enumerate(away, 1)]


def flat(values):
    return values.reshape(-1, values.shape[-1])


def add_low(keep, came):
    return (keep.astype(jnp.float32) + came.astype(jnp.float32)).astype(BF)


def sum_pair(values, first, second):
    parts = [values, swap(values, (second,)), swap(values, (first,)), swap(values, (first, second))]
    return jnp.stack(parts), lax.axis_index(first) * 2 + lax.axis_index(second)


def add_pair(parts, place):
    return sum(pick(parts, place ^ m) for m in range(4))


def sum_highs(values):
    size, bits = lax.axis_size("h"), 1
    while bits < size:
        values = values + lax.ppermute(values, "h", [(s, s ^ bits) for s in range(size)])
        bits *= 2
    return values


def body(
    hidden_in,
    segments,
    mix_weights,
    ffn_weights,
    norm1_gain,
    norm2_gain,
    head_gain,
    lower_bound,
    out_grad,
):
    core, member = lax.axis_index("tensor"), own_member()
    core_at = jnp.stack([core, member]).astype(jnp.int32)
    rows = mix_weights.shape[0]
    offsets = source_rows(rows)
    quarter, units = lower_bound.shape[0] // 4, ffn_weights.shape[2] // 4
    model = hidden_in.shape[1]
    channels = 4 * quarter
    lanes = -(-3 * units // 128) * 128

    def slices(weights, width):
        split = weights.reshape(rows, weights.shape[1], 4, -1).transpose(2, 0, 1, 3)
        split = split.reshape(4, rows, -1)
        return jnp.pad(split, ((0, 0), (0, 0), (0, width - split.shape[2])))

    length = segments.shape[1]
    labels = jnp.pad(segments.astype(BF), ((0, 15), (0, channels - length)))
    labels = jnp.broadcast_to(labels, (4,) + labels.shape)
    hidden = hidden_in.astype(jnp.float32)
    scale_one = rms_of(hidden)
    normed = (hidden * scale_one * norm1_gain).astype(BF)
    floor = lax.dynamic_slice_in_dim(lower_bound, member * quarter, quarter)
    feed = slices(ffn_weights, lanes)
    mix = slices(mix_weights, channels)

    mix = trade(jnp.concatenate([slices(mix_weights, channels), labels], axis=1))

    gate = (mix, normed, feed)
    mix, normed, feed = lax.optimization_barrier(gate)
    labels = mix[:, rows, :length].astype(jnp.int32)
    labels = jnp.stack([pick(labels, member ^ m) for m in range(4)])
    mix = mix[:, :rows]
    cuts = [0, 512, 1024, 1152, 1408, 1664, 1920, lanes]
    feed_cut = cuts[4]
    mix_far = far(mix)
    mix_near = over_y(mix)
    feed_one = trade(feed[..., :feed_cut])
    feed_rest = after(feed[..., feed_cut:], gate)
    normed_x, normed_z = over_x(normed), over_z(normed)
    top_x = over_x(after(out_grad, gate))

    columns = jnp.broadcast_to(labels[:, :, None], labels.shape + (1,))
    gate = (mix_far, mix_near, feed_one, feed_rest, normed_x, normed_z, top_x, floor, columns)
    floor = after(floor, gate)
    labels = (after(columns, gate), labels[:, None, :])
    mix_cross = near(after(mix_far, gate))
    ones = [feed_one[..., low:high] for low, high in zip(cuts[:4], cuts[1:5])]
    far_a = far(after(ones[0], gate))
    normed_xz = over_x(after(normed_z, gate))
    normed_three = jnp.stack(after([normed, normed_x, normed_z], gate))
    top_z = over_z(after(out_grad, gate))
    near_a = over_y(after(feed_one[..., :256], gate))

    gate = (mix_cross, far_a, normed_xz, normed_three, top_z, ones, near_a)
    normed_c, normed_cxz = over_c(after(normed_three, gate)), over_c(after(normed_xz, gate))
    normed = [normed, normed_x, normed_z, normed_xz, normed_c, normed_cxz]
    mix_sources = [(0, 0, mix), (1, 0, mix_near)] + pieces(0, mix_far, mix_cross)

    gate = (normed_c, normed_cxz)
    far_b = far(after(ones[1], gate))
    near_b = over_y(after(feed_one[..., 256:768], gate))
    cross_a = near(after(far_a, gate))
    top_xz = over_x(after(top_z, gate))
    feed_two = trade(after(feed_rest, gate))
    projected, mixed, send, send_xz, keep = mixer_forward(
        core_at, offsets, after(normed, gate), mix_sources, labels, floor, head_gain
    )

    gate = (send, far_b, near_b, cross_a, top_xz, feed_two)
    came_xz = over_c(after(send_xz, gate))
    came = over_c(after(send, gate))
    near_c = over_y(after(feed_one[..., 768:1024], gate))
    far_c = far(after(ones[2], gate))
    to_xz = add_last(keep, came_xz)

    gate = (to_xz, near_c, far_c)
    from_x = over_x(after(to_xz, gate))
    far_d = far(after(ones[3], gate))
    cross_b = near(after(far_b, gate))
    own, to_x, to_z = add_cores(keep, after(came, gate))
    top_three = jnp.stack(after([out_grad, top_x, top_z], gate))

    gate = (from_x, far_d, cross_b, own, top_three)
    to_z = add_low(to_z, after(from_x, gate))
    of_x = over_x(after(to_x, gate))
    of_z = over_z(to_z)
    far_e = far(after(feed_two[..., : cuts[5] - feed_cut], gate))
    near_d = over_y(after(feed_one[..., 1024:], gate))
    near_e = over_y(after(feed_two[..., :384], gate))

    gate = (of_x, of_z, far_e, near_d, near_e)
    far_f = far(after(feed_two[..., cuts[5] - feed_cut : cuts[6] - feed_cut], gate))
    near_f = over_y(after(feed_two[..., 384:], gate))
    cross_cd = [
        over_y(jnp.concatenate([one, two], axis=-1))
        for one, two in zip(after(far_c, gate), after(far_d, gate))
    ]
    middle, normed_two = row_call(
        middle_kernel, "middle", [jnp.float32, BF], *after((own, of_x, of_z), gate), hidden_in,
        norm2_gain[None],
    )
    two_x, two_z = over_x(normed_two), over_z(normed_two)

    gate = (far_f, near_f, cross_cd, two_x, two_z)
    far_g = far(after(feed_two[..., cuts[6] - feed_cut :], gate))
    cross_e, cross_f = near(after(far_e, gate)), near(after(far_f, gate))
    two_xz = over_x(after(two_z, gate))
    two_three = jnp.stack(after([normed_two, two_x, two_z], gate))

    gate = (far_g, cross_e, cross_f, two_xz, two_three)
    cross_g = near(after(far_g, gate))
    two_c, two_cxz = over_c(after(two_three, gate)), over_c(after(two_xz, gate))
    top_c, top_cxz = over_c(after(top_three, gate)), over_c(after(top_xz, gate))
    tops = [out_grad, top_x, top_z, top_xz, top_c, top_cxz]
    normed_two = [normed_two, two_x, two_z, two_xz, two_c, two_cxz]
    feed_sources = [(0, 0, feed_one), (0, feed_cut, feed_two)]
    feed_sources += [(1, 0, near_a), (1, 256, near_b), (1, 768, near_c), (1, 1024, near_d)]
    feed_sources += [(1, feed_cut, near_e), (1, feed_cut + 384, near_f)]
    fars = [far_a, far_b, far_c, far_d, far_e, far_f, far_g]
    for low, part in zip(cuts, fars):
        feed_sources += [(2 * k, low, one) for k, one in enumerate(part, 1)]
    crosses = [cross_a, cross_b, cross_cd, cross_e, cross_f, cross_g]
    for low, part in zip(cuts[:3] + cuts[4:], crosses):
        feed_sources += [(2 * k + 1, low, one) for k, one in enumerate(part, 1)]

    widths = [128, 256, 384, 256, 256, 128, 256, 256, lanes - 1920]
    *grads, send, send_xz, keep = ffn(core_at, offsets, normed_two, tops, feed_sources, units, widths)
    gates, downs = grads[:6], grads[6:]
    came_xz, came = over_c(send_xz), over_c(send)
    down_sends = grad_sends(core_at, after(tops, send), downs, LONG)
    to_xz = add_last(keep, after(came_xz, down_sends))

    gate = (to_xz,)
    from_x = over_x(after(to_xz, gate))
    down_one = over_y(after(down_sends[0], gate))
    gate_sends = grad_sends(core_at, after(normed_two, gate), gates, LONG)
    own, to_x, to_z = add_cores(keep, after(came, gate_sends))

    gate = (from_x, down_one, own)
    to_z = add_low(to_z, after(from_x, gate))
    of_x = over_x(after(to_x, gate))
    of_z = over_z(to_z)
    down_two = over_y(after(down_sends[1], gate))
    down_keeps = grad_keeps(core_at, after(tops, gate), downs, LONG)
    down_home, down_away = near_sums([(down_keeps[0], after(down_one, gate))])

    gate = (of_x, of_z, down_two, down_away)
    down_fars = send_far(after(down_away, gate))
    down_three = over_y(after(down_sends[2], gate))
    one_came = over_y(after(gate_sends[0], gate))
    middle_grad, middle_low, gain_two_grad = row_call(
        back_kernel, "middle_grad", [jnp.float32, BF, None], *after((own, of_x, of_z), gate),
        middle, out_grad, norm2_gain[None],
    )
    grad_x, grad_z = over_x(middle_low), over_z(middle_low)
    gate_keeps = grad_keeps(core_at, after(normed_two, middle_low), gates, LONG)
    down_home_two, down_away_two = near_sums(
        [(after(down_keeps[1], gate_keeps), after(down_two, gate))]
    )

    gate = (grad_x, grad_z, down_three, one_came, down_away_two, down_fars)
    down_fars_two = send_far(after(down_away_two, gate))
    two_came = over_y(after(gate_sends[1], gate))
    grad_xz = over_x(after(grad_z, gate))
    grad_three = jnp.stack(after([middle_low, grad_x, grad_z], gate))
    branch = rows_product(
        core_at, offsets, after(downs, gate), feed_sources, 2 * units, model, LONG
    )

    gate = (grad_xz, grad_three, branch, down_fars_two, two_came)
    grad_c, grad_cxz = over_c(after(grad_three, gate)), over_c(after(grad_xz, gate))
    one_home, one_away = near_sums(
        [
            (down_keeps[2], after(down_three, gate)),
            (gate_keeps[0], after(one_came, gate)),
            (gate_keeps[1], after(two_came, gate)),
        ],
        LONG,
    )
    middle_full = [middle_low, grad_x, grad_z, grad_xz, grad_c, grad_cxz]

    gate = (grad_c, grad_cxz, one_away)
    one_fars = send_far(after(one_away, gate))
    three_came, four_came = [over_y(after(part, gate)) for part in gate_sends[2:4]]
    branch = lax.psum_scatter(
        after(branch, gate).reshape(-1, model), GROUP + ("tensor",), scatter_dimension=0, tiled=True
    )
    middle_full = after(middle_full, gate)
    *mix_grads, send, send_xz, keep, floor_sums, gain_sums = mixer_backward(
        core_at, offsets, middle_full, mix_sources, projected, labels, floor, head_gain
    )

    gate = (send, one_fars, three_came, four_came)
    came_xz, came = over_c(after(send_xz, gate)), over_c(after(send, gate))
    five_came = over_y(after(gate_sends[4], gate))
    three_home, three_away = near_sums([(gate_keeps[2], after(three_came, gate))], LONG)
    to_xz = add_last(keep, after(came_xz, three_away))

    gate = (to_xz,)
    three_fars = send_far(after(three_away, gate))
    from_x = over_x(after(to_xz, gate))
    six_came = over_y(after(gate_sends[5], gate))
    query_send, forget_send, value_send = grad_sends(core_at, after(normed, gate), mix_grads, LONG)
    own, to_x, to_z = add_cores(keep, after(came, value_send))
    four_home, four_away = near_sums(
        [
            (gate_keeps[3], after(four_came, own)),
            (gate_keeps[4], five_came),
            (gate_keeps[5], six_came),
        ]
    )

    gate = (from_x, three_fars, four_away)
    four_fars = send_far(after(four_away, gate))
    to_z = add_low(to_z, after(from_x, gate))
    of_x = over_x(after(to_x, gate))
    of_z = over_z(to_z)
    value_came, query_came = over_y(after(value_send, gate)), over_y(after(query_send, gate))
    query_keep, forget_keep, value_keep = grad_keeps(core_at, after(normed, gate), mix_grads, LONG)
    (last_send,) = grad_sends(core_at, after(middle_full, value_keep), [mixed])
    down_parts = [(down_home, down_fars), (down_home_two, down_fars_two), (one_home, one_fars)]
    down_parts = far_sums(after(down_parts, last_send))
    near_home, near_away = near_sums(
        [(value_keep, after(value_came, down_parts)), (query_keep, query_came)]
    )

    gate = (of_x, of_z, four_fars, near_away)
    near_fars = send_far(after(near_away, gate))
    last_came, forget_came = over_y(after(last_send, gate)), over_y(after(forget_send, gate))
    down_parts = trade(after(down_parts, gate))
    input_grad, _, gain_one_grad = row_call(
        back_kernel, "input_grad", [jnp.float32, BF, None], *after((own, of_x, of_z), gate),
        hidden_in, middle_grad, norm1_gain[None],
    )
    (last_keep,) = grad_keeps(core_at, after(middle_full, input_grad), [mixed])
    head_grad = jnp.sum(after(gain_sums, gate).reshape(-1, HEAD), axis=0)
    lower_grad = jnp.zeros((2, 4, quarter), jnp.float32)
    lower_grad = lax.dynamic_update_slice(
        lower_grad,
        jnp.sum(after(floor_sums, gate), axis=(0, 1)).reshape(1, 1, quarter),
        (core, member, 0),
    )
    sums = [gain_one_grad[0], gain_two_grad[0], head_grad, lower_grad.reshape(-1)]
    sums = jnp.concatenate(sums).reshape(-1, HEAD)
    block_out = (middle + after(branch, last_keep).astype(jnp.float32)).astype(BF)
    gate_parts = [(three_home, three_fars), (four_home, four_fars)]
    gate_parts = far_sums(after(gate_parts, block_out))
    pair_home, pair_away = near_sums(
        [(last_keep, after(last_came, gate_parts)), (forget_keep, forget_came)]
    )

    gate = (near_fars, down_parts, sums, pair_away, gate_parts, block_out)
    pair_fars = send_far(after(pair_away, gate))
    gate_parts = trade(after(gate_parts, gate))
    sums, place = sum_pair(after(sums, gate), "l", "x")

    gate = (pair_fars, gate_parts, sums)
    mix_parts = far_sums(after([(near_home, near_fars), (pair_home, pair_fars)], gate))
    sums, place = sum_pair(add_pair(after(sums, mix_parts), place), "y", "tensor")
    sums = sum_highs(add_pair(sums, place)).reshape(-1)
    mix_parts = trade(mix_parts)
    gain_one, gain_two, head, lower = jnp.split(sums, [model, 2 * model, 2 * model + HEAD])
    ffn_grad = ffn_grad_of(after([down_parts, gate_parts], gate), units)
    mix_grad = mix_grad_of(mix_parts)
    return (block_out, input_grad, mix_grad, ffn_grad, gain_one, gain_two, head, lower)


def solution(mesh):
    total, cores = mesh.shape["dp"], mesh.shape["tensor"]
    fine = Mesh(mesh.devices.reshape(total // 8, 2, 2, 2, cores), ("h", "l", "y", "x", "tensor"))
    dp = ("h", "l", "y", "x")
    rows = P(dp + ("tensor",), None)
    weights = P(dp, None, "tensor")
    return jax.shard_map(
        body,
        mesh=fine,
        in_specs=(rows, P(dp, None), weights, weights, P(), P(), P(), P("tensor"), rows),
        out_specs=(rows, rows, weights, weights, P(), P(), P(), P()),
        check_vma=False,
    )
```

```python
import functools

import jax
import jax.numpy as jnp
from jax import lax
from jax.experimental import pallas as pl
from jax.experimental.pallas import tpu as pltpu
from jax.sharding import Mesh, PartitionSpec as P

HEAD = 128
STRIP = 32
CAP = 50.0
BF = jnp.bfloat16
epsilon = 1e-06
PARAMS = pltpu.CompilerParams(vmem_limit_bytes=56 * 1024 * 1024)


LONG, SHORT = [pl.CostEstimate(flops=f, bytes_accessed=1, transcendentals=0) for f in (5 * 10**10, 1)]


NN, NT, TN = ((1,), (0,)), ((1,), (1,)), ((0,), (0,))


def dot(a, b, dims=NN):
    return lax.dot_general(a, b, (dims, ((), ())), preferred_element_type=jnp.float32)


def exact_dot(ones, values):
    high = values.astype(BF)
    rest = values - high.astype(jnp.float32)
    mid = rest.astype(BF)
    tail = (rest - mid.astype(jnp.float32)).astype(BF)
    return dot(ones, high) + dot(ones, mid) + dot(ones, tail)


def gates(p0, p1, floor):
    swish = jax.nn.sigmoid(p0)
    gate = jax.nn.sigmoid(p1)
    return swish, gate, floor + (1.0 - floor) * gate


def masks(seg_col, seg_row):
    length = seg_col.shape[0]
    row = lax.broadcasted_iota(jnp.int32, (length, length), 0)
    col = lax.broadcasted_iota(jnp.int32, (length, length), 1)
    same = seg_col == seg_row
    return same & (col <= row), (col <= row).astype(BF), (same & (col >= row)).astype(BF)


def strips(length):
    return [(s, -(-(s + STRIP) // 128) * 128) for s in range(0, length, STRIP)]


def fill_scores(query, key, totals, allowed, scores, kept=None):
    length = query.shape[0]
    for k, (start, wide) in enumerate(strips(length)):
        rows = slice(start, start + STRIP)
        ref = totals[start + STRIP // 2 - 1 : start + STRIP // 2]
        lead_scale = jnp.exp(totals[rows] - ref)
        trail_scale = jnp.exp(jnp.minimum(ref - totals[:wide], CAP))
        lead = (query[rows] * lead_scale).astype(BF)
        trail = (key[:wide] * trail_scale).astype(BF)
        if kept is not None:
            leads, lead_scales, trails, trail_scales = kept
            leads[rows, :], lead_scales[rows, :] = lead, lead_scale
            trails[k, :wide, :], trail_scales[k, :wide, :] = trail, trail_scale
        part = jnp.where(allowed[rows, :wide], dot(lead, trail, NT), 0.0)
        scores[rows, :wide] = part.astype(BF)
        if wide < length:
            scores[rows, wide:] = jnp.zeros((STRIP, length - wide), BF)


def head_forward(p0, p1, p2, seen, floor, gain, scores):
    swish, gate, forget = gates(p0, p1, floor)
    allowed, tri, _ = seen
    totals = exact_dot(tri, jnp.log(forget))
    fill_scores(p0 * swish, 1.0 - forget, totals, allowed, scores)
    rec = dot(scores[...], p2.astype(BF))
    rms = lax.rsqrt(jnp.mean(rec * rec, axis=-1, keepdims=True) + epsilon)
    return (rec * rms * gain).astype(BF)


def head_backward(
    p0, p1, p2, mixed_grad, seen, carry, floor, gain, scores, key_grad, decay_grad, query_grad, *kept
):
    length = p0.shape[0]
    swish, gate, forget = gates(p0, p1, floor)
    query = p0 * swish
    key = 1.0 - forget
    allowed, tri, later = seen
    totals = exact_dot(tri, jnp.log(forget))
    fill_scores(query, key, totals, allowed, scores, kept)
    value = p2.astype(BF)
    rec = dot(scores[...], value)
    rms = lax.rsqrt(jnp.mean(rec * rec, axis=-1, keepdims=True) + epsilon)
    unit = rec * rms
    scaled = mixed_grad * gain
    rec_grad = rms * (scaled - unit * jnp.mean(scaled * unit, axis=-1, keepdims=True))
    rec_low = rec_grad.astype(BF)
    value_grad = dot(scores[...], rec_low, TN).astype(BF)
    score_grad = jnp.where(allowed, dot(rec_low, value, NT), 0.0).astype(BF)
    key_grad[...] = jnp.zeros_like(key_grad)
    decay_grad[...] = jnp.zeros_like(decay_grad)
    leads, lead_scales, trails, trail_scales = kept
    for k, (start, wide) in enumerate(strips(length)):
        rows = slice(start, start + STRIP)
        lead, lead_scale = leads[rows, :], lead_scales[rows, :]
        trail, trail_scale = trails[k, :wide, :], trail_scales[k, :wide, :]
        part = score_grad[rows, :wide]
        lead_grad = dot(part, trail)
        trail_grad = dot(part, lead, TN)
        query_grad[rows, :] = lead_grad * lead_scale
        key_grad[:wide, :] += trail_grad * trail_scale
        decay_grad[:wide, :] -= trail_grad * trail.astype(jnp.float32)
        decay_grad[rows, :] += lead_grad * lead.astype(jnp.float32)
    forget_grad = exact_dot(later, decay_grad[...]) * carry / forget
    joint = forget_grad - key_grad[...]
    floor_sum = jnp.sum(joint * (1.0 - gate), axis=0, keepdims=True)
    gain_sum = jnp.sum(mixed_grad * unit, axis=0, keepdims=True)
    g0 = (query_grad[...] * swish * (1.0 + p0 * (1.0 - swish))).astype(BF)
    g1 = (joint * (1.0 - floor) * gate * (1.0 - gate)).astype(BF)
    return g0, g1, value_grad, floor_sum, gain_sum


def load_weight(offsets_ref, sources, refs, whole, sems, begin=0):
    end = begin + whole.shape[1]
    copies = []
    for (piece, low), ref in zip(sources, refs):
        rows, lanes = ref.shape[1:]
        first, last = max(low, begin), min(low + lanes, end)
        if first >= last:
            continue
        for m in range(4):
            at = pl.multiple_of(offsets_ref[4 * piece + m], rows)
            copies.append(
                pltpu.make_async_copy(
                    ref.at[m, :, pl.ds(first - low, last - first)],
                    whole.at[pl.ds(at, rows), pl.ds(first - begin, last - first)],
                    sems.at[len(copies)],
                )
            )
    for copy in copies:
        copy.start()
    for copy in copies:
        copy.wait()


def row_copies(core, refs, whole, sems):
    count = refs[0].shape[0]
    for side in range(2):
        at = pl.multiple_of((core if side == 0 else 1 - core) * count, count)
        for m in range(4):
            ref = refs[m] if side == 0 else refs[4].at[m] if m < 3 else refs[5]
            yield m, pltpu.make_async_copy(
                ref, whole.at[m, pl.ds(at, count), :], sems.at[side, m]
            )


def start_rows(core, refs, whole, sems):
    for _, copy in row_copies(core, refs, whole, sems):
        copy.start()


def wait_rows(core, refs, whole, sems, sequence):
    for m, copy in row_copies(core, refs, whole, sems):

        @pl.when(sequence == m)
        def _():
            copy.wait()


def row_scratch(count, model):
    return [pltpu.VMEM((4, 2 * count, model), BF), pltpu.SemaphoreType.DMA((2, 4))]


def store_sends(values, send_ref, last_ref):
    sequence = pl.program_id(0)

    @pl.when(sequence < 3)
    def _():
        send_ref[0] = values.astype(BF)

    @pl.when(sequence == 3)
    def _():
        last_ref[...] = values.astype(BF)


def mixer_forward_kernel(core_ref, offsets_ref, *refs, sources):
    rows, refs = refs[:6], refs[6:]
    (col_ref, row_ref, floor_ref, gain_ref, p_ref, mixed_ref, send_ref, last_ref, keep_ref, scores, whole,
     back, tokens, token_sems, weight, sems) = refs[len(sources) :]

    sequence = pl.program_id(0)

    @pl.when(sequence == 0)
    def _():
        start_rows(core_ref[0], rows, tokens, token_sems)
        load_weight(offsets_ref, sources, refs, weight, sems)

    wait_rows(core_ref[0], rows, tokens, token_sems, sequence)

    count = rows[0].shape[0]
    width = whole.shape[1]
    mine = pl.multiple_of(core_ref[0] * count, count)
    theirs = pl.multiple_of((1 - core_ref[0]) * count, count)
    p_ref[0] = dot(tokens[sequence], weight[:, : 3 * width])
    seen = masks(col_ref[0], row_ref[0])
    for h in range(width // HEAD):
        p0, p1, p2 = [p_ref[0, :, pl.ds(j * width + h * HEAD, HEAD)] for j in range(3)]
        lanes = slice(h * HEAD, (h + 1) * HEAD)
        whole[:, lanes] = head_forward(
            p0, p1, p2, seen, floor_ref[:, lanes], gain_ref[...], scores.at[h]
        )
    mixed_ref[0] = whole[...]
    back[...] = dot(whole[...], weight[:, 3 * width :], NT)
    store_sends(back[pl.ds(theirs, count), :], send_ref, last_ref)
    keep_ref[0] = back[pl.ds(mine, count), :]


def mixer_backward_kernel(core_ref, offsets_ref, *refs, sources):
    rows, refs = refs[:6], refs[6:]
    (p_ref, col_ref, row_ref, floor_ref, gain_ref, g0_ref, g1_ref, g2_ref, send_ref, last_ref, keep_ref,
     floor_sum_ref, gain_sum_ref, scores, key_grad, decay_grad, query_grad, *kept, mixed_grad, parts,
     back, tokens, token_sems, weight, sems) = refs[len(sources) :]

    sequence = pl.program_id(0)

    @pl.when(sequence == 0)
    def _():
        start_rows(core_ref[0], rows, tokens, token_sems)
        load_weight(offsets_ref, sources, refs, weight, sems)

    wait_rows(core_ref[0], rows, tokens, token_sems, sequence)

    count = rows[0].shape[0]
    width = mixed_grad.shape[1]
    mine = pl.multiple_of(core_ref[0] * count, count)
    theirs = pl.multiple_of((1 - core_ref[0]) * count, count)
    seg_col = col_ref[0]
    before = jnp.concatenate([seg_col[:1] - 1, seg_col[:-1]], axis=0)
    carry = (seg_col == before).astype(jnp.float32)
    mixed_grad[...] = dot(tokens[sequence], weight[:, 3 * width :])
    seen = masks(col_ref[0], row_ref[0])
    for h in range(width // HEAD):
        p0, p1, p2 = [p_ref[0, :, pl.ds(j * width + h * HEAD, HEAD)] for j in range(3)]
        lanes = slice(h * HEAD, (h + 1) * HEAD)
        g0, g1, g2, floor_sum, gain_sum = head_backward(
            p0, p1, p2, mixed_grad[:, lanes], seen, carry, floor_ref[:, lanes],
            gain_ref[...], scores.at[h], key_grad.at[h], decay_grad.at[h], query_grad.at[h],
            *[ref.at[h] for ref in kept],
        )
        for j, g in enumerate((g0, g1, g2)):
            parts[:, pl.ds(j * width + h * HEAD, HEAD)] = g
        floor_sum_ref[0, :, lanes] = jnp.broadcast_to(floor_sum, (8, HEAD)) * 0.125
        gain_sum_ref[0, :, lanes] = jnp.broadcast_to(gain_sum, (8, HEAD)) * 0.125

    for j, g_ref in enumerate((g0_ref, g1_ref, g2_ref)):
        g_ref[0] = parts[:, j * width : (j + 1) * width]
    back[...] = dot(parts[...], weight[:, : 3 * width], NT)
    store_sends(back[pl.ds(theirs, count), :], send_ref, last_ref)
    keep_ref[0] = back[pl.ds(mine, count), :]


def mixer_specs(count, model, width, length):
    def at(shape, index):
        return pl.BlockSpec(shape, lambda s, c, o: index(s))

    side = [
        at((1, count, model), lambda s: (jnp.minimum(s, 2), 0, 0)),
        at((count, model), lambda s: (0, 0)),
        at((1, count, model), lambda s: (s, 0, 0)),
    ]
    col = at((1, length, 1), lambda s: (s, 0, 0))
    row = at((1, 1, length), lambda s: (s, 0, 0))
    floor = at((1, width), lambda s: (0, 0))
    gain = at((1, HEAD), lambda s: (0, 0))
    wide = at((1, length, 3 * width), lambda s: (s, 0, 0))
    pair = at((1, length, width), lambda s: (s, 0, 0))
    return at, side, wide, pair, [col, row, floor, gain]


def weight_scratch(model, lanes, sources):
    return [pltpu.VMEM((model, lanes), BF), pltpu.SemaphoreType.DMA((4 * len(sources),))]


def layout_of(sources):
    return tuple((piece, low) for piece, low, _ in sources), [part for _, _, part in sources]


def mixer_forward(core, offsets, tokens, sources, segments, floor, gain):
    groups, length, _ = segments[0].shape
    count, model = tokens[0].shape
    width = floor.shape[0]
    at, side, wide, pair, small = mixer_specs(count, model, width, length)
    layout, parts = layout_of(sources)
    shape = jax.ShapeDtypeStruct
    return pl.pallas_call(
        functools.partial(mixer_forward_kernel, sources=layout),
        grid_spec=pltpu.PrefetchScalarGridSpec(
            num_scalar_prefetch=2,
            grid=(groups,),
            in_specs=[pl.BlockSpec(memory_space=pl.ANY)] * (6 + len(parts)) + small,
            out_specs=[wide, pair] + side,
            scratch_shapes=[
                pltpu.VMEM((width // HEAD, length, length), BF),
                pltpu.VMEM((length, width), BF),
                pltpu.VMEM((length, model), jnp.float32),
            ]
            + row_scratch(count, model)
            + weight_scratch(model, 4 * width, parts),
        ),
        out_shape=[
            shape((groups, length, 3 * width), jnp.float32),
            shape((groups, length, width), BF),
            shape((groups - 1, count, model), BF),
            shape((count, model), BF),
            shape((groups, count, model), jnp.float32),
        ],
        compiler_params=PARAMS,
        cost_estimate=LONG,
        name="mixer_forward",
    )(
        core, offsets, *tokens, *parts, segments[0],
        segments[1], floor[None], gain[None],
    )


def mixer_backward(core, offsets, tokens, sources, projected, segments, floor, gain):
    groups, length, _ = segments[0].shape
    count, model = tokens[0].shape
    width = floor.shape[0]
    at, side, wide, pair, small = mixer_specs(count, model, width, length)
    layout, parts = layout_of(sources)
    heads = width // HEAD
    sums = at((1, 8, width), lambda s: (s, 0, 0))
    shape = jax.ShapeDtypeStruct
    return pl.pallas_call(
        functools.partial(mixer_backward_kernel, sources=layout),
        grid_spec=pltpu.PrefetchScalarGridSpec(
            num_scalar_prefetch=2,
            grid=(groups,),
            in_specs=[pl.BlockSpec(memory_space=pl.ANY)] * (6 + len(parts))
            + [wide]
            + small,
            out_specs=[pair] * 3 + side + [sums, sums],
            scratch_shapes=[pltpu.VMEM((heads, length, length), BF)]
            + [pltpu.VMEM((heads, length, HEAD), jnp.float32)] * 3
            + [pltpu.VMEM((heads, length, HEAD), kind) for kind in (BF, jnp.float32)]
            + [
                pltpu.VMEM((heads, length // STRIP, length, HEAD), kind)
                for kind in (BF, jnp.float32)
            ]
            + [pltpu.VMEM((length, width), jnp.float32), pltpu.VMEM((length, 3 * width), BF)]
            + [pltpu.VMEM((length, model), jnp.float32)]
            + row_scratch(count, model)
            + weight_scratch(model, 4 * width, parts),
        ),
        out_shape=[
            shape((groups, length, width), BF),
            shape((groups, length, width), BF),
            shape((groups, length, width), BF),
            shape((groups - 1, count, model), BF),
            shape((count, model), BF),
            shape((groups, count, model), jnp.float32),
        ]
        + [shape((groups, 8, width), jnp.float32)] * 2,
        compiler_params=PARAMS,
        cost_estimate=LONG,
        name="mixer_backward",
    )(
        core, offsets, *tokens, *parts, projected, segments[0],
        segments[1], floor[None], gain[None],
    )


def tops_kernel(core_ref, offsets_ref, *refs, sources):
    rows, refs = refs[:6], refs[6:]
    out_ref, tokens, token_sems, weight, sems = refs[len(sources) :]
    sequence = pl.program_id(0)

    @pl.when(sequence == 0)
    def _():
        start_rows(core_ref[0], rows, tokens, token_sems)
        load_weight(offsets_ref, sources, refs, weight, sems)

    wait_rows(core_ref[0], rows, tokens, token_sems, sequence)
    out_ref[0] = dot(tokens[sequence], weight[...])


def tops_product(core, offsets, tokens, sources, width):
    count, model = tokens[0].shape
    layout, parts = layout_of(sources)
    return pl.pallas_call(
        functools.partial(tops_kernel, sources=layout),
        grid_spec=pltpu.PrefetchScalarGridSpec(
            num_scalar_prefetch=2,
            grid=(4,),
            in_specs=[pl.BlockSpec(memory_space=pl.ANY)] * (6 + len(parts)),
            out_specs=pl.BlockSpec((1, 2 * count, width), lambda s, c, o: (s, 0, 0)),
            scratch_shapes=row_scratch(count, model) + weight_scratch(model, width, parts),
        ),
        out_shape=jax.ShapeDtypeStruct((4, 2 * count, width), jnp.float32),
        compiler_params=PARAMS,
        cost_estimate=LONG,
        name="tops_product",
    )(core, offsets, *tokens, *parts)


def ffn_kernel(core_ref, offsets_ref, *refs, sources, units):
    rows, active_grad_ref, refs = refs[:6], refs[6], refs[7:]
    (*parts, send_ref, last_ref, keep_ref, grads, back,
     tokens, token_sems, weight, sems) = refs[len(sources) :]
    sequence = pl.program_id(0)

    @pl.when(sequence == 0)
    def _():
        start_rows(core_ref[0], rows, tokens, token_sems)
        load_weight(offsets_ref, sources, refs, weight, sems, grads.shape[1] - 2 * units)

    wait_rows(core_ref[0], rows, tokens, token_sems, sequence)
    width = units
    count = rows[0].shape[0]
    mine = pl.multiple_of(core_ref[0] * count, count)
    theirs = pl.multiple_of((1 - core_ref[0]) * count, count)
    both = dot(tokens[sequence], weight[...])
    gate, up = both[:, :width], both[:, width:]
    active_grad = active_grad_ref[0, :, :width]
    squash = jax.nn.sigmoid(gate)
    swish = gate * squash
    gate_grad = active_grad * up * squash * (1.0 + gate * (1.0 - squash))
    grads[:, : 2 * width] = jnp.concatenate([gate_grad, active_grad * swish], axis=1).astype(BF)
    spare = jnp.zeros((2 * count, grads.shape[1] - 3 * width), BF)
    grads[:, 2 * width :] = jnp.concatenate([(swish * up).astype(BF), spare], axis=1)
    low = 0
    for part_ref in parts:
        part_ref[0] = grads[:, low : low + part_ref.shape[2]]
        low += part_ref.shape[2]
    back[...] = dot(grads[:, : 2 * width], weight[...], NT)
    store_sends(back[pl.ds(theirs, count), :], send_ref, last_ref)
    keep_ref[0] = back[pl.ds(mine, count), :]


def ffn(core, offsets, tokens, active_grad, sources, width, widths):
    count, model = tokens[0].shape
    groups, length = 4, 2 * count
    total = sum(widths)
    layout, parts = layout_of(sources)

    def at(rows, lanes):
        return pl.BlockSpec((1, rows, lanes), lambda s, c, o: (s, 0, 0))

    shape = jax.ShapeDtypeStruct
    return pl.pallas_call(
        functools.partial(ffn_kernel, sources=layout, units=width),
        grid_spec=pltpu.PrefetchScalarGridSpec(
            num_scalar_prefetch=2,
            grid=(groups,),
            in_specs=[pl.BlockSpec(memory_space=pl.ANY)] * 6
            + [at(length, active_grad.shape[2])]
            + [pl.BlockSpec(memory_space=pl.ANY)] * len(parts),
            out_specs=[at(length, n) for n in widths]
            + [
                pl.BlockSpec((1, count, model), lambda s, c, o: (jnp.minimum(s, 2), 0, 0)),
                pl.BlockSpec((count, model), lambda s, c, o: (0, 0)),
                at(count, model),
            ],
            scratch_shapes=[
                pltpu.VMEM((length, total), BF),
                pltpu.VMEM((length, model), jnp.float32),
            ]
            + row_scratch(count, model)
            + weight_scratch(model, 2 * width, parts),
        ),
        out_shape=[
            *[shape((groups, length, n), BF) for n in widths],
            shape((groups - 1, count, model), BF),
            shape((count, model), BF),
            shape((groups, count, model), jnp.float32),
        ],
        compiler_params=PARAMS,
        cost_estimate=LONG,
        name="ffn",
    )(core, offsets, *tokens, active_grad, *parts)


def rows_kernel(core_ref, offsets_ref, *refs, sources, begin, number):
    own, refs = refs[:number], refs[number:]
    out_ref, whole, sems = refs[len(sources) :]

    @pl.when(pl.program_id(0) == 0)
    def _():
        load_weight(offsets_ref, sources, refs, whole, sems, begin)

    out_ref[0] = dot(jnp.concatenate([r[0] for r in own], axis=1), whole[...], NT).astype(BF)


def rows_product(core, offsets, own, sources, begin, model, estimate=SHORT):
    groups, length, _ = own[0].shape
    width = sum(o.shape[2] for o in own)
    layout, parts = layout_of(sources)

    def at(rows, lanes):
        return pl.BlockSpec((1, rows, lanes), lambda s, c, o: (s, 0, 0))

    shape = jax.ShapeDtypeStruct
    return pl.pallas_call(
        functools.partial(rows_kernel, sources=layout, begin=begin, number=len(own)),
        grid_spec=pltpu.PrefetchScalarGridSpec(
            num_scalar_prefetch=2,
            grid=(groups,),
            in_specs=[at(length, o.shape[2]) for o in own] + [pl.BlockSpec(memory_space=pl.ANY)] * len(parts),
            out_specs=pl.BlockSpec((1, length, model), lambda s, c, o: (s ^ c[1], 0, 0)),
            scratch_shapes=weight_scratch(model, width, parts),
        ),
        out_shape=shape((groups, length, model), BF),
        compiler_params=PARAMS,
        cost_estimate=estimate,
        name="rows_product",
    )(core, offsets, *own, *parts)


def grad_kernel(core_ref, blocks_ref, *refs, number):
    rows, grads, outs, tokens = refs[:6], refs[6 : 6 + number], refs[6 + number : -1], refs[-1]
    count = rows[0].shape[0]
    for side in range(2):
        at = core_ref[0] if side == 0 else 1 - core_ref[0]
        for m in range(4):
            first = pl.multiple_of((2 * m + at) * count, count)
            part = rows[m][...] if side == 0 else rows[4][m] if m < 3 else rows[5][...]
            tokens[pl.ds(first, count), :] = part
    for grad_ref, out_ref in zip(grads, outs):
        out_ref[0] = dot(tokens[...], grad_ref[...], TN).astype(out_ref.dtype)


def grad_product(core, tokens, grads, blocks, wide, kind, estimate):
    count, model = tokens[0].shape
    side = pl.BlockSpec((count, wide), lambda i, c, b: (0, b[i]))
    three = pl.BlockSpec((3, count, wide), lambda i, c, b: (0, 0, b[i]))
    number = blocks.shape[0]
    return pl.pallas_call(
        functools.partial(grad_kernel, number=len(grads)),
        grid_spec=pltpu.PrefetchScalarGridSpec(
            num_scalar_prefetch=2,
            grid=(number,),
            in_specs=[side] * 4
            + [three, side]
            + [pl.BlockSpec(g.shape, lambda i, c, b: (0, 0)) for g in grads],
            out_specs=[pl.BlockSpec((1, wide, g.shape[1]), lambda i, c, b: (i, 0, 0)) for g in grads],
            scratch_shapes=[pltpu.VMEM((8 * count, wide), BF)],
        ),
        out_shape=[jax.ShapeDtypeStruct((number, wide, g.shape[1]), kind) for g in grads],
        compiler_params=PARAMS,
        cost_estimate=estimate,
        name="grad_product",
    )(core, blocks, *tokens, *grads)


def rms_of(values):
    return lax.rsqrt(jnp.mean(values * values, axis=-1, keepdims=True) + epsilon)


def last_kernel(keep_ref, came_ref, out_ref):
    out_ref[...] = (keep_ref[0] + came_ref[...].astype(jnp.float32)).astype(BF)


def add_last(keep, came):
    count, model = came.shape
    block = count // 2
    return pl.pallas_call(
        last_kernel,
        grid=(2,),
        in_specs=[
            pl.BlockSpec((1, block, model), lambda i: (3, i, 0)),
            pl.BlockSpec((block, model), lambda i: (i, 0)),
        ],
        out_specs=pl.BlockSpec((block, model), lambda i: (i, 0)),
        out_shape=jax.ShapeDtypeStruct(came.shape, BF),
        compiler_params=PARAMS,
        cost_estimate=SHORT,
        name="add_last",
    )(keep, came)


def cores_kernel(keep_ref, came_ref, own_ref, x_ref, z_ref):
    own_ref[...] = keep_ref[0] + came_ref[0].astype(jnp.float32)
    for m, out_ref in enumerate((x_ref, z_ref), 1):
        out_ref[...] = (keep_ref[m] + came_ref[m].astype(jnp.float32)).astype(BF)


def add_cores(keep, came):
    count, model = keep.shape[1:]
    block = count // 2
    three = pl.BlockSpec((3, block, model), lambda i: (0, i, 0))
    one = pl.BlockSpec((block, model), lambda i: (i, 0))
    shape = jax.ShapeDtypeStruct
    return pl.pallas_call(
        cores_kernel,
        grid=(2,),
        in_specs=[three, three],
        out_specs=[one] * 3,
        out_shape=[shape((count, model), jnp.float32)] + [shape((count, model), BF)] * 2,
        compiler_params=PARAMS,
        cost_estimate=SHORT,
        name="add_cores",
    )(keep, came)


def middle_kernel(own_ref, x_ref, z_ref, hidden_ref, gain_ref, middle_ref, normed_ref):
    branch = own_ref[...] + x_ref[...].astype(jnp.float32) + z_ref[...].astype(jnp.float32)
    middle = hidden_ref[...].astype(jnp.float32) + branch
    middle_ref[...] = middle
    normed_ref[...] = (middle * rms_of(middle) * gain_ref[...]).astype(BF)


def back_kernel(own_ref, x_ref, z_ref, values_ref, add_ref, gain_ref, out_ref, low_ref, sum_ref):
    grad = own_ref[...] + x_ref[...].astype(jnp.float32) + z_ref[...].astype(jnp.float32)
    values = values_ref[...].astype(jnp.float32)
    scale = rms_of(values)
    unit = values * scale
    wide = grad * gain_ref[...]
    inner = wide - unit * jnp.mean(wide * unit, axis=-1, keepdims=True)
    out = add_ref[...].astype(jnp.float32) + scale * inner
    out_ref[...] = out
    low_ref[...] = out.astype(BF)

    @pl.when(pl.program_id(0) == 0)
    def _():
        sum_ref[...] = jnp.zeros_like(sum_ref)

    sum_ref[...] += jnp.sum(grad * unit, axis=0, keepdims=True)


def row_call(kernel, name, kinds, *args):
    count, model = args[0].shape
    block = count // 4

    def spec(one):
        if one:
            return pl.BlockSpec((1, model), lambda i: (0, 0))
        return pl.BlockSpec((block, model), lambda i: (i, 0))

    shapes = [jax.ShapeDtypeStruct((1 if k is None else count, model), k or jnp.float32) for k in kinds]
    return pl.pallas_call(
        kernel,
        grid=(4,),
        in_specs=[spec(a.shape[0] == 1) for a in args],
        out_specs=[spec(k is None) for k in kinds],
        out_shape=shapes,
        compiler_params=PARAMS,
        cost_estimate=LONG,
        name=name,
    )(*args)


def mix_grad_kernel(parts_ref, out_ref):
    quarter = parts_ref.shape[2] // 4
    for j, at in enumerate((1, 3, 0, 2)):
        for m in range(4):
            part = parts_ref[m, :, at * quarter : (at + 1) * quarter]
            out_ref[:, j, m * quarter : (m + 1) * quarter] = part.astype(jnp.float32)


def mix_grad_of(parts):
    _, rows, wide = parts.shape
    block = min(rows, 64)
    return pl.pallas_call(
        mix_grad_kernel,
        grid=(rows // block,),
        in_specs=[pl.BlockSpec((4, block, wide), lambda i: (0, i, 0))],
        out_specs=pl.BlockSpec((block, 4, wide), lambda i: (i, 0, 0)),
        out_shape=jax.ShapeDtypeStruct((rows, 4, wide), jnp.float32),
        compiler_params=PARAMS,
        cost_estimate=SHORT,
        name="mix_grad",
    )(parts)


DOWN_FIRST = 256


def ffn_grad_kernel(first_ref, second_ref, out_ref):
    units = out_ref.shape[2] // 4
    for j in range(3):
        parts = []
        for m in range(4):
            down = first_ref.shape[2] - DOWN_FIRST
            gates = jnp.concatenate([first_ref[m, :, down:], second_ref[m]], axis=1)
            parts.append(first_ref[m, :, :units] if j == 2 else gates[:, j * units : (j + 1) * units])
        out_ref[j] = jnp.concatenate(parts, axis=1).astype(jnp.float32)


def ffn_grad_of(parts, units):
    rows = parts[0].shape[1]
    block = min(rows, 32)
    out = pl.pallas_call(
        ffn_grad_kernel,
        grid=(rows // block,),
        in_specs=[pl.BlockSpec((4, block, p.shape[2]), lambda i: (0, i, 0)) for p in parts],
        out_specs=pl.BlockSpec((3, block, 4 * units), lambda i: (0, i, 0)),
        out_shape=jax.ShapeDtypeStruct((3, rows, 4 * units), jnp.float32),
        compiler_params=PARAMS,
        cost_estimate=LONG,
        name="ffn_grad",
    )(*parts)
    return out.transpose(1, 0, 2)


def near_kernel(*refs, number, ends):
    home_ref, away_ref = refs[2 * number :]
    block = pl.program_id(0)
    last = pl.num_programs(0) // ends
    for k in range(number):
        keep_ref, came_ref = refs[2 * k], refs[2 * k + 1]
        low = sum(refs[2 * j].shape[2] for j in range(k))
        total = keep_ref[0] + came_ref[0].astype(jnp.float32)
        lanes = slice(low, low + keep_ref.shape[2])

        @pl.when(block < pl.num_programs(0) - last)
        def _():
            away_ref[0, :, lanes] = total.astype(BF)

        @pl.when(block >= pl.num_programs(0) - last)
        def _():
            home_ref[0, :, lanes] = total


def near_sums(pairs, estimate=SHORT):
    highs = lax.axis_size("h")
    blocks, rows, _ = pairs[0][0].shape
    away_count = blocks - 2
    wide = sum(keep.shape[2] for keep, _ in pairs)
    specs, args = [], []
    for pair in pairs:
        specs += [pl.BlockSpec((1,) + pair[0].shape[1:], lambda i: (i, 0, 0))] * 2
        args += list(pair)
    home, away = pl.pallas_call(
        functools.partial(near_kernel, number=len(pairs), ends=highs),
        grid=(blocks,),
        in_specs=specs,
        out_specs=[
            pl.BlockSpec((1, rows, wide), lambda i: (jnp.maximum(i - away_count, 0), 0, 0)),
            pl.BlockSpec((1, rows, wide), lambda i: (jnp.minimum(i, away_count - 1), 0, 0)),
        ],
        out_shape=[
            jax.ShapeDtypeStruct((2, rows, wide), jnp.float32),
            jax.ShapeDtypeStruct((away_count, rows, wide), BF),
        ],
        compiler_params=PARAMS,
        cost_estimate=estimate,
        name="near_sums",
    )(*args)
    return home, [away[2 * k : 2 * k + 2] for k in range(highs - 1)]


def far_kernel(*refs, counts):
    out_ref = refs[-1]
    low, at = 0, 0
    for count in counts:
        total = refs[at][0]
        for ref in refs[at + 1 : at + 1 + count]:
            total = total + ref[0].astype(jnp.float32)
        out_ref[0, :, low : low + total.shape[1]] = total.astype(BF)
        low, at = low + total.shape[1], at + 1 + count


def far_sums(pairs, estimate=SHORT):
    _, rows, _ = pairs[0][0].shape
    wide = sum(home.shape[2] for home, _ in pairs)
    args = [part for home, fars in pairs for part in (home, *fars)]
    out = pl.pallas_call(
        functools.partial(far_kernel, counts=[len(fars) for _, fars in pairs]),
        grid=(2,),
        in_specs=[pl.BlockSpec((1,) + a.shape[1:], lambda i: (i, 0, 0)) for a in args],
        out_specs=pl.BlockSpec((1, rows, wide), lambda i: (i, 0, 0)),
        out_shape=jax.ShapeDtypeStruct((2, rows, wide), BF),
        compiler_params=PARAMS,
        cost_estimate=estimate,
        name="far_sums",
    )(*args)
    return out.reshape(4, rows // 2, wide)


GROUP = ("l", "x")


def swap(values, axes):
    total = 2 ** len(axes)
    return lax.ppermute(values, axes, [(s, total - 1 - s) for s in range(total)])


def shift(values, steps):
    total = lax.axis_size("h")
    return lax.ppermute(values, "h", [(s, (s + steps) % total) for s in range(total)])


def pick(values, index):
    return lax.dynamic_index_in_dim(values, index, 0, keepdims=False)


def over_c(values):
    return swap(values, ("tensor",))


def over_x(values):
    return swap(values, ("x",))


def over_y(values):
    return swap(values, ("y",))


def over_z(values):
    return swap(values, ("l",))


def own_member():
    return lax.axis_index("l") * 2 + lax.axis_index("x")


def source_rows(rows):
    y, high = lax.axis_index("y"), lax.axis_index("h")
    highs = lax.axis_size("h")
    starts = []
    for k in range(highs):
        for side in (y, 1 - y):
            for member in range(4):
                block = ((high - k) % highs) * 8 + (member >> 1) * 4 + side * 2 + (member & 1)
                starts.append(block * rows)
    return jnp.stack(starts).astype(jnp.int32)


def trade(slices):
    return lax.all_to_all(slices, GROUP, 0, 0, tiled=True)


def after(values, *others):
    return lax.optimization_barrier((values, others))[0]


def far(block):
    return [shift(block, k) for k in range(1, lax.axis_size("h"))]


def near(parts):
    return [over_y(part) for part in parts]


def pieces(low, straight, crossed):
    out = []
    for k, (one, two) in enumerate(zip(straight, crossed), 1):
        out += [(2 * k, low, one), (2 * k + 1, low, two)]
    return out


def half_grads(core, tokens, grads, yy, kind, estimate):
    highs, high = lax.axis_size("h"), lax.axis_index("h")
    wide = tokens[0].shape[1] // (4 * highs)
    order = [(high + k) % highs for k in range(1, highs)] + [high]
    blocks = jnp.stack([(h * 2 + z) * 2 + yy for h in order for z in range(2)]).astype(jnp.int32)
    grads = [flat(g) for g in grads]
    if wide % 128 == 0:
        return grad_product(core, tokens, grads, blocks, wide, kind, estimate)
    sides = [jnp.stack(tokens[:4]), jnp.concatenate([tokens[4], tokens[5][None]])]
    ordered = [jnp.where(core[0] == 0, a, b) for a, b in (sides, sides[::-1])]
    whole = jnp.stack(ordered, axis=1)
    split = jnp.take(whole.reshape(grads[0].shape[0], -1, wide), blocks, axis=1)
    return [
        jnp.einsum("tad,tx->adx", split, g, preferred_element_type=jnp.float32).astype(kind)
        for g in grads
    ]


def grad_sends(core, tokens, grads, estimate=SHORT):
    return half_grads(core, tokens, grads, 1 - lax.axis_index("y"), BF, estimate)


def grad_keeps(core, tokens, grads, estimate=SHORT):
    return half_grads(core, tokens, grads, lax.axis_index("y"), jnp.float32, estimate)


def send_far(away):
    return [shift(part, k) for k, part in enumerate(away, 1)]


def flat(values):
    return values.reshape(-1, values.shape[-1])


def add_low(keep, came):
    return (keep.astype(jnp.float32) + came.astype(jnp.float32)).astype(BF)


def sum_pair(values, first, second):
    parts = [values, swap(values, (second,)), swap(values, (first,)), swap(values, (first, second))]
    return jnp.stack(parts), lax.axis_index(first) * 2 + lax.axis_index(second)


def add_pair(parts, place):
    return sum(pick(parts, place ^ m) for m in range(4))


def sum_highs(values):
    size, bits = lax.axis_size("h"), 1
    while bits < size:
        values = values + lax.ppermute(values, "h", [(s, s ^ bits) for s in range(size)])
        bits *= 2
    return values


def body(
    hidden_in,
    segments,
    mix_weights,
    ffn_weights,
    norm1_gain,
    norm2_gain,
    head_gain,
    lower_bound,
    out_grad,
):
    core, member = lax.axis_index("tensor"), own_member()
    core_at = jnp.stack([core, member]).astype(jnp.int32)
    rows = mix_weights.shape[0]
    offsets = source_rows(rows)
    quarter, units = lower_bound.shape[0] // 4, ffn_weights.shape[2] // 4
    model = hidden_in.shape[1]
    channels = 4 * quarter
    lanes = -(-3 * units // 128) * 128

    def slices(weights, width):
        split = weights.reshape(rows, weights.shape[1], 4, -1).transpose(2, 0, 1, 3)
        split = split.reshape(4, rows, -1)
        return jnp.pad(split, ((0, 0), (0, 0), (0, width - split.shape[2])))

    length = segments.shape[1]
    labels = jnp.pad(segments.astype(BF), ((0, 15), (0, channels - length)))
    labels = jnp.broadcast_to(labels, (4,) + labels.shape)
    hidden = hidden_in.astype(jnp.float32)
    scale_one = rms_of(hidden)
    normed = (hidden * scale_one * norm1_gain).astype(BF)
    floor = lax.dynamic_slice_in_dim(lower_bound, member * quarter, quarter)
    feed = slices(ffn_weights, 3 * units)
    spare = lanes - 3 * units
    down = jnp.pad(feed[..., 2 * units :], ((0, 0), (0, 0), (0, spare)))
    feed = jnp.concatenate([down, feed[..., : 2 * units]], axis=-1)
    mix = slices(mix_weights, channels)

    mix = trade(jnp.concatenate([slices(mix_weights, channels), labels], axis=1))

    gate = (mix, normed, feed)
    mix, normed, feed = lax.optimization_barrier(gate)
    labels = mix[:, rows, :length].astype(jnp.int32)
    labels = jnp.stack([pick(labels, member ^ m) for m in range(4)])
    mix = mix[:, :rows]
    cuts = [0, 512, 1024, 1152, 1408, 1664, 1920, lanes]
    feed_cut = cuts[4]
    mix_far = far(mix)
    mix_near = over_y(mix)
    feed_one = trade(feed[..., :feed_cut])
    feed_rest = after(feed[..., feed_cut:], gate)
    normed_x, normed_z = over_x(normed), over_z(normed)
    top_x = over_x(after(out_grad, gate))

    columns = jnp.broadcast_to(labels[:, :, None], labels.shape + (1,))
    gate = (mix_far, mix_near, feed_one, feed_rest, normed_x, normed_z, top_x, floor, columns)
    floor = after(floor, gate)
    labels = (after(columns, gate), labels[:, None, :])
    mix_cross = near(after(mix_far, gate))
    ones = [feed_one[..., low:high] for low, high in zip(cuts[:4], cuts[1:5])]
    far_a = far(after(ones[0], gate))
    normed_xz = over_x(after(normed_z, gate))
    normed_three = jnp.stack(after([normed, normed_x, normed_z], gate))
    top_z = over_z(after(out_grad, gate))
    near_a = over_y(after(feed_one[..., :256], gate))

    gate = (mix_cross, far_a, normed_xz, normed_three, top_z, ones, near_a)
    normed_c, normed_cxz = over_c(after(normed_three, gate)), over_c(after(normed_xz, gate))
    normed = [normed, normed_x, normed_z, normed_xz, normed_c, normed_cxz]
    mix_sources = [(0, 0, mix), (1, 0, mix_near)] + pieces(0, mix_far, mix_cross)

    gate = (normed_c, normed_cxz)
    far_b = far(after(ones[1], gate))
    near_b = over_y(after(feed_one[..., 256:768], gate))
    cross_a = near(after(far_a, gate))
    top_xz = over_x(after(top_z, gate))
    feed_two = trade(after(feed_rest, gate))
    projected, mixed, send, send_xz, keep = mixer_forward(
        core_at, offsets, after(normed, gate), mix_sources, labels, floor, head_gain
    )

    gate = (send, far_b, near_b, cross_a, top_xz, feed_two)
    came_xz = over_c(after(send_xz, gate))
    came = over_c(after(send, gate))
    near_c = over_y(after(feed_one[..., 768:1024], gate))
    top_cxz = over_c(after(top_xz, gate))
    top_three = jnp.stack(after([out_grad, top_x, top_z], gate))
    far_c = far(after(ones[2], gate))
    to_xz = add_last(keep, came_xz)

    gate = (to_xz, near_c, far_c, top_cxz, top_three)
    from_x = over_x(after(to_xz, gate))
    far_d = far(after(ones[3], gate))
    cross_b = near(after(far_b, gate))
    own, to_x, to_z = add_cores(keep, after(came, gate))
    top_c = over_c(after(top_three, gate))
    tops = [out_grad, top_x, top_z, top_xz, top_c, top_cxz]

    gate = (from_x, far_d, cross_b, own, top_c)
    to_z = add_low(to_z, after(from_x, gate))
    of_x = over_x(after(to_x, gate))
    of_z = over_z(to_z)
    far_e = far(after(feed_two[..., : cuts[5] - feed_cut], gate))
    near_d = over_y(after(feed_one[..., 1024:], gate))
    near_e = over_y(after(feed_two[..., :384], gate))

    gate = (of_x, of_z, far_e, near_d, near_e)
    far_f = far(after(feed_two[..., cuts[5] - feed_cut : cuts[6] - feed_cut], gate))
    near_f = over_y(after(feed_two[..., 384:], gate))
    cross_cd = [
        over_y(jnp.concatenate([one, two], axis=-1))
        for one, two in zip(after(far_c, gate), after(far_d, gate))
    ]
    middle, normed_two = row_call(
        middle_kernel, "middle", [jnp.float32, BF], *after((own, of_x, of_z), gate), hidden_in,
        norm2_gain[None],
    )
    two_x, two_z = over_x(normed_two), over_z(normed_two)
    down_sources = [(0, 0, feed_one), (1, 0, near_a), (1, 256, near_b)]
    for low, straight, crossed in zip(cuts, [far_a, far_b], [cross_a, cross_b]):
        down_sources += pieces(low, straight, crossed)
    active_grad = tops_product(
        core_at, offsets, after(tops, normed_two), down_sources, lanes - 2 * units
    )

    gate = (far_f, near_f, cross_cd, two_x, two_z, active_grad)
    far_g = far(after(feed_two[..., cuts[6] - feed_cut :], gate))
    cross_e, cross_f = near(after(far_e, gate)), near(after(far_f, gate))
    two_xz = over_x(after(two_z, gate))
    two_three = jnp.stack(after([normed_two, two_x, two_z], gate))

    gate = (far_g, cross_e, cross_f, two_xz, two_three)
    cross_g = near(after(far_g, gate))
    two_c, two_cxz = over_c(after(two_three, gate)), over_c(after(two_xz, gate))
    normed_two = [normed_two, two_x, two_z, two_xz, two_c, two_cxz]
    feed_sources = [(0, 0, feed_one), (0, feed_cut, feed_two)]
    feed_sources += [(1, 0, near_a), (1, 256, near_b), (1, 768, near_c), (1, 1024, near_d)]
    feed_sources += [(1, feed_cut, near_e), (1, feed_cut + 384, near_f)]
    fars = [far_a, far_b, far_c, far_d, far_e, far_f, far_g]
    for low, part in zip(cuts, fars):
        feed_sources += [(2 * k, low, one) for k, one in enumerate(part, 1)]
    crosses = [cross_a, cross_b, cross_cd, cross_e, cross_f, cross_g]
    for low, part in zip(cuts[:3] + cuts[4:], crosses):
        feed_sources += [(2 * k + 1, low, one) for k, one in enumerate(part, 1)]

    widths = [256, 128, 384, 256, 256, 128, 256, 256, lanes - 1920]
    *grads, send, send_xz, keep = ffn(
        core_at, offsets, normed_two, active_grad, feed_sources, units, widths
    )
    gates, downs = grads[:6], grads[6:]
    came_xz, came = over_c(send_xz), over_c(send)
    down_sends = grad_sends(core_at, after(tops, send), downs, LONG)
    to_xz = add_last(keep, after(came_xz, down_sends))

    gate = (to_xz,)
    from_x = over_x(after(to_xz, gate))
    down_one = over_y(after(down_sends[0], gate))
    gate_sends = grad_sends(core_at, after(normed_two, gate), gates, LONG)
    own, to_x, to_z = add_cores(keep, after(came, gate_sends))

    gate = (from_x, down_one, own)
    to_z = add_low(to_z, after(from_x, gate))
    of_x = over_x(after(to_x, gate))
    of_z = over_z(to_z)
    down_two = over_y(after(down_sends[1], gate))
    down_keeps = grad_keeps(core_at, after(tops, gate), downs, LONG)
    down_home, down_away = near_sums([(down_keeps[0], after(down_one, gate))])

    gate = (of_x, of_z, down_two, down_away)
    down_fars = send_far(after(down_away, gate))
    down_three = over_y(after(down_sends[2], gate))
    two_came = over_y(after(gate_sends[1], gate))
    middle_grad, middle_low, gain_two_grad = row_call(
        back_kernel, "middle_grad", [jnp.float32, BF, None], *after((own, of_x, of_z), gate),
        middle, out_grad, norm2_gain[None],
    )
    grad_x, grad_z = over_x(middle_low), over_z(middle_low)
    gate_keeps = grad_keeps(core_at, after(normed_two, middle_low), gates, LONG)
    down_home_two, down_away_two = near_sums(
        [(after(down_keeps[1], gate_keeps), after(down_two, gate))]
    )

    gate = (grad_x, grad_z, down_three, two_came, down_away_two, down_fars)
    down_fars_two = send_far(after(down_away_two, gate))
    one_came = over_y(after(gate_sends[0], gate))
    grad_xz = over_x(after(grad_z, gate))
    grad_three = jnp.stack(after([middle_low, grad_x, grad_z], gate))
    branch = rows_product(
        core_at, offsets, after(downs, gate), down_sources, 0, model, LONG
    )

    gate = early = (grad_xz, grad_three, branch, down_fars_two, one_came)
    grad_c, grad_cxz = over_c(after(grad_three, gate)), over_c(after(grad_xz, gate))
    one_home, one_away = near_sums(
        [
            (down_keeps[2], after(down_three, gate)),
            (gate_keeps[0], after(one_came, gate)),
        ],
        LONG,
    )
    middle_full = [middle_low, grad_x, grad_z, grad_xz, grad_c, grad_cxz]

    gate = (grad_c, grad_cxz, one_away)
    one_fars = send_far(after(one_away, gate))
    three_came, four_came = [over_y(after(part, early)) for part in gate_sends[2:4]]
    branch = lax.psum_scatter(
        after(branch, gate).reshape(-1, model), GROUP + ("tensor",), scatter_dimension=0, tiled=True
    )
    middle_full = after(middle_full, gate)
    *mix_grads, send, send_xz, keep, floor_sums, gain_sums = mixer_backward(
        core_at, offsets, middle_full, mix_sources, projected, labels, floor, head_gain
    )

    gate = (send, one_fars, three_came, four_came)
    came_xz, came = over_c(after(send_xz, gate)), over_c(after(send, gate))
    five_came = over_y(after(gate_sends[4], gate))
    three_home, three_away = near_sums(
        [(gate_keeps[1], after(two_came, gate)), (gate_keeps[2], three_came)], LONG
    )
    to_xz = add_last(keep, after(came_xz, three_away))

    gate = (to_xz,)
    three_fars = send_far(after(three_away, gate))
    from_x = over_x(after(to_xz, gate))
    six_came = over_y(after(gate_sends[5], gate))
    query_send, forget_send, value_send = grad_sends(core_at, after(normed, gate), mix_grads, LONG)
    own, to_x, to_z = add_cores(keep, after(came, value_send))
    four_home, four_away = near_sums(
        [
            (gate_keeps[3], after(four_came, own)),
            (gate_keeps[4], five_came),
            (gate_keeps[5], six_came),
        ]
    )

    gate = (from_x, three_fars, four_away)
    four_fars = send_far(after(four_away, gate))
    to_z = add_low(to_z, after(from_x, gate))
    of_x = over_x(after(to_x, gate))
    of_z = over_z(to_z)
    value_came, query_came = over_y(after(value_send, gate)), over_y(after(query_send, gate))
    query_keep, forget_keep, value_keep = grad_keeps(core_at, after(normed, gate), mix_grads, LONG)
    (last_send,) = grad_sends(core_at, after(middle_full, value_keep), [mixed])
    down_parts = [(down_home, down_fars), (down_home_two, down_fars_two), (one_home, one_fars)]
    down_parts = far_sums(after(down_parts, last_send))
    near_home, near_away = near_sums(
        [(value_keep, after(value_came, down_parts)), (query_keep, query_came)]
    )

    gate = (of_x, of_z, four_fars, near_away)
    near_fars = send_far(after(near_away, gate))
    last_came, forget_came = over_y(after(last_send, gate)), over_y(after(forget_send, gate))
    down_parts = trade(after(down_parts, gate))
    input_grad, _, gain_one_grad = row_call(
        back_kernel, "input_grad", [jnp.float32, BF, None], *after((own, of_x, of_z), gate),
        hidden_in, middle_grad, norm1_gain[None],
    )
    (last_keep,) = grad_keeps(core_at, after(middle_full, input_grad), [mixed])
    head_grad = jnp.sum(after(gain_sums, gate).reshape(-1, HEAD), axis=0)
    lower_grad = jnp.zeros((2, 4, quarter), jnp.float32)
    lower_grad = lax.dynamic_update_slice(
        lower_grad,
        jnp.sum(after(floor_sums, gate), axis=(0, 1)).reshape(1, 1, quarter),
        (core, member, 0),
    )
    sums = [gain_one_grad[0], gain_two_grad[0], head_grad, lower_grad.reshape(-1)]
    sums = jnp.concatenate(sums).reshape(-1, HEAD)
    block_out = (middle + after(branch, last_keep).astype(jnp.float32)).astype(BF)
    gate_parts = [(three_home, three_fars), (four_home, four_fars)]
    gate_parts = far_sums(after(gate_parts, block_out))
    pair_home, pair_away = near_sums(
        [(last_keep, after(last_came, gate_parts)), (forget_keep, forget_came)]
    )

    gate = (near_fars, down_parts, sums, pair_away, gate_parts, block_out)
    pair_fars = send_far(after(pair_away, gate))
    gate_parts = trade(after(gate_parts, gate))
    sums, place = sum_pair(after(sums, gate), "l", "x")

    gate = (pair_fars, gate_parts, sums)
    mix_parts = far_sums(after([(near_home, near_fars), (pair_home, pair_fars)], gate))
    sums, place = sum_pair(add_pair(after(sums, mix_parts), place), "y", "tensor")
    sums = sum_highs(add_pair(sums, place)).reshape(-1)
    mix_parts = trade(mix_parts)
    gain_one, gain_two, head, lower = jnp.split(sums, [model, 2 * model, 2 * model + HEAD])
    ffn_grad = ffn_grad_of(after([down_parts, gate_parts], gate), units)
    mix_grad = mix_grad_of(mix_parts)
    return (block_out, input_grad, mix_grad, ffn_grad, gain_one, gain_two, head, lower)


def solution(mesh):
    total, cores = mesh.shape["dp"], mesh.shape["tensor"]
    fine = Mesh(mesh.devices.reshape(total // 8, 2, 2, 2, cores), ("h", "l", "y", "x", "tensor"))
    dp = ("h", "l", "y", "x")
    rows = P(dp + ("tensor",), None)
    weights = P(dp, None, "tensor")
    return jax.shard_map(
        body,
        mesh=fine,
        in_specs=(rows, P(dp, None), weights, weights, P(), P(), P(), P("tensor"), rows),
        out_specs=(rows, rows, weights, weights, P(), P(), P(), P()),
        check_vma=False,
    )
```

```python
import functools

import jax
import jax.numpy as jnp
from jax import lax
from jax.experimental import pallas as pl
from jax.experimental.pallas import tpu as pltpu
from jax.sharding import Mesh, PartitionSpec as P

HEAD = 128
STRIP = 32
CAP = 50.0
BF = jnp.bfloat16
epsilon = 1e-06
PARAMS = pltpu.CompilerParams(vmem_limit_bytes=56 * 1024 * 1024)


LONG, SHORT = [pl.CostEstimate(flops=f, bytes_accessed=1, transcendentals=0) for f in (5 * 10**10, 1)]


NN, NT, TN = ((1,), (0,)), ((1,), (1,)), ((0,), (0,))


def dot(a, b, dims=NN):
    return lax.dot_general(a, b, (dims, ((), ())), preferred_element_type=jnp.float32)


def exact_dot(ones, values):
    high = values.astype(BF)
    rest = values - high.astype(jnp.float32)
    mid = rest.astype(BF)
    tail = (rest - mid.astype(jnp.float32)).astype(BF)
    return dot(ones, high) + dot(ones, mid) + dot(ones, tail)


def gates(p0, p1, floor):
    swish = jax.nn.sigmoid(p0)
    gate = jax.nn.sigmoid(p1)
    return swish, gate, floor + (1.0 - floor) * gate


def masks(seg_col, seg_row):
    length = seg_col.shape[0]
    row = lax.broadcasted_iota(jnp.int32, (length, length), 0)
    col = lax.broadcasted_iota(jnp.int32, (length, length), 1)
    same = seg_col == seg_row
    return same & (col <= row), (col <= row).astype(BF), (same & (col >= row)).astype(BF)


def strips(length):
    return [(s, -(-(s + STRIP) // 128) * 128) for s in range(0, length, STRIP)]


def fill_scores(query, key, totals, allowed, scores, kept=None):
    length = query.shape[0]
    for k, (start, wide) in enumerate(strips(length)):
        rows = slice(start, start + STRIP)
        ref = totals[start + STRIP // 2 - 1 : start + STRIP // 2]
        lead_scale = jnp.exp(totals[rows] - ref)
        trail_scale = jnp.exp(jnp.minimum(ref - totals[:wide], CAP))
        lead = (query[rows] * lead_scale).astype(BF)
        trail = (key[:wide] * trail_scale).astype(BF)
        if kept is not None:
            leads, lead_scales, trails, trail_scales = kept
            leads[rows, :], lead_scales[rows, :] = lead, lead_scale
            trails[k, :wide, :], trail_scales[k, :wide, :] = trail, trail_scale
        part = jnp.where(allowed[rows, :wide], dot(lead, trail, NT), 0.0)
        scores[rows, :wide] = part.astype(BF)
        if wide < length:
            scores[rows, wide:] = jnp.zeros((STRIP, length - wide), BF)


def head_forward(p0, p1, p2, seen, floor, gain, scores):
    swish, gate, forget = gates(p0, p1, floor)
    allowed, tri, _ = seen
    totals = exact_dot(tri, jnp.log(forget))
    fill_scores(p0 * swish, 1.0 - forget, totals, allowed, scores)
    rec = dot(scores[...], p2.astype(BF))
    rms = lax.rsqrt(jnp.mean(rec * rec, axis=-1, keepdims=True) + epsilon)
    return (rec * rms * gain).astype(BF)


def head_backward(
    p0, p1, p2, mixed_grad, seen, carry, floor, gain, scores, key_grad, decay_grad, query_grad, *kept
):
    length = p0.shape[0]
    swish, gate, forget = gates(p0, p1, floor)
    query = p0 * swish
    key = 1.0 - forget
    allowed, tri, later = seen
    totals = exact_dot(tri, jnp.log(forget))
    fill_scores(query, key, totals, allowed, scores, kept)
    value = p2.astype(BF)
    rec = dot(scores[...], value)
    rms = lax.rsqrt(jnp.mean(rec * rec, axis=-1, keepdims=True) + epsilon)
    unit = rec * rms
    scaled = mixed_grad * gain
    rec_grad = rms * (scaled - unit * jnp.mean(scaled * unit, axis=-1, keepdims=True))
    rec_low = rec_grad.astype(BF)
    value_grad = dot(scores[...], rec_low, TN).astype(BF)
    score_grad = jnp.where(allowed, dot(rec_low, value, NT), 0.0).astype(BF)
    key_grad[...] = jnp.zeros_like(key_grad)
    decay_grad[...] = jnp.zeros_like(decay_grad)
    leads, lead_scales, trails, trail_scales = kept
    for k, (start, wide) in enumerate(strips(length)):
        rows = slice(start, start + STRIP)
        lead, lead_scale = leads[rows, :], lead_scales[rows, :]
        trail, trail_scale = trails[k, :wide, :], trail_scales[k, :wide, :]
        part = score_grad[rows, :wide]
        lead_grad = dot(part, trail)
        trail_grad = dot(part, lead, TN)
        query_grad[rows, :] = lead_grad * lead_scale
        key_grad[:wide, :] += trail_grad * trail_scale
        decay_grad[:wide, :] -= trail_grad * trail.astype(jnp.float32)
        decay_grad[rows, :] += lead_grad * lead.astype(jnp.float32)
    forget_grad = exact_dot(later, decay_grad[...]) * carry / forget
    joint = forget_grad - key_grad[...]
    floor_sum = jnp.sum(joint * (1.0 - gate), axis=0, keepdims=True)
    gain_sum = jnp.sum(mixed_grad * unit, axis=0, keepdims=True)
    g0 = (query_grad[...] * swish * (1.0 + p0 * (1.0 - swish))).astype(BF)
    g1 = (joint * (1.0 - floor) * gate * (1.0 - gate)).astype(BF)
    return g0, g1, value_grad, floor_sum, gain_sum


def load_weight(offsets_ref, sources, refs, whole, sems, begin=0):
    end = begin + whole.shape[1]
    copies = []
    for (piece, low), ref in zip(sources, refs):
        rows, lanes = ref.shape[1:]
        first, last = max(low, begin), min(low + lanes, end)
        if first >= last:
            continue
        for m in range(4):
            at = pl.multiple_of(offsets_ref[4 * piece + m], rows)
            copies.append(
                pltpu.make_async_copy(
                    ref.at[m, :, pl.ds(first - low, last - first)],
                    whole.at[pl.ds(at, rows), pl.ds(first - begin, last - first)],
                    sems.at[len(copies)],
                )
            )
    for copy in copies:
        copy.start()
    for copy in copies:
        copy.wait()


def row_copies(core, refs, whole, sems):
    count = refs[0].shape[0]
    for side in range(2):
        at = pl.multiple_of((core if side == 0 else 1 - core) * count, count)
        for m in range(4):
            ref = refs[m] if side == 0 else refs[4].at[m] if m < 3 else refs[5]
            yield m, pltpu.make_async_copy(
                ref, whole.at[m, pl.ds(at, count), :], sems.at[side, m]
            )


def start_rows(core, refs, whole, sems):
    for _, copy in row_copies(core, refs, whole, sems):
        copy.start()


def wait_rows(core, refs, whole, sems, sequence):
    for m, copy in row_copies(core, refs, whole, sems):

        @pl.when(sequence == m)
        def _():
            copy.wait()


def row_scratch(count, model):
    return [pltpu.VMEM((4, 2 * count, model), BF), pltpu.SemaphoreType.DMA((2, 4))]


def store_sends(values, send_ref, last_ref):
    sequence = pl.program_id(0)

    @pl.when(sequence < 3)
    def _():
        send_ref[0] = values.astype(BF)

    @pl.when(sequence == 3)
    def _():
        last_ref[...] = values.astype(BF)


def mixer_forward_kernel(core_ref, offsets_ref, *refs, sources):
    rows, refs = refs[:6], refs[6:]
    (col_ref, row_ref, floor_ref, gain_ref, p_ref, mixed_ref, send_ref, last_ref, keep_ref, scores, whole,
     back, tokens, token_sems, weight, sems) = refs[len(sources) :]

    sequence = pl.program_id(0)

    @pl.when(sequence == 0)
    def _():
        start_rows(core_ref[0], rows, tokens, token_sems)
        load_weight(offsets_ref, sources, refs, weight, sems)

    wait_rows(core_ref[0], rows, tokens, token_sems, sequence)

    count = rows[0].shape[0]
    width = whole.shape[1]
    mine = pl.multiple_of(core_ref[0] * count, count)
    theirs = pl.multiple_of((1 - core_ref[0]) * count, count)
    p_ref[0] = dot(tokens[sequence], weight[:, : 3 * width])
    seen = masks(col_ref[0], row_ref[0])
    for h in range(width // HEAD):
        p0, p1, p2 = [p_ref[0, :, pl.ds(j * width + h * HEAD, HEAD)] for j in range(3)]
        lanes = slice(h * HEAD, (h + 1) * HEAD)
        whole[:, lanes] = head_forward(
            p0, p1, p2, seen, floor_ref[:, lanes], gain_ref[...], scores.at[h]
        )
    mixed_ref[0] = whole[...]
    back[...] = dot(whole[...], weight[:, 3 * width :], NT)
    store_sends(back[pl.ds(theirs, count), :], send_ref, last_ref)
    keep_ref[0] = back[pl.ds(mine, count), :]


def mixer_backward_kernel(core_ref, offsets_ref, *refs, sources):
    rows, refs = refs[:6], refs[6:]
    (p_ref, col_ref, row_ref, floor_ref, gain_ref, g0_ref, g1_ref, g2_ref, send_ref, last_ref, keep_ref,
     floor_sum_ref, gain_sum_ref, scores, key_grad, decay_grad, query_grad, *kept, mixed_grad, parts,
     back, tokens, token_sems, weight, sems) = refs[len(sources) :]

    sequence = pl.program_id(0)

    @pl.when(sequence == 0)
    def _():
        start_rows(core_ref[0], rows, tokens, token_sems)
        load_weight(offsets_ref, sources, refs, weight, sems)

    wait_rows(core_ref[0], rows, tokens, token_sems, sequence)

    count = rows[0].shape[0]
    width = mixed_grad.shape[1]
    mine = pl.multiple_of(core_ref[0] * count, count)
    theirs = pl.multiple_of((1 - core_ref[0]) * count, count)
    seg_col = col_ref[0]
    before = jnp.concatenate([seg_col[:1] - 1, seg_col[:-1]], axis=0)
    carry = (seg_col == before).astype(jnp.float32)
    mixed_grad[...] = dot(tokens[sequence], weight[:, 3 * width :])
    seen = masks(col_ref[0], row_ref[0])
    for h in range(width // HEAD):
        p0, p1, p2 = [p_ref[0, :, pl.ds(j * width + h * HEAD, HEAD)] for j in range(3)]
        lanes = slice(h * HEAD, (h + 1) * HEAD)
        g0, g1, g2, floor_sum, gain_sum = head_backward(
            p0, p1, p2, mixed_grad[:, lanes], seen, carry, floor_ref[:, lanes],
            gain_ref[...], scores.at[h], key_grad.at[h], decay_grad.at[h], query_grad.at[h],
            *[ref.at[h] for ref in kept],
        )
        for j, g in enumerate((g0, g1, g2)):
            parts[:, pl.ds(j * width + h * HEAD, HEAD)] = g
        floor_sum_ref[0, :, lanes] = jnp.broadcast_to(floor_sum, (8, HEAD)) * 0.125
        gain_sum_ref[0, :, lanes] = jnp.broadcast_to(gain_sum, (8, HEAD)) * 0.125

    for j, g_ref in enumerate((g0_ref, g1_ref, g2_ref)):
        g_ref[0] = parts[:, j * width : (j + 1) * width]
    back[...] = dot(parts[...], weight[:, : 3 * width], NT)
    store_sends(back[pl.ds(theirs, count), :], send_ref, last_ref)
    keep_ref[0] = back[pl.ds(mine, count), :]


def mixer_specs(count, model, width, length):
    def at(shape, index):
        return pl.BlockSpec(shape, lambda s, c, o: index(s))

    side = [
        at((1, count, model), lambda s: (jnp.minimum(s, 2), 0, 0)),
        at((count, model), lambda s: (0, 0)),
        at((1, count, model), lambda s: (s, 0, 0)),
    ]
    col = at((1, length, 1), lambda s: (s, 0, 0))
    row = at((1, 1, length), lambda s: (s, 0, 0))
    floor = at((1, width), lambda s: (0, 0))
    gain = at((1, HEAD), lambda s: (0, 0))
    wide = at((1, length, 3 * width), lambda s: (s, 0, 0))
    pair = at((1, length, width), lambda s: (s, 0, 0))
    return at, side, wide, pair, [col, row, floor, gain]


def weight_scratch(model, lanes, sources):
    return [pltpu.VMEM((model, lanes), BF), pltpu.SemaphoreType.DMA((4 * len(sources),))]


def layout_of(sources):
    return tuple((piece, low) for piece, low, _ in sources), [part for _, _, part in sources]


def mixer_forward(core, offsets, tokens, sources, segments, floor, gain):
    groups, length, _ = segments[0].shape
    count, model = tokens[0].shape
    width = floor.shape[0]
    at, side, wide, pair, small = mixer_specs(count, model, width, length)
    layout, parts = layout_of(sources)
    shape = jax.ShapeDtypeStruct
    return pl.pallas_call(
        functools.partial(mixer_forward_kernel, sources=layout),
        grid_spec=pltpu.PrefetchScalarGridSpec(
            num_scalar_prefetch=2,
            grid=(groups,),
            in_specs=[pl.BlockSpec(memory_space=pl.ANY)] * (6 + len(parts)) + small,
            out_specs=[wide, pair] + side,
            scratch_shapes=[
                pltpu.VMEM((width // HEAD, length, length), BF),
                pltpu.VMEM((length, width), BF),
                pltpu.VMEM((length, model), jnp.float32),
            ]
            + row_scratch(count, model)
            + weight_scratch(model, 4 * width, parts),
        ),
        out_shape=[
            shape((groups, length, 3 * width), jnp.float32),
            shape((groups, length, width), BF),
            shape((groups - 1, count, model), BF),
            shape((count, model), BF),
            shape((groups, count, model), jnp.float32),
        ],
        compiler_params=PARAMS,
        cost_estimate=LONG,
        name="mixer_forward",
    )(
        core, offsets, *tokens, *parts, segments[0],
        segments[1], floor[None], gain[None],
    )


def mixer_backward(core, offsets, tokens, sources, projected, segments, floor, gain):
    groups, length, _ = segments[0].shape
    count, model = tokens[0].shape
    width = floor.shape[0]
    at, side, wide, pair, small = mixer_specs(count, model, width, length)
    layout, parts = layout_of(sources)
    heads = width // HEAD
    sums = at((1, 8, width), lambda s: (s, 0, 0))
    shape = jax.ShapeDtypeStruct
    return pl.pallas_call(
        functools.partial(mixer_backward_kernel, sources=layout),
        grid_spec=pltpu.PrefetchScalarGridSpec(
            num_scalar_prefetch=2,
            grid=(groups,),
            in_specs=[pl.BlockSpec(memory_space=pl.ANY)] * (6 + len(parts))
            + [wide]
            + small,
            out_specs=[pair] * 3 + side + [sums, sums],
            scratch_shapes=[pltpu.VMEM((heads, length, length), BF)]
            + [pltpu.VMEM((heads, length, HEAD), jnp.float32)] * 3
            + [pltpu.VMEM((heads, length, HEAD), kind) for kind in (BF, jnp.float32)]
            + [
                pltpu.VMEM((heads, length // STRIP, length, HEAD), kind)
                for kind in (BF, jnp.float32)
            ]
            + [pltpu.VMEM((length, width), jnp.float32), pltpu.VMEM((length, 3 * width), BF)]
            + [pltpu.VMEM((length, model), jnp.float32)]
            + row_scratch(count, model)
            + weight_scratch(model, 4 * width, parts),
        ),
        out_shape=[
            shape((groups, length, width), BF),
            shape((groups, length, width), BF),
            shape((groups, length, width), BF),
            shape((groups - 1, count, model), BF),
            shape((count, model), BF),
            shape((groups, count, model), jnp.float32),
        ]
        + [shape((groups, 8, width), jnp.float32)] * 2,
        compiler_params=PARAMS,
        cost_estimate=LONG,
        name="mixer_backward",
    )(
        core, offsets, *tokens, *parts, projected, segments[0],
        segments[1], floor[None], gain[None],
    )


def tops_kernel(core_ref, offsets_ref, *refs, sources):
    rows, refs = refs[:6], refs[6:]
    out_ref, tokens, token_sems, weight, sems = refs[len(sources) :]
    sequence = pl.program_id(0)

    @pl.when(sequence == 0)
    def _():
        start_rows(core_ref[0], rows, tokens, token_sems)
        load_weight(offsets_ref, sources, refs, weight, sems)

    wait_rows(core_ref[0], rows, tokens, token_sems, sequence)
    out_ref[0] = dot(tokens[sequence], weight[...])


def tops_product(core, offsets, tokens, sources, width):
    count, model = tokens[0].shape
    layout, parts = layout_of(sources)
    return pl.pallas_call(
        functools.partial(tops_kernel, sources=layout),
        grid_spec=pltpu.PrefetchScalarGridSpec(
            num_scalar_prefetch=2,
            grid=(4,),
            in_specs=[pl.BlockSpec(memory_space=pl.ANY)] * (6 + len(parts)),
            out_specs=pl.BlockSpec((1, 2 * count, width), lambda s, c, o: (s, 0, 0)),
            scratch_shapes=row_scratch(count, model) + weight_scratch(model, width, parts),
        ),
        out_shape=jax.ShapeDtypeStruct((4, 2 * count, width), jnp.float32),
        compiler_params=PARAMS,
        cost_estimate=LONG,
        name="tops_product",
    )(core, offsets, *tokens, *parts)


def ffn_kernel(core_ref, offsets_ref, *refs, sources, units):
    rows, active_grad_ref, refs = refs[:6], refs[6], refs[7:]
    (*parts, send_ref, last_ref, keep_ref, grads, back,
     tokens, token_sems, weight, sems) = refs[len(sources) :]
    sequence = pl.program_id(0)

    @pl.when(sequence == 0)
    def _():
        start_rows(core_ref[0], rows, tokens, token_sems)
        load_weight(offsets_ref, sources, refs, weight, sems, grads.shape[1] - 2 * units)

    wait_rows(core_ref[0], rows, tokens, token_sems, sequence)
    width = units
    count = rows[0].shape[0]
    mine = pl.multiple_of(core_ref[0] * count, count)
    theirs = pl.multiple_of((1 - core_ref[0]) * count, count)
    both = dot(tokens[sequence], weight[...])
    gate, up = both[:, :width], both[:, width:]
    active_grad = active_grad_ref[0, :, :width]
    squash = jax.nn.sigmoid(gate)
    swish = gate * squash
    gate_grad = active_grad * up * squash * (1.0 + gate * (1.0 - squash))
    grads[:, : 2 * width] = jnp.concatenate([gate_grad, active_grad * swish], axis=1).astype(BF)
    spare = jnp.zeros((2 * count, grads.shape[1] - 3 * width), BF)
    grads[:, 2 * width :] = jnp.concatenate([(swish * up).astype(BF), spare], axis=1)
    low = 0
    for part_ref in parts:
        part_ref[0] = grads[:, low : low + part_ref.shape[2]]
        low += part_ref.shape[2]
    back[...] = dot(grads[:, : 2 * width], weight[...], NT)
    store_sends(back[pl.ds(theirs, count), :], send_ref, last_ref)
    keep_ref[0] = back[pl.ds(mine, count), :]


def ffn(core, offsets, tokens, active_grad, sources, width, widths):
    count, model = tokens[0].shape
    groups, length = 4, 2 * count
    total = sum(widths)
    layout, parts = layout_of(sources)

    def at(rows, lanes):
        return pl.BlockSpec((1, rows, lanes), lambda s, c, o: (s, 0, 0))

    shape = jax.ShapeDtypeStruct
    return pl.pallas_call(
        functools.partial(ffn_kernel, sources=layout, units=width),
        grid_spec=pltpu.PrefetchScalarGridSpec(
            num_scalar_prefetch=2,
            grid=(groups,),
            in_specs=[pl.BlockSpec(memory_space=pl.ANY)] * 6
            + [at(length, active_grad.shape[2])]
            + [pl.BlockSpec(memory_space=pl.ANY)] * len(parts),
            out_specs=[at(length, n) for n in widths]
            + [
                pl.BlockSpec((1, count, model), lambda s, c, o: (jnp.minimum(s, 2), 0, 0)),
                pl.BlockSpec((count, model), lambda s, c, o: (0, 0)),
                at(count, model),
            ],
            scratch_shapes=[
                pltpu.VMEM((length, total), BF),
                pltpu.VMEM((length, model), jnp.float32),
            ]
            + row_scratch(count, model)
            + weight_scratch(model, 2 * width, parts),
        ),
        out_shape=[
            *[shape((groups, length, n), BF) for n in widths],
            shape((groups - 1, count, model), BF),
            shape((count, model), BF),
            shape((groups, count, model), jnp.float32),
        ],
        compiler_params=PARAMS,
        cost_estimate=LONG,
        name="ffn",
    )(core, offsets, *tokens, active_grad, *parts)


def rows_kernel(core_ref, offsets_ref, *refs, sources, begin, number):
    own, refs = refs[:number], refs[number:]
    out_ref, whole, sems = refs[len(sources) :]

    @pl.when(pl.program_id(0) == 0)
    def _():
        load_weight(offsets_ref, sources, refs, whole, sems, begin)

    out_ref[0] = dot(jnp.concatenate([r[0] for r in own], axis=1), whole[...], NT).astype(BF)


def rows_product(core, offsets, own, sources, begin, model, estimate=SHORT):
    groups, length, _ = own[0].shape
    width = sum(o.shape[2] for o in own)
    layout, parts = layout_of(sources)

    def at(rows, lanes):
        return pl.BlockSpec((1, rows, lanes), lambda s, c, o: (s, 0, 0))

    shape = jax.ShapeDtypeStruct
    return pl.pallas_call(
        functools.partial(rows_kernel, sources=layout, begin=begin, number=len(own)),
        grid_spec=pltpu.PrefetchScalarGridSpec(
            num_scalar_prefetch=2,
            grid=(groups,),
            in_specs=[at(length, o.shape[2]) for o in own] + [pl.BlockSpec(memory_space=pl.ANY)] * len(parts),
            out_specs=pl.BlockSpec((1, length, model), lambda s, c, o: (s ^ c[1], 0, 0)),
            scratch_shapes=weight_scratch(model, width, parts),
        ),
        out_shape=shape((groups, length, model), BF),
        compiler_params=PARAMS,
        cost_estimate=estimate,
        name="rows_product",
    )(core, offsets, *own, *parts)


def grad_kernel(core_ref, blocks_ref, *refs, number):
    rows, grads, outs, tokens = refs[:6], refs[6 : 6 + number], refs[6 + number : -1], refs[-1]
    count = rows[0].shape[0]
    for side in range(2):
        at = core_ref[0] if side == 0 else 1 - core_ref[0]
        for m in range(4):
            first = pl.multiple_of((2 * m + at) * count, count)
            part = rows[m][...] if side == 0 else rows[4][m] if m < 3 else rows[5][...]
            tokens[pl.ds(first, count), :] = part
    for grad_ref, out_ref in zip(grads, outs):
        out_ref[0] = dot(tokens[...], grad_ref[...], TN).astype(out_ref.dtype)


def grad_product(core, tokens, grads, blocks, wide, kind, estimate):
    count, model = tokens[0].shape
    side = pl.BlockSpec((count, wide), lambda i, c, b: (0, b[i]))
    three = pl.BlockSpec((3, count, wide), lambda i, c, b: (0, 0, b[i]))
    number = blocks.shape[0]
    return pl.pallas_call(
        functools.partial(grad_kernel, number=len(grads)),
        grid_spec=pltpu.PrefetchScalarGridSpec(
            num_scalar_prefetch=2,
            grid=(number,),
            in_specs=[side] * 4
            + [three, side]
            + [pl.BlockSpec(g.shape, lambda i, c, b: (0, 0)) for g in grads],
            out_specs=[pl.BlockSpec((1, wide, g.shape[1]), lambda i, c, b: (i, 0, 0)) for g in grads],
            scratch_shapes=[pltpu.VMEM((8 * count, wide), BF)],
        ),
        out_shape=[jax.ShapeDtypeStruct((number, wide, g.shape[1]), kind) for g in grads],
        compiler_params=PARAMS,
        cost_estimate=estimate,
        name="grad_product",
    )(core, blocks, *tokens, *grads)


def rms_of(values):
    return lax.rsqrt(jnp.mean(values * values, axis=-1, keepdims=True) + epsilon)


def last_kernel(keep_ref, came_ref, out_ref):
    out_ref[...] = (keep_ref[0] + came_ref[...].astype(jnp.float32)).astype(BF)


def add_last(keep, came):
    count, model = came.shape
    block = count // 2
    return pl.pallas_call(
        last_kernel,
        grid=(2,),
        in_specs=[
            pl.BlockSpec((1, block, model), lambda i: (3, i, 0)),
            pl.BlockSpec((block, model), lambda i: (i, 0)),
        ],
        out_specs=pl.BlockSpec((block, model), lambda i: (i, 0)),
        out_shape=jax.ShapeDtypeStruct(came.shape, BF),
        compiler_params=PARAMS,
        cost_estimate=SHORT,
        name="add_last",
    )(keep, came)


def cores_kernel(keep_ref, came_ref, own_ref, x_ref, z_ref):
    own_ref[...] = keep_ref[0] + came_ref[0].astype(jnp.float32)
    for m, out_ref in enumerate((x_ref, z_ref), 1):
        out_ref[...] = (keep_ref[m] + came_ref[m].astype(jnp.float32)).astype(BF)


def add_cores(keep, came):
    count, model = keep.shape[1:]
    block = count // 2
    three = pl.BlockSpec((3, block, model), lambda i: (0, i, 0))
    one = pl.BlockSpec((block, model), lambda i: (i, 0))
    shape = jax.ShapeDtypeStruct
    return pl.pallas_call(
        cores_kernel,
        grid=(2,),
        in_specs=[three, three],
        out_specs=[one] * 3,
        out_shape=[shape((count, model), jnp.float32)] + [shape((count, model), BF)] * 2,
        compiler_params=PARAMS,
        cost_estimate=SHORT,
        name="add_cores",
    )(keep, came)


def middle_kernel(own_ref, x_ref, z_ref, hidden_ref, gain_ref, middle_ref, normed_ref):
    branch = own_ref[...] + x_ref[...].astype(jnp.float32) + z_ref[...].astype(jnp.float32)
    middle = hidden_ref[...].astype(jnp.float32) + branch
    middle_ref[...] = middle
    normed_ref[...] = (middle * rms_of(middle) * gain_ref[...]).astype(BF)


def back_kernel(own_ref, x_ref, z_ref, values_ref, add_ref, gain_ref, out_ref, low_ref, sum_ref):
    grad = own_ref[...] + x_ref[...].astype(jnp.float32) + z_ref[...].astype(jnp.float32)
    values = values_ref[...].astype(jnp.float32)
    scale = rms_of(values)
    unit = values * scale
    wide = grad * gain_ref[...]
    inner = wide - unit * jnp.mean(wide * unit, axis=-1, keepdims=True)
    out = add_ref[...].astype(jnp.float32) + scale * inner
    out_ref[...] = out
    low_ref[...] = out.astype(BF)

    @pl.when(pl.program_id(0) == 0)
    def _():
        sum_ref[...] = jnp.zeros_like(sum_ref)

    sum_ref[...] += jnp.sum(grad * unit, axis=0, keepdims=True)


def row_call(kernel, name, kinds, *args):
    count, model = args[0].shape
    block = count // 2

    def spec(one):
        if one:
            return pl.BlockSpec((1, model), lambda i: (0, 0))
        return pl.BlockSpec((block, model), lambda i: (i, 0))

    shapes = [jax.ShapeDtypeStruct((1 if k is None else count, model), k or jnp.float32) for k in kinds]
    return pl.pallas_call(
        kernel,
        grid=(2,),
        in_specs=[spec(a.shape[0] == 1) for a in args],
        out_specs=[spec(k is None) for k in kinds],
        out_shape=shapes,
        compiler_params=PARAMS,
        cost_estimate=LONG,
        name=name,
    )(*args)


def mix_grad_kernel(parts_ref, out_ref):
    quarter = parts_ref.shape[2] // 4
    for j, at in enumerate((1, 3, 0, 2)):
        for m in range(4):
            part = parts_ref[m, :, at * quarter : (at + 1) * quarter]
            out_ref[:, j, m * quarter : (m + 1) * quarter] = part.astype(jnp.float32)


def mix_grad_of(parts):
    _, rows, wide = parts.shape
    block = min(rows, 64)
    return pl.pallas_call(
        mix_grad_kernel,
        grid=(rows // block,),
        in_specs=[pl.BlockSpec((4, block, wide), lambda i: (0, i, 0))],
        out_specs=pl.BlockSpec((block, 4, wide), lambda i: (i, 0, 0)),
        out_shape=jax.ShapeDtypeStruct((rows, 4, wide), jnp.float32),
        compiler_params=PARAMS,
        cost_estimate=SHORT,
        name="mix_grad",
    )(parts)


DOWN_FIRST = 256


def ffn_grad_kernel(first_ref, second_ref, out_ref):
    units = out_ref.shape[2] // 4
    for j in range(3):
        parts = []
        for m in range(4):
            down = first_ref.shape[2] - DOWN_FIRST
            gates = jnp.concatenate([first_ref[m, :, down:], second_ref[m]], axis=1)
            parts.append(first_ref[m, :, :units] if j == 2 else gates[:, j * units : (j + 1) * units])
        out_ref[j] = jnp.concatenate(parts, axis=1).astype(jnp.float32)


def ffn_grad_of(parts, units):
    rows = parts[0].shape[1]
    block = min(rows, 32)
    out = pl.pallas_call(
        ffn_grad_kernel,
        grid=(rows // block,),
        in_specs=[pl.BlockSpec((4, block, p.shape[2]), lambda i: (0, i, 0)) for p in parts],
        out_specs=pl.BlockSpec((3, block, 4 * units), lambda i: (0, i, 0)),
        out_shape=jax.ShapeDtypeStruct((3, rows, 4 * units), jnp.float32),
        compiler_params=PARAMS,
        cost_estimate=LONG,
        name="ffn_grad",
    )(*parts)
    return out.transpose(1, 0, 2)


def near_kernel(*refs, number):
    home_ref, away_ref = refs[2 * number :]
    at_home = pl.program_id(0) == pl.num_programs(0) - 1
    low = 0
    for keep_ref, came_ref in zip(refs[: 2 * number : 2], refs[1 : 2 * number : 2]):
        lanes = slice(low, low + keep_ref.shape[2])
        low += keep_ref.shape[2]

        @pl.when(jnp.logical_not(at_home))
        def _():
            total = keep_ref[...] + came_ref[...].astype(jnp.float32)
            away_ref[:, :, lanes] = total.astype(BF)

        @pl.when(at_home)
        def _():
            home_ref[:, :, lanes] = keep_ref[...] + came_ref[...].astype(jnp.float32)


def near_sums(pairs, estimate=SHORT):
    highs = lax.axis_size("h")
    blocks, rows, _ = pairs[0][0].shape
    wide = sum(keep.shape[2] for keep, _ in pairs)
    specs, args = [], []
    for pair in pairs:
        specs += [pl.BlockSpec((2,) + pair[0].shape[1:], lambda i: (i, 0, 0))] * 2
        args += list(pair)
    home, away = pl.pallas_call(
        functools.partial(near_kernel, number=len(pairs)),
        grid=(highs,),
        in_specs=specs,
        out_specs=[
            pl.BlockSpec((2, rows, wide), lambda i: (0, 0, 0)),
            pl.BlockSpec((2, rows, wide), lambda i: (jnp.minimum(i, highs - 2), 0, 0)),
        ],
        out_shape=[
            jax.ShapeDtypeStruct((2, rows, wide), jnp.float32),
            jax.ShapeDtypeStruct((blocks - 2, rows, wide), BF),
        ],
        compiler_params=PARAMS,
        cost_estimate=estimate,
        name="near_sums",
    )(*args)
    return home, [away[2 * k : 2 * k + 2] for k in range(highs - 1)]


def far_kernel(*refs, counts):
    out_ref = refs[-1]
    low, at = 0, 0
    for count in counts:
        total = refs[at][0]
        for ref in refs[at + 1 : at + 1 + count]:
            total = total + ref[0].astype(jnp.float32)
        out_ref[0, :, low : low + total.shape[1]] = total.astype(BF)
        low, at = low + total.shape[1], at + 1 + count


def far_sums(pairs, estimate=SHORT):
    _, rows, _ = pairs[0][0].shape
    wide = sum(home.shape[2] for home, _ in pairs)
    args = [part for home, fars in pairs for part in (home, *fars)]
    out = pl.pallas_call(
        functools.partial(far_kernel, counts=[len(fars) for _, fars in pairs]),
        grid=(2,),
        in_specs=[pl.BlockSpec((1,) + a.shape[1:], lambda i: (i, 0, 0)) for a in args],
        out_specs=pl.BlockSpec((1, rows, wide), lambda i: (i, 0, 0)),
        out_shape=jax.ShapeDtypeStruct((2, rows, wide), BF),
        compiler_params=PARAMS,
        cost_estimate=estimate,
        name="far_sums",
    )(*args)
    return out.reshape(4, rows // 2, wide)


GROUP = ("l", "x")


def swap(values, axes):
    total = 2 ** len(axes)
    return lax.ppermute(values, axes, [(s, total - 1 - s) for s in range(total)])


def shift(values, steps):
    total = lax.axis_size("h")
    return lax.ppermute(values, "h", [(s, (s + steps) % total) for s in range(total)])


def pick(values, index):
    return lax.dynamic_index_in_dim(values, index, 0, keepdims=False)


def over_c(values):
    return swap(values, ("tensor",))


def over_x(values):
    return swap(values, ("x",))


def over_y(values):
    return swap(values, ("y",))


def over_z(values):
    return swap(values, ("l",))


def own_member():
    return lax.axis_index("l") * 2 + lax.axis_index("x")


def source_rows(rows):
    y, high = lax.axis_index("y"), lax.axis_index("h")
    highs = lax.axis_size("h")
    starts = []
    for k in range(highs):
        for side in (y, 1 - y):
            for member in range(4):
                block = ((high - k) % highs) * 8 + (member >> 1) * 4 + side * 2 + (member & 1)
                starts.append(block * rows)
    return jnp.stack(starts).astype(jnp.int32)


def trade(slices):
    return lax.all_to_all(slices, GROUP, 0, 0, tiled=True)


def after(values, *others):
    return lax.optimization_barrier((values, others))[0]


def far(block):
    return [shift(block, k) for k in range(1, lax.axis_size("h"))]


def near(parts):
    return [over_y(part) for part in parts]


def pieces(low, straight, crossed):
    out = []
    for k, (one, two) in enumerate(zip(straight, crossed), 1):
        out += [(2 * k, low, one), (2 * k + 1, low, two)]
    return out


def half_grads(core, tokens, grads, yy, kind, estimate):
    highs, high = lax.axis_size("h"), lax.axis_index("h")
    wide = tokens[0].shape[1] // (4 * highs)
    order = [(high + k) % highs for k in range(1, highs)] + [high]
    blocks = jnp.stack([(h * 2 + z) * 2 + yy for h in order for z in range(2)]).astype(jnp.int32)
    grads = [flat(g) for g in grads]
    if wide % 128 == 0:
        return grad_product(core, tokens, grads, blocks, wide, kind, estimate)
    sides = [jnp.stack(tokens[:4]), jnp.concatenate([tokens[4], tokens[5][None]])]
    ordered = [jnp.where(core[0] == 0, a, b) for a, b in (sides, sides[::-1])]
    whole = jnp.stack(ordered, axis=1)
    split = jnp.take(whole.reshape(grads[0].shape[0], -1, wide), blocks, axis=1)
    return [
        jnp.einsum("tad,tx->adx", split, g, preferred_element_type=jnp.float32).astype(kind)
        for g in grads
    ]


def grad_sends(core, tokens, grads, estimate=SHORT):
    return half_grads(core, tokens, grads, 1 - lax.axis_index("y"), BF, estimate)


def grad_keeps(core, tokens, grads, estimate=SHORT):
    return half_grads(core, tokens, grads, lax.axis_index("y"), jnp.float32, estimate)


def send_far(away):
    return [shift(part, k) for k, part in enumerate(away, 1)]


def flat(values):
    return values.reshape(-1, values.shape[-1])


def add_low(keep, came):
    return (keep.astype(jnp.float32) + came.astype(jnp.float32)).astype(BF)


def sum_pair(values, first, second):
    parts = [values, swap(values, (second,)), swap(values, (first,)), swap(values, (first, second))]
    return jnp.stack(parts), lax.axis_index(first) * 2 + lax.axis_index(second)


def add_pair(parts, place):
    return sum(pick(parts, place ^ m) for m in range(4))


def sum_highs(values):
    size, bits = lax.axis_size("h"), 1
    while bits < size:
        values = values + lax.ppermute(values, "h", [(s, s ^ bits) for s in range(size)])
        bits *= 2
    return values


def body(
    hidden_in,
    segments,
    mix_weights,
    ffn_weights,
    norm1_gain,
    norm2_gain,
    head_gain,
    lower_bound,
    out_grad,
):
    core, member = lax.axis_index("tensor"), own_member()
    core_at = jnp.stack([core, member]).astype(jnp.int32)
    rows = mix_weights.shape[0]
    offsets = source_rows(rows)
    quarter, units = lower_bound.shape[0] // 4, ffn_weights.shape[2] // 4
    model = hidden_in.shape[1]
    channels = 4 * quarter
    lanes = -(-3 * units // 128) * 128

    def slices(weights, width):
        split = weights.reshape(rows, weights.shape[1], 4, -1).transpose(2, 0, 1, 3)
        split = split.reshape(4, rows, -1)
        return jnp.pad(split, ((0, 0), (0, 0), (0, width - split.shape[2])))

    length = segments.shape[1]
    labels = jnp.pad(segments.astype(BF), ((0, 15), (0, channels - length)))
    labels = jnp.broadcast_to(labels, (4,) + labels.shape)
    hidden = hidden_in.astype(jnp.float32)
    scale_one = rms_of(hidden)
    normed = (hidden * scale_one * norm1_gain).astype(BF)
    floor = lax.dynamic_slice_in_dim(lower_bound, member * quarter, quarter)
    feed = slices(ffn_weights, 3 * units)
    spare = lanes - 3 * units
    down = jnp.pad(feed[..., 2 * units :], ((0, 0), (0, 0), (0, spare)))
    feed = jnp.concatenate([down, feed[..., : 2 * units]], axis=-1)
    mix = slices(mix_weights, channels)

    mix = trade(jnp.concatenate([slices(mix_weights, channels), labels], axis=1))

    gate = (mix, normed, feed)
    mix, normed, feed = lax.optimization_barrier(gate)
    labels = mix[:, rows, :length].astype(jnp.int32)
    labels = jnp.stack([pick(labels, member ^ m) for m in range(4)])
    mix = mix[:, :rows]
    cuts = [0, 512, 1024, 1152, 1408, 1664, 1920, lanes]
    feed_cut = cuts[4]
    mix_far = far(mix)
    mix_near = over_y(mix)
    feed_one = trade(feed[..., :feed_cut])
    feed_rest = after(feed[..., feed_cut:], gate)
    normed_x, normed_z = over_x(normed), over_z(normed)
    top_x = over_x(after(out_grad, gate))

    columns = jnp.broadcast_to(labels[:, :, None], labels.shape + (1,))
    gate = (mix_far, mix_near, feed_one, feed_rest, normed_x, normed_z, top_x, floor, columns)
    floor = after(floor, gate)
    labels = (after(columns, gate), labels[:, None, :])
    mix_cross = near(after(mix_far, gate))
    ones = [feed_one[..., low:high] for low, high in zip(cuts[:4], cuts[1:5])]
    far_a = far(after(ones[0], gate))
    normed_xz = over_x(after(normed_z, gate))
    normed_three = jnp.stack(after([normed, normed_x, normed_z], gate))
    top_z = over_z(after(out_grad, gate))
    near_a = over_y(after(feed_one[..., :256], gate))

    gate = (mix_cross, far_a, normed_xz, normed_three, top_z, ones, near_a)
    normed_c, normed_cxz = over_c(after(normed_three, gate)), over_c(after(normed_xz, gate))
    normed = [normed, normed_x, normed_z, normed_xz, normed_c, normed_cxz]
    mix_sources = [(0, 0, mix), (1, 0, mix_near)] + pieces(0, mix_far, mix_cross)

    gate = (normed_c, normed_cxz)
    far_b = far(after(ones[1], gate))
    near_b = over_y(after(feed_one[..., 256:768], gate))
    cross_a = near(after(far_a, gate))
    top_xz = over_x(after(top_z, gate))
    feed_two = trade(after(feed_rest, gate))
    projected, mixed, send, send_xz, keep = mixer_forward(
        core_at, offsets, after(normed, gate), mix_sources, labels, floor, head_gain
    )

    gate = (send, far_b, near_b, cross_a, top_xz, feed_two)
    came_xz = over_c(after(send_xz, gate))
    came = over_c(after(send, gate))
    near_c = over_y(after(feed_one[..., 768:1024], gate))
    top_cxz = over_c(after(top_xz, gate))
    top_three = jnp.stack(after([out_grad, top_x, top_z], gate))
    far_c = far(after(ones[2], gate))
    to_xz = add_last(keep, came_xz)

    gate = (to_xz, near_c, far_c, top_cxz, top_three)
    from_x = over_x(after(to_xz, gate))
    far_d = far(after(ones[3], gate))
    cross_b = near(after(far_b, gate))
    own, to_x, to_z = add_cores(keep, after(came, gate))
    top_c = over_c(after(top_three, gate))
    tops = [out_grad, top_x, top_z, top_xz, top_c, top_cxz]

    gate = (from_x, far_d, cross_b, own, top_c)
    to_z = add_low(to_z, after(from_x, gate))
    of_x = over_x(after(to_x, gate))
    of_z = over_z(to_z)
    far_e = far(after(feed_two[..., : cuts[5] - feed_cut], gate))
    near_d = over_y(after(feed_one[..., 1024:], gate))
    near_e = over_y(after(feed_two[..., :384], gate))

    gate = (of_x, of_z, far_e, near_d, near_e)
    far_f = far(after(feed_two[..., cuts[5] - feed_cut : cuts[6] - feed_cut], gate))
    near_f = over_y(after(feed_two[..., 384:], gate))
    cross_cd = [
        over_y(jnp.concatenate([one, two], axis=-1))
        for one, two in zip(after(far_c, gate), after(far_d, gate))
    ]
    middle, normed_two = row_call(
        middle_kernel, "middle", [jnp.float32, BF], *after((own, of_x, of_z), gate), hidden_in,
        norm2_gain[None],
    )
    two_x, two_z = over_x(normed_two), over_z(normed_two)
    down_sources = [(0, 0, feed_one), (1, 0, near_a), (1, 256, near_b)]
    for low, straight, crossed in zip(cuts, [far_a, far_b], [cross_a, cross_b]):
        down_sources += pieces(low, straight, crossed)
    active_grad = tops_product(
        core_at, offsets, after(tops, normed_two), down_sources, lanes - 2 * units
    )

    gate = (far_f, near_f, cross_cd, two_x, two_z, active_grad)
    far_g = far(after(feed_two[..., cuts[6] - feed_cut :], gate))
    cross_e, cross_f = near(after(far_e, gate)), near(after(far_f, gate))
    two_xz = over_x(after(two_z, gate))
    two_three = jnp.stack(after([normed_two, two_x, two_z], gate))

    gate = (far_g, cross_e, cross_f, two_xz, two_three)
    cross_g = near(after(far_g, gate))
    two_c, two_cxz = over_c(after(two_three, gate)), over_c(after(two_xz, gate))
    normed_two = [normed_two, two_x, two_z, two_xz, two_c, two_cxz]
    feed_sources = [(0, 0, feed_one), (0, feed_cut, feed_two)]
    feed_sources += [(1, 0, near_a), (1, 256, near_b), (1, 768, near_c), (1, 1024, near_d)]
    feed_sources += [(1, feed_cut, near_e), (1, feed_cut + 384, near_f)]
    fars = [far_a, far_b, far_c, far_d, far_e, far_f, far_g]
    for low, part in zip(cuts, fars):
        feed_sources += [(2 * k, low, one) for k, one in enumerate(part, 1)]
    crosses = [cross_a, cross_b, cross_cd, cross_e, cross_f, cross_g]
    for low, part in zip(cuts[:3] + cuts[4:], crosses):
        feed_sources += [(2 * k + 1, low, one) for k, one in enumerate(part, 1)]

    widths = [256, 128, 384, 256, 256, 128, 256, 256, lanes - 1920]
    *grads, send, send_xz, keep = ffn(
        core_at, offsets, normed_two, active_grad, feed_sources, units, widths
    )
    gates, downs = grads[:6], grads[6:]
    came_xz, came = over_c(send_xz), over_c(send)
    down_sends = grad_sends(core_at, after(tops, send), downs, LONG)
    to_xz = add_last(keep, after(came_xz, down_sends))

    gate = (to_xz,)
    from_x = over_x(after(to_xz, gate))
    down_one = over_y(after(down_sends[0], gate))
    gate_sends = grad_sends(core_at, after(normed_two, gate), gates, LONG)
    own, to_x, to_z = add_cores(keep, after(came, gate_sends))

    gate = (from_x, down_one, own)
    to_z = add_low(to_z, after(from_x, gate))
    of_x = over_x(after(to_x, gate))
    of_z = over_z(to_z)
    down_two = over_y(after(down_sends[1], gate))
    down_keeps = grad_keeps(core_at, after(tops, gate), downs, LONG)
    down_home, down_away = near_sums([(down_keeps[0], after(down_one, gate))])

    gate = (of_x, of_z, down_two, down_away)
    down_fars = send_far(after(down_away, gate))
    down_three = over_y(after(down_sends[2], gate))
    two_came = over_y(after(gate_sends[1], gate))
    middle_grad, middle_low, gain_two_grad = row_call(
        back_kernel, "middle_grad", [jnp.float32, BF, None], *after((own, of_x, of_z), gate),
        middle, out_grad, norm2_gain[None],
    )
    grad_x, grad_z = over_x(middle_low), over_z(middle_low)
    gate_keeps = grad_keeps(core_at, after(normed_two, middle_low), gates, LONG)
    down_home_two, down_away_two = near_sums(
        [(after(down_keeps[1], gate_keeps), after(down_two, gate))]
    )

    gate = (grad_x, grad_z, down_three, two_came, down_away_two, down_fars)
    down_fars_two = send_far(after(down_away_two, gate))
    one_came = over_y(after(gate_sends[0], gate))
    grad_xz = over_x(after(grad_z, gate))
    grad_three = jnp.stack(after([middle_low, grad_x, grad_z], gate))
    branch = rows_product(
        core_at, offsets, after(downs, gate), down_sources, 0, model, LONG
    )

    gate = early = (grad_xz, grad_three, branch, down_fars_two, one_came)
    grad_c, grad_cxz = over_c(after(grad_three, gate)), over_c(after(grad_xz, gate))
    one_home, one_away = near_sums(
        [
            (down_keeps[2], after(down_three, gate)),
            (gate_keeps[0], after(one_came, gate)),
        ],
        LONG,
    )
    middle_full = [middle_low, grad_x, grad_z, grad_xz, grad_c, grad_cxz]

    gate = (grad_c, grad_cxz, one_away)
    one_fars = send_far(after(one_away, gate))
    three_came, four_came = [over_y(after(part, early)) for part in gate_sends[2:4]]
    branch = lax.psum_scatter(
        after(branch, gate).reshape(-1, model), GROUP + ("tensor",), scatter_dimension=0, tiled=True
    )
    middle_full = after(middle_full, gate)
    *mix_grads, send, send_xz, keep, floor_sums, gain_sums = mixer_backward(
        core_at, offsets, middle_full, mix_sources, projected, labels, floor, head_gain
    )

    gate = (send, one_fars, three_came, four_came)
    came_xz, came = over_c(after(send_xz, gate)), over_c(after(send, gate))
    five_came = over_y(after(gate_sends[4], gate))
    three_home, three_away = near_sums(
        [(gate_keeps[1], after(two_came, gate)), (gate_keeps[2], three_came)], LONG
    )
    to_xz = add_last(keep, after(came_xz, three_away))

    gate = (to_xz,)
    three_fars = send_far(after(three_away, gate))
    from_x = over_x(after(to_xz, gate))
    six_came = over_y(after(gate_sends[5], gate))
    query_send, forget_send, value_send = grad_sends(core_at, after(normed, gate), mix_grads, LONG)
    own, to_x, to_z = add_cores(keep, after(came, value_send))
    four_home, four_away = near_sums(
        [
            (gate_keeps[3], after(four_came, own)),
            (gate_keeps[4], five_came),
            (gate_keeps[5], six_came),
        ]
    )

    gate = (from_x, three_fars, four_away)
    four_fars = send_far(after(four_away, gate))
    to_z = add_low(to_z, after(from_x, gate))
    of_x = over_x(after(to_x, gate))
    of_z = over_z(to_z)
    value_came, query_came = over_y(after(value_send, gate)), over_y(after(query_send, gate))
    query_keep, forget_keep, value_keep = grad_keeps(core_at, after(normed, gate), mix_grads, LONG)
    (last_send,) = grad_sends(core_at, after(middle_full, value_keep), [mixed])
    down_parts = [(down_home, down_fars), (down_home_two, down_fars_two), (one_home, one_fars)]
    down_parts = far_sums(after(down_parts, last_send))
    near_home, near_away = near_sums(
        [(value_keep, after(value_came, down_parts)), (query_keep, query_came)]
    )

    gate = (of_x, of_z, four_fars, near_away)
    near_fars = send_far(after(near_away, gate))
    last_came, forget_came = over_y(after(last_send, gate)), over_y(after(forget_send, gate))
    down_parts = trade(after(down_parts, gate))
    input_grad, _, gain_one_grad = row_call(
        back_kernel, "input_grad", [jnp.float32, BF, None], *after((own, of_x, of_z), gate),
        hidden_in, middle_grad, norm1_gain[None],
    )
    (last_keep,) = grad_keeps(core_at, after(middle_full, input_grad), [mixed])
    head_grad = jnp.sum(after(gain_sums, gate).reshape(-1, HEAD), axis=0)
    lower_grad = jnp.zeros((2, 4, quarter), jnp.float32)
    lower_grad = lax.dynamic_update_slice(
        lower_grad,
        jnp.sum(after(floor_sums, gate), axis=(0, 1)).reshape(1, 1, quarter),
        (core, member, 0),
    )
    sums = [gain_one_grad[0], gain_two_grad[0], head_grad, lower_grad.reshape(-1)]
    sums = jnp.concatenate(sums).reshape(-1, HEAD)
    block_out = (middle + after(branch, last_keep).astype(jnp.float32)).astype(BF)
    gate_parts = [(three_home, three_fars), (four_home, four_fars)]
    gate_parts = far_sums(after(gate_parts, block_out))
    pair_home, pair_away = near_sums(
        [(last_keep, after(last_came, gate_parts)), (forget_keep, forget_came)]
    )

    gate = (near_fars, down_parts, sums, pair_away, gate_parts, block_out)
    pair_fars = send_far(after(pair_away, gate))
    gate_parts = trade(after(gate_parts, gate))
    sums, place = sum_pair(after(sums, gate), "l", "x")

    gate = (pair_fars, gate_parts, sums)
    mix_parts = far_sums(after([(near_home, near_fars), (pair_home, pair_fars)], gate))
    sums, place = sum_pair(add_pair(after(sums, mix_parts), place), "y", "tensor")
    sums = sum_highs(add_pair(sums, place)).reshape(-1)
    mix_parts = trade(mix_parts)
    gain_one, gain_two, head, lower = jnp.split(sums, [model, 2 * model, 2 * model + HEAD])
    ffn_grad = ffn_grad_of(after([down_parts, gate_parts], gate), units)
    mix_grad = mix_grad_of(mix_parts)
    return (block_out, input_grad, mix_grad, ffn_grad, gain_one, gain_two, head, lower)


def solution(mesh):
    total, cores = mesh.shape["dp"], mesh.shape["tensor"]
    fine = Mesh(mesh.devices.reshape(total // 8, 2, 2, 2, cores), ("h", "l", "y", "x", "tensor"))
    dp = ("h", "l", "y", "x")
    rows = P(dp + ("tensor",), None)
    weights = P(dp, None, "tensor")
    return jax.shard_map(
        body,
        mesh=fine,
        in_specs=(rows, P(dp, None), weights, weights, P(), P(), P(), P("tensor"), rows),
        out_specs=(rows, rows, weights, weights, P(), P(), P(), P()),
        check_vma=False,
    )
```

```python
import functools

import jax
import jax.numpy as jnp
from jax import lax
from jax.experimental import pallas as pl
from jax.experimental.pallas import tpu as pltpu
from jax.sharding import Mesh, PartitionSpec as P

HEAD = 128
STRIP = 32
CAP = 50.0
BF = jnp.bfloat16
epsilon = 1e-06
PARAMS = pltpu.CompilerParams(vmem_limit_bytes=56 * 1024 * 1024)


LONG, SHORT = [pl.CostEstimate(flops=f, bytes_accessed=1, transcendentals=0) for f in (5 * 10**10, 1)]


NN, NT, TN = ((1,), (0,)), ((1,), (1,)), ((0,), (0,))


def dot(a, b, dims=NN):
    return lax.dot_general(a, b, (dims, ((), ())), preferred_element_type=jnp.float32)


def exact_dot(ones, values):
    high = values.astype(BF)
    rest = values - high.astype(jnp.float32)
    mid = rest.astype(BF)
    tail = (rest - mid.astype(jnp.float32)).astype(BF)
    return dot(ones, high) + dot(ones, mid) + dot(ones, tail)


def gates(p0, p1, floor):
    swish = jax.nn.sigmoid(p0)
    gate = jax.nn.sigmoid(p1)
    return swish, gate, floor + (1.0 - floor) * gate


def masks(seg_col, seg_row):
    length = seg_col.shape[0]
    row = lax.broadcasted_iota(jnp.int32, (length, length), 0)
    col = lax.broadcasted_iota(jnp.int32, (length, length), 1)
    same = seg_col == seg_row
    return same & (col <= row), (col <= row).astype(BF), (same & (col >= row)).astype(BF)


def strips(length):
    return [(s, -(-(s + STRIP) // 128) * 128) for s in range(0, length, STRIP)]


def fill_scores(query, key, totals, allowed, scores, kept=None):
    length = query.shape[0]
    for k, (start, wide) in enumerate(strips(length)):
        rows = slice(start, start + STRIP)
        ref = totals[start + STRIP // 2 - 1 : start + STRIP // 2]
        lead_scale = jnp.exp(totals[rows] - ref)
        trail_scale = jnp.exp(jnp.minimum(ref - totals[:wide], CAP))
        lead = (query[rows] * lead_scale).astype(BF)
        trail = (key[:wide] * trail_scale).astype(BF)
        if kept is not None:
            leads, lead_scales, trails, trail_scales = kept
            leads[rows, :], lead_scales[rows, :] = lead, lead_scale
            trails[k, :wide, :], trail_scales[k, :wide, :] = trail, trail_scale
        part = jnp.where(allowed[rows, :wide], dot(lead, trail, NT), 0.0)
        scores[rows, :wide] = part.astype(BF)
        if wide < length:
            scores[rows, wide:] = jnp.zeros((STRIP, length - wide), BF)


def head_forward(p0, p1, p2, seen, floor, gain, scores):
    swish, gate, forget = gates(p0, p1, floor)
    allowed, tri, _ = seen
    totals = exact_dot(tri, jnp.log(forget))
    fill_scores(p0 * swish, 1.0 - forget, totals, allowed, scores)
    rec = dot(scores[...], p2.astype(BF))
    rms = lax.rsqrt(jnp.mean(rec * rec, axis=-1, keepdims=True) + epsilon)
    return (rec * rms * gain).astype(BF)


def head_backward(
    p0, p1, p2, mixed_grad, seen, carry, floor, gain, scores, key_grad, decay_grad, query_grad, *kept
):
    length = p0.shape[0]
    swish, gate, forget = gates(p0, p1, floor)
    query = p0 * swish
    key = 1.0 - forget
    allowed, tri, later = seen
    totals = exact_dot(tri, jnp.log(forget))
    fill_scores(query, key, totals, allowed, scores, kept)
    value = p2.astype(BF)
    rec = dot(scores[...], value)
    rms = lax.rsqrt(jnp.mean(rec * rec, axis=-1, keepdims=True) + epsilon)
    unit = rec * rms
    scaled = mixed_grad * gain
    rec_grad = rms * (scaled - unit * jnp.mean(scaled * unit, axis=-1, keepdims=True))
    rec_low = rec_grad.astype(BF)
    value_grad = dot(scores[...], rec_low, TN).astype(BF)
    score_grad = jnp.where(allowed, dot(rec_low, value, NT), 0.0).astype(BF)
    key_grad[...] = jnp.zeros_like(key_grad)
    decay_grad[...] = jnp.zeros_like(decay_grad)
    leads, lead_scales, trails, trail_scales = kept
    for k, (start, wide) in enumerate(strips(length)):
        rows = slice(start, start + STRIP)
        lead, lead_scale = leads[rows, :], lead_scales[rows, :]
        trail, trail_scale = trails[k, :wide, :], trail_scales[k, :wide, :]
        part = score_grad[rows, :wide]
        lead_grad = dot(part, trail)
        trail_grad = dot(part, lead, TN)
        query_grad[rows, :] = lead_grad * lead_scale
        key_grad[:wide, :] += trail_grad * trail_scale
        decay_grad[:wide, :] -= trail_grad * trail.astype(jnp.float32)
        decay_grad[rows, :] += lead_grad * lead.astype(jnp.float32)
    forget_grad = exact_dot(later, decay_grad[...]) * carry / forget
    joint = forget_grad - key_grad[...]
    floor_sum = jnp.sum(joint * (1.0 - gate), axis=0, keepdims=True)
    gain_sum = jnp.sum(mixed_grad * unit, axis=0, keepdims=True)
    g0 = (query_grad[...] * swish * (1.0 + p0 * (1.0 - swish))).astype(BF)
    g1 = (joint * (1.0 - floor) * gate * (1.0 - gate)).astype(BF)
    return g0, g1, value_grad, floor_sum, gain_sum


def load_weight(offsets_ref, sources, refs, whole, sems, begin=0):
    end = begin + whole.shape[1]
    copies = []
    for (piece, low), ref in zip(sources, refs):
        rows, lanes = ref.shape[1:]
        first, last = max(low, begin), min(low + lanes, end)
        if first >= last:
            continue
        for m in range(4):
            at = pl.multiple_of(offsets_ref[4 * piece + m], rows)
            copies.append(
                pltpu.make_async_copy(
                    ref.at[m, :, pl.ds(first - low, last - first)],
                    whole.at[pl.ds(at, rows), pl.ds(first - begin, last - first)],
                    sems.at[len(copies)],
                )
            )
    for copy in copies:
        copy.start()
    for copy in copies:
        copy.wait()


def row_copies(core, refs, whole, sems):
    count = refs[0].shape[0]
    for side in range(2):
        at = pl.multiple_of((core if side == 0 else 1 - core) * count, count)
        for m in range(4):
            ref = refs[m] if side == 0 else refs[4].at[m] if m < 3 else refs[5]
            yield m, pltpu.make_async_copy(
                ref, whole.at[m, pl.ds(at, count), :], sems.at[side, m]
            )


def start_rows(core, refs, whole, sems):
    for _, copy in row_copies(core, refs, whole, sems):
        copy.start()


def wait_rows(core, refs, whole, sems, sequence):
    for m, copy in row_copies(core, refs, whole, sems):

        @pl.when(sequence == m)
        def _():
            copy.wait()


def row_scratch(count, model):
    return [pltpu.VMEM((4, 2 * count, model), BF), pltpu.SemaphoreType.DMA((2, 4))]


def store_sends(values, send_ref, last_ref):
    sequence = pl.program_id(0)

    @pl.when(sequence < 3)
    def _():
        send_ref[0] = values.astype(BF)

    @pl.when(sequence == 3)
    def _():
        last_ref[...] = values.astype(BF)


def mixer_forward_kernel(core_ref, offsets_ref, *refs, sources):
    rows, refs = refs[:6], refs[6:]
    (col_ref, row_ref, floor_ref, gain_ref, p_ref, mixed_ref, send_ref, last_ref, keep_ref, scores, whole,
     back, tokens, token_sems, weight, sems) = refs[len(sources) :]

    sequence = pl.program_id(0)

    @pl.when(sequence == 0)
    def _():
        start_rows(core_ref[0], rows, tokens, token_sems)
        load_weight(offsets_ref, sources, refs, weight, sems)

    wait_rows(core_ref[0], rows, tokens, token_sems, sequence)

    count = rows[0].shape[0]
    width = whole.shape[1]
    mine = pl.multiple_of(core_ref[0] * count, count)
    theirs = pl.multiple_of((1 - core_ref[0]) * count, count)
    p_ref[0] = dot(tokens[sequence], weight[:, : 3 * width])
    seen = masks(col_ref[0], row_ref[0])
    for h in range(width // HEAD):
        p0, p1, p2 = [p_ref[0, :, pl.ds(j * width + h * HEAD, HEAD)] for j in range(3)]
        lanes = slice(h * HEAD, (h + 1) * HEAD)
        whole[:, lanes] = head_forward(
            p0, p1, p2, seen, floor_ref[:, lanes], gain_ref[...], scores.at[h]
        )
    mixed_ref[0] = whole[...]
    back[...] = dot(whole[...], weight[:, 3 * width :], NT)
    store_sends(back[pl.ds(theirs, count), :], send_ref, last_ref)
    keep_ref[0] = back[pl.ds(mine, count), :]


def mixer_backward_kernel(core_ref, offsets_ref, *refs, sources):
    rows, refs = refs[:6], refs[6:]
    (p_ref, col_ref, row_ref, floor_ref, gain_ref, g0_ref, g1_ref, g2_ref, send_ref, last_ref, keep_ref,
     floor_sum_ref, gain_sum_ref, scores, key_grad, decay_grad, query_grad, *kept, mixed_grad, parts,
     back, tokens, token_sems, weight, sems) = refs[len(sources) :]

    sequence = pl.program_id(0)

    @pl.when(sequence == 0)
    def _():
        start_rows(core_ref[0], rows, tokens, token_sems)
        load_weight(offsets_ref, sources, refs, weight, sems)

    wait_rows(core_ref[0], rows, tokens, token_sems, sequence)

    count = rows[0].shape[0]
    width = mixed_grad.shape[1]
    mine = pl.multiple_of(core_ref[0] * count, count)
    theirs = pl.multiple_of((1 - core_ref[0]) * count, count)
    seg_col = col_ref[0]
    before = jnp.concatenate([seg_col[:1] - 1, seg_col[:-1]], axis=0)
    carry = (seg_col == before).astype(jnp.float32)
    mixed_grad[...] = dot(tokens[sequence], weight[:, 3 * width :])
    seen = masks(col_ref[0], row_ref[0])
    for h in range(width // HEAD):
        p0, p1, p2 = [p_ref[0, :, pl.ds(j * width + h * HEAD, HEAD)] for j in range(3)]
        lanes = slice(h * HEAD, (h + 1) * HEAD)
        g0, g1, g2, floor_sum, gain_sum = head_backward(
            p0, p1, p2, mixed_grad[:, lanes], seen, carry, floor_ref[:, lanes],
            gain_ref[...], scores.at[h], key_grad.at[h], decay_grad.at[h], query_grad.at[h],
            *[ref.at[h] for ref in kept],
        )
        for j, g in enumerate((g0, g1, g2)):
            parts[:, pl.ds(j * width + h * HEAD, HEAD)] = g
        floor_sum_ref[0, :, lanes] = jnp.broadcast_to(floor_sum, (8, HEAD)) * 0.125
        gain_sum_ref[0, :, lanes] = jnp.broadcast_to(gain_sum, (8, HEAD)) * 0.125

    for j, g_ref in enumerate((g0_ref, g1_ref, g2_ref)):
        g_ref[0] = parts[:, j * width : (j + 1) * width]
    back[...] = dot(parts[...], weight[:, : 3 * width], NT)
    store_sends(back[pl.ds(theirs, count), :], send_ref, last_ref)
    keep_ref[0] = back[pl.ds(mine, count), :]


def mixer_specs(count, model, width, length):
    def at(shape, index):
        return pl.BlockSpec(shape, lambda s, c, o: index(s))

    side = [
        at((1, count, model), lambda s: (jnp.minimum(s, 2), 0, 0)),
        at((count, model), lambda s: (0, 0)),
        at((1, count, model), lambda s: (s, 0, 0)),
    ]
    col = at((1, length, 1), lambda s: (s, 0, 0))
    row = at((1, 1, length), lambda s: (s, 0, 0))
    floor = at((1, width), lambda s: (0, 0))
    gain = at((1, HEAD), lambda s: (0, 0))
    wide = at((1, length, 3 * width), lambda s: (s, 0, 0))
    pair = at((1, length, width), lambda s: (s, 0, 0))
    return at, side, wide, pair, [col, row, floor, gain]


def weight_scratch(model, lanes, sources):
    return [pltpu.VMEM((model, lanes), BF), pltpu.SemaphoreType.DMA((4 * len(sources),))]


def layout_of(sources):
    return tuple((piece, low) for piece, low, _ in sources), [part for _, _, part in sources]


def mixer_forward(core, offsets, tokens, sources, segments, floor, gain):
    groups, length, _ = segments[0].shape
    count, model = tokens[0].shape
    width = floor.shape[0]
    at, side, wide, pair, small = mixer_specs(count, model, width, length)
    layout, parts = layout_of(sources)
    shape = jax.ShapeDtypeStruct
    return pl.pallas_call(
        functools.partial(mixer_forward_kernel, sources=layout),
        grid_spec=pltpu.PrefetchScalarGridSpec(
            num_scalar_prefetch=2,
            grid=(groups,),
            in_specs=[pl.BlockSpec(memory_space=pl.ANY)] * (6 + len(parts)) + small,
            out_specs=[wide, pair] + side,
            scratch_shapes=[
                pltpu.VMEM((width // HEAD, length, length), BF),
                pltpu.VMEM((length, width), BF),
                pltpu.VMEM((length, model), jnp.float32),
            ]
            + row_scratch(count, model)
            + weight_scratch(model, 4 * width, parts),
        ),
        out_shape=[
            shape((groups, length, 3 * width), jnp.float32),
            shape((groups, length, width), BF),
            shape((groups - 1, count, model), BF),
            shape((count, model), BF),
            shape((groups, count, model), jnp.float32),
        ],
        compiler_params=PARAMS,
        cost_estimate=LONG,
        name="mixer_forward",
    )(
        core, offsets, *tokens, *parts, segments[0],
        segments[1], floor[None], gain[None],
    )


def mixer_backward(core, offsets, tokens, sources, projected, segments, floor, gain):
    groups, length, _ = segments[0].shape
    count, model = tokens[0].shape
    width = floor.shape[0]
    at, side, wide, pair, small = mixer_specs(count, model, width, length)
    layout, parts = layout_of(sources)
    heads = width // HEAD
    sums = at((1, 8, width), lambda s: (s, 0, 0))
    shape = jax.ShapeDtypeStruct
    return pl.pallas_call(
        functools.partial(mixer_backward_kernel, sources=layout),
        grid_spec=pltpu.PrefetchScalarGridSpec(
            num_scalar_prefetch=2,
            grid=(groups,),
            in_specs=[pl.BlockSpec(memory_space=pl.ANY)] * (6 + len(parts))
            + [wide]
            + small,
            out_specs=[pair] * 3 + side + [sums, sums],
            scratch_shapes=[pltpu.VMEM((heads, length, length), BF)]
            + [pltpu.VMEM((heads, length, HEAD), jnp.float32)] * 3
            + [pltpu.VMEM((heads, length, HEAD), kind) for kind in (BF, jnp.float32)]
            + [
                pltpu.VMEM((heads, length // STRIP, length, HEAD), kind)
                for kind in (BF, jnp.float32)
            ]
            + [pltpu.VMEM((length, width), jnp.float32), pltpu.VMEM((length, 3 * width), BF)]
            + [pltpu.VMEM((length, model), jnp.float32)]
            + row_scratch(count, model)
            + weight_scratch(model, 4 * width, parts),
        ),
        out_shape=[
            shape((groups, length, width), BF),
            shape((groups, length, width), BF),
            shape((groups, length, width), BF),
            shape((groups - 1, count, model), BF),
            shape((count, model), BF),
            shape((groups, count, model), jnp.float32),
        ]
        + [shape((groups, 8, width), jnp.float32)] * 2,
        compiler_params=PARAMS,
        cost_estimate=LONG,
        name="mixer_backward",
    )(
        core, offsets, *tokens, *parts, projected, segments[0],
        segments[1], floor[None], gain[None],
    )


def tops_kernel(core_ref, offsets_ref, *refs, sources):
    rows, refs = refs[:6], refs[6:]
    out_ref, tokens, token_sems, weight, sems = refs[len(sources) :]
    sequence = pl.program_id(0)

    @pl.when(sequence == 0)
    def _():
        start_rows(core_ref[0], rows, tokens, token_sems)
        load_weight(offsets_ref, sources, refs, weight, sems)

    wait_rows(core_ref[0], rows, tokens, token_sems, sequence)
    out_ref[0] = dot(tokens[sequence], weight[...])


def tops_product(core, offsets, tokens, sources, width):
    count, model = tokens[0].shape
    layout, parts = layout_of(sources)
    return pl.pallas_call(
        functools.partial(tops_kernel, sources=layout),
        grid_spec=pltpu.PrefetchScalarGridSpec(
            num_scalar_prefetch=2,
            grid=(4,),
            in_specs=[pl.BlockSpec(memory_space=pl.ANY)] * (6 + len(parts)),
            out_specs=pl.BlockSpec((1, 2 * count, width), lambda s, c, o: (s, 0, 0)),
            scratch_shapes=row_scratch(count, model) + weight_scratch(model, width, parts),
        ),
        out_shape=jax.ShapeDtypeStruct((4, 2 * count, width), jnp.float32),
        compiler_params=PARAMS,
        cost_estimate=LONG,
        name="tops_product",
    )(core, offsets, *tokens, *parts)


def ffn_kernel(core_ref, offsets_ref, *refs, sources, units):
    rows, active_grad_ref, refs = refs[:6], refs[6], refs[7:]
    (*parts, send_ref, last_ref, keep_ref, grads, back,
     tokens, token_sems, weight, sems) = refs[len(sources) :]
    sequence = pl.program_id(0)

    @pl.when(sequence == 0)
    def _():
        start_rows(core_ref[0], rows, tokens, token_sems)
        load_weight(offsets_ref, sources, refs, weight, sems, grads.shape[1] - 2 * units)

    wait_rows(core_ref[0], rows, tokens, token_sems, sequence)
    width = units
    count = rows[0].shape[0]
    mine = pl.multiple_of(core_ref[0] * count, count)
    theirs = pl.multiple_of((1 - core_ref[0]) * count, count)
    both = dot(tokens[sequence], weight[...])
    gate, up = both[:, :width], both[:, width:]
    active_grad = active_grad_ref[0, :, :width]
    squash = jax.nn.sigmoid(gate)
    swish = gate * squash
    gate_grad = active_grad * up * squash * (1.0 + gate * (1.0 - squash))
    grads[:, : 2 * width] = jnp.concatenate([gate_grad, active_grad * swish], axis=1).astype(BF)
    spare = jnp.zeros((2 * count, grads.shape[1] - 3 * width), BF)
    grads[:, 2 * width :] = jnp.concatenate([(swish * up).astype(BF), spare], axis=1)
    low = 0
    for part_ref in parts:
        part_ref[0] = grads[:, low : low + part_ref.shape[2]]
        low += part_ref.shape[2]
    back[...] = dot(grads[:, : 2 * width], weight[...], NT)
    store_sends(back[pl.ds(theirs, count), :], send_ref, last_ref)
    keep_ref[0] = back[pl.ds(mine, count), :]


def ffn(core, offsets, tokens, active_grad, sources, width, widths):
    count, model = tokens[0].shape
    groups, length = 4, 2 * count
    total = sum(widths)
    layout, parts = layout_of(sources)

    def at(rows, lanes):
        return pl.BlockSpec((1, rows, lanes), lambda s, c, o: (s, 0, 0))

    shape = jax.ShapeDtypeStruct
    return pl.pallas_call(
        functools.partial(ffn_kernel, sources=layout, units=width),
        grid_spec=pltpu.PrefetchScalarGridSpec(
            num_scalar_prefetch=2,
            grid=(groups,),
            in_specs=[pl.BlockSpec(memory_space=pl.ANY)] * 6
            + [at(length, active_grad.shape[2])]
            + [pl.BlockSpec(memory_space=pl.ANY)] * len(parts),
            out_specs=[at(length, n) for n in widths]
            + [
                pl.BlockSpec((1, count, model), lambda s, c, o: (jnp.minimum(s, 2), 0, 0)),
                pl.BlockSpec((count, model), lambda s, c, o: (0, 0)),
                at(count, model),
            ],
            scratch_shapes=[
                pltpu.VMEM((length, total), BF),
                pltpu.VMEM((length, model), jnp.float32),
            ]
            + row_scratch(count, model)
            + weight_scratch(model, 2 * width, parts),
        ),
        out_shape=[
            *[shape((groups, length, n), BF) for n in widths],
            shape((groups - 1, count, model), BF),
            shape((count, model), BF),
            shape((groups, count, model), jnp.float32),
        ],
        compiler_params=PARAMS,
        cost_estimate=LONG,
        name="ffn",
    )(core, offsets, *tokens, active_grad, *parts)


def rows_kernel(core_ref, offsets_ref, *refs, sources, begin, number):
    own, refs = refs[:number], refs[number:]
    out_ref, whole, sems = refs[len(sources) :]

    @pl.when(pl.program_id(0) == 0)
    def _():
        load_weight(offsets_ref, sources, refs, whole, sems, begin)

    out_ref[0] = dot(jnp.concatenate([r[0] for r in own], axis=1), whole[...], NT).astype(BF)


def rows_product(core, offsets, own, sources, begin, model, estimate=SHORT):
    groups, length, _ = own[0].shape
    width = sum(o.shape[2] for o in own)
    layout, parts = layout_of(sources)

    def at(rows, lanes):
        return pl.BlockSpec((1, rows, lanes), lambda s, c, o: (s, 0, 0))

    shape = jax.ShapeDtypeStruct
    return pl.pallas_call(
        functools.partial(rows_kernel, sources=layout, begin=begin, number=len(own)),
        grid_spec=pltpu.PrefetchScalarGridSpec(
            num_scalar_prefetch=2,
            grid=(groups,),
            in_specs=[at(length, o.shape[2]) for o in own] + [pl.BlockSpec(memory_space=pl.ANY)] * len(parts),
            out_specs=pl.BlockSpec((1, length, model), lambda s, c, o: (s ^ c[1], 0, 0)),
            scratch_shapes=weight_scratch(model, width, parts),
        ),
        out_shape=shape((groups, length, model), BF),
        compiler_params=PARAMS,
        cost_estimate=estimate,
        name="rows_product",
    )(core, offsets, *own, *parts)


def grad_kernel(core_ref, blocks_ref, *refs, number):
    rows, grads, outs, tokens = refs[:6], refs[6 : 6 + number], refs[6 + number : -1], refs[-1]
    count = rows[0].shape[0]
    for side in range(2):
        at = core_ref[0] if side == 0 else 1 - core_ref[0]
        for m in range(4):
            first = pl.multiple_of((2 * m + at) * count, count)
            part = rows[m][...] if side == 0 else rows[4][m] if m < 3 else rows[5][...]
            tokens[pl.ds(first, count), :] = part
    for grad_ref, out_ref in zip(grads, outs):
        out_ref[0] = dot(tokens[...], grad_ref[...], TN).astype(out_ref.dtype)


def grad_product(core, tokens, grads, blocks, wide, kind, estimate):
    count, model = tokens[0].shape
    side = pl.BlockSpec((count, wide), lambda i, c, b: (0, b[i]))
    three = pl.BlockSpec((3, count, wide), lambda i, c, b: (0, 0, b[i]))
    number = blocks.shape[0]
    return pl.pallas_call(
        functools.partial(grad_kernel, number=len(grads)),
        grid_spec=pltpu.PrefetchScalarGridSpec(
            num_scalar_prefetch=2,
            grid=(number,),
            in_specs=[side] * 4
            + [three, side]
            + [pl.BlockSpec(g.shape, lambda i, c, b: (0, 0)) for g in grads],
            out_specs=[pl.BlockSpec((1, wide, g.shape[1]), lambda i, c, b: (i, 0, 0)) for g in grads],
            scratch_shapes=[pltpu.VMEM((8 * count, wide), BF)],
        ),
        out_shape=[jax.ShapeDtypeStruct((number, wide, g.shape[1]), kind) for g in grads],
        compiler_params=PARAMS,
        cost_estimate=estimate,
        name="grad_product",
    )(core, blocks, *tokens, *grads)


def rms_of(values):
    return lax.rsqrt(jnp.mean(values * values, axis=-1, keepdims=True) + epsilon)


def last_kernel(keep_ref, came_ref, out_ref):
    out_ref[...] = (keep_ref[0] + came_ref[...].astype(jnp.float32)).astype(BF)


def add_last(keep, came):
    count, model = came.shape
    block = count
    return pl.pallas_call(
        last_kernel,
        grid=(1,),
        in_specs=[
            pl.BlockSpec((1, block, model), lambda i: (3, i, 0)),
            pl.BlockSpec((block, model), lambda i: (i, 0)),
        ],
        out_specs=pl.BlockSpec((block, model), lambda i: (i, 0)),
        out_shape=jax.ShapeDtypeStruct(came.shape, BF),
        compiler_params=PARAMS,
        cost_estimate=SHORT,
        name="add_last",
    )(keep, came)


def cores_kernel(keep_ref, came_ref, own_ref, x_ref, z_ref):
    own_ref[...] = keep_ref[0] + came_ref[0].astype(jnp.float32)
    for m, out_ref in enumerate((x_ref, z_ref), 1):
        out_ref[...] = (keep_ref[m] + came_ref[m].astype(jnp.float32)).astype(BF)


def add_cores(keep, came):
    count, model = keep.shape[1:]
    block = count // 2
    three = pl.BlockSpec((3, block, model), lambda i: (0, i, 0))
    one = pl.BlockSpec((block, model), lambda i: (i, 0))
    shape = jax.ShapeDtypeStruct
    return pl.pallas_call(
        cores_kernel,
        grid=(2,),
        in_specs=[three, three],
        out_specs=[one] * 3,
        out_shape=[shape((count, model), jnp.float32)] + [shape((count, model), BF)] * 2,
        compiler_params=PARAMS,
        cost_estimate=SHORT,
        name="add_cores",
    )(keep, came)


def middle_kernel(own_ref, x_ref, z_ref, hidden_ref, gain_ref, middle_ref, normed_ref):
    branch = own_ref[...] + x_ref[...].astype(jnp.float32) + z_ref[...].astype(jnp.float32)
    middle = hidden_ref[...].astype(jnp.float32) + branch
    middle_ref[...] = middle
    normed_ref[...] = (middle * rms_of(middle) * gain_ref[...]).astype(BF)


def back_kernel(own_ref, x_ref, z_ref, values_ref, add_ref, gain_ref, out_ref, low_ref, sum_ref):
    grad = own_ref[...] + x_ref[...].astype(jnp.float32) + z_ref[...].astype(jnp.float32)
    values = values_ref[...].astype(jnp.float32)
    scale = rms_of(values)
    unit = values * scale
    wide = grad * gain_ref[...]
    inner = wide - unit * jnp.mean(wide * unit, axis=-1, keepdims=True)
    out = add_ref[...].astype(jnp.float32) + scale * inner
    out_ref[...] = out
    low_ref[...] = out.astype(BF)

    @pl.when(pl.program_id(0) == 0)
    def _():
        sum_ref[...] = jnp.zeros_like(sum_ref)

    sum_ref[...] += jnp.sum(grad * unit, axis=0, keepdims=True)


def row_call(kernel, name, kinds, *args):
    count, model = args[0].shape
    block = count // 4

    def spec(one):
        if one:
            return pl.BlockSpec((1, model), lambda i: (0, 0))
        return pl.BlockSpec((block, model), lambda i: (i, 0))

    shapes = [jax.ShapeDtypeStruct((1 if k is None else count, model), k or jnp.float32) for k in kinds]
    return pl.pallas_call(
        kernel,
        grid=(4,),
        in_specs=[spec(a.shape[0] == 1) for a in args],
        out_specs=[spec(k is None) for k in kinds],
        out_shape=shapes,
        compiler_params=PARAMS,
        cost_estimate=LONG,
        name=name,
    )(*args)


def mix_grad_kernel(parts_ref, out_ref):
    quarter = parts_ref.shape[2] // 4
    for j, at in enumerate((1, 3, 0, 2)):
        for m in range(4):
            part = parts_ref[m, :, at * quarter : (at + 1) * quarter]
            out_ref[:, j, m * quarter : (m + 1) * quarter] = part.astype(jnp.float32)


def mix_grad_of(parts):
    _, rows, wide = parts.shape
    block = min(rows, 64)
    return pl.pallas_call(
        mix_grad_kernel,
        grid=(rows // block,),
        in_specs=[pl.BlockSpec((4, block, wide), lambda i: (0, i, 0))],
        out_specs=pl.BlockSpec((block, 4, wide), lambda i: (i, 0, 0)),
        out_shape=jax.ShapeDtypeStruct((rows, 4, wide), jnp.float32),
        compiler_params=PARAMS,
        cost_estimate=SHORT,
        name="mix_grad",
    )(parts)


DOWN_FIRST = 256


def ffn_grad_kernel(first_ref, second_ref, out_ref):
    units = out_ref.shape[2] // 4
    for j in range(3):
        parts = []
        for m in range(4):
            down = first_ref.shape[2] - DOWN_FIRST
            gates = jnp.concatenate([first_ref[m, :, down:], second_ref[m]], axis=1)
            parts.append(first_ref[m, :, :units] if j == 2 else gates[:, j * units : (j + 1) * units])
        out_ref[j] = jnp.concatenate(parts, axis=1).astype(jnp.float32)


def ffn_grad_of(parts, units):
    rows = parts[0].shape[1]
    block = min(rows, 32)
    out = pl.pallas_call(
        ffn_grad_kernel,
        grid=(rows // block,),
        in_specs=[pl.BlockSpec((4, block, p.shape[2]), lambda i: (0, i, 0)) for p in parts],
        out_specs=pl.BlockSpec((3, block, 4 * units), lambda i: (0, i, 0)),
        out_shape=jax.ShapeDtypeStruct((3, rows, 4 * units), jnp.float32),
        compiler_params=PARAMS,
        cost_estimate=LONG,
        name="ffn_grad",
    )(*parts)
    return out.transpose(1, 0, 2)


def near_kernel(*refs, number):
    home_ref, away_ref = refs[2 * number :]
    at_home = pl.program_id(0) == pl.num_programs(0) - 1
    low = 0
    for keep_ref, came_ref in zip(refs[: 2 * number : 2], refs[1 : 2 * number : 2]):
        lanes = slice(low, low + keep_ref.shape[2])
        low += keep_ref.shape[2]

        @pl.when(jnp.logical_not(at_home))
        def _():
            total = keep_ref[...] + came_ref[...].astype(jnp.float32)
            away_ref[:, :, lanes] = total.astype(BF)

        @pl.when(at_home)
        def _():
            home_ref[:, :, lanes] = keep_ref[...] + came_ref[...].astype(jnp.float32)


def near_sums(pairs, estimate=SHORT):
    highs = lax.axis_size("h")
    blocks, rows, _ = pairs[0][0].shape
    wide = sum(keep.shape[2] for keep, _ in pairs)
    specs, args = [], []
    for pair in pairs:
        specs += [pl.BlockSpec((2,) + pair[0].shape[1:], lambda i: (i, 0, 0))] * 2
        args += list(pair)
    home, away = pl.pallas_call(
        functools.partial(near_kernel, number=len(pairs)),
        grid=(highs,),
        in_specs=specs,
        out_specs=[
            pl.BlockSpec((2, rows, wide), lambda i: (0, 0, 0)),
            pl.BlockSpec((2, rows, wide), lambda i: (jnp.minimum(i, highs - 2), 0, 0)),
        ],
        out_shape=[
            jax.ShapeDtypeStruct((2, rows, wide), jnp.float32),
            jax.ShapeDtypeStruct((blocks - 2, rows, wide), BF),
        ],
        compiler_params=PARAMS,
        cost_estimate=estimate,
        name="near_sums",
    )(*args)
    return home, [away[2 * k : 2 * k + 2] for k in range(highs - 1)]


def far_kernel(*refs, counts):
    out_ref = refs[-1]
    low, at = 0, 0
    for count in counts:
        total = refs[at][0]
        for ref in refs[at + 1 : at + 1 + count]:
            total = total + ref[0].astype(jnp.float32)
        out_ref[0, :, low : low + total.shape[1]] = total.astype(BF)
        low, at = low + total.shape[1], at + 1 + count


def far_sums(pairs, estimate=SHORT):
    _, rows, _ = pairs[0][0].shape
    wide = sum(home.shape[2] for home, _ in pairs)
    args = [part for home, fars in pairs for part in (home, *fars)]
    out = pl.pallas_call(
        functools.partial(far_kernel, counts=[len(fars) for _, fars in pairs]),
        grid=(2,),
        in_specs=[pl.BlockSpec((1,) + a.shape[1:], lambda i: (i, 0, 0)) for a in args],
        out_specs=pl.BlockSpec((1, rows, wide), lambda i: (i, 0, 0)),
        out_shape=jax.ShapeDtypeStruct((2, rows, wide), BF),
        compiler_params=PARAMS,
        cost_estimate=estimate,
        name="far_sums",
    )(*args)
    return out.reshape(4, rows // 2, wide)


GROUP = ("l", "x")


def swap(values, axes):
    total = 2 ** len(axes)
    return lax.ppermute(values, axes, [(s, total - 1 - s) for s in range(total)])


def shift(values, steps):
    total = lax.axis_size("h")
    return lax.ppermute(values, "h", [(s, (s + steps) % total) for s in range(total)])


def pick(values, index):
    return lax.dynamic_index_in_dim(values, index, 0, keepdims=False)


def over_c(values):
    return swap(values, ("tensor",))


def over_x(values):
    return swap(values, ("x",))


def over_y(values):
    return swap(values, ("y",))


def over_z(values):
    return swap(values, ("l",))


def own_member():
    return lax.axis_index("l") * 2 + lax.axis_index("x")


def source_rows(rows):
    y, high = lax.axis_index("y"), lax.axis_index("h")
    highs = lax.axis_size("h")
    starts = []
    for k in range(highs):
        for side in (y, 1 - y):
            for member in range(4):
                block = ((high - k) % highs) * 8 + (member >> 1) * 4 + side * 2 + (member & 1)
                starts.append(block * rows)
    return jnp.stack(starts).astype(jnp.int32)


def trade(slices):
    return lax.all_to_all(slices, GROUP, 0, 0, tiled=True)


def after(values, *others):
    return lax.optimization_barrier((values, others))[0]


def far(block):
    return [shift(block, k) for k in range(1, lax.axis_size("h"))]


def near(parts):
    return [over_y(part) for part in parts]


def pieces(low, straight, crossed):
    out = []
    for k, (one, two) in enumerate(zip(straight, crossed), 1):
        out += [(2 * k, low, one), (2 * k + 1, low, two)]
    return out


def half_grads(core, tokens, grads, yy, kind, estimate):
    highs, high = lax.axis_size("h"), lax.axis_index("h")
    wide = tokens[0].shape[1] // (4 * highs)
    order = [(high + k) % highs for k in range(1, highs)] + [high]
    blocks = jnp.stack([(h * 2 + z) * 2 + yy for h in order for z in range(2)]).astype(jnp.int32)
    grads = [flat(g) for g in grads]
    if wide % 128 == 0:
        return grad_product(core, tokens, grads, blocks, wide, kind, estimate)
    sides = [jnp.stack(tokens[:4]), jnp.concatenate([tokens[4], tokens[5][None]])]
    ordered = [jnp.where(core[0] == 0, a, b) for a, b in (sides, sides[::-1])]
    whole = jnp.stack(ordered, axis=1)
    split = jnp.take(whole.reshape(grads[0].shape[0], -1, wide), blocks, axis=1)
    return [
        jnp.einsum("tad,tx->adx", split, g, preferred_element_type=jnp.float32).astype(kind)
        for g in grads
    ]


def grad_sends(core, tokens, grads, estimate=SHORT):
    return half_grads(core, tokens, grads, 1 - lax.axis_index("y"), BF, estimate)


def grad_keeps(core, tokens, grads, estimate=SHORT):
    return half_grads(core, tokens, grads, lax.axis_index("y"), jnp.float32, estimate)


def send_far(away):
    return [shift(part, k) for k, part in enumerate(away, 1)]


def flat(values):
    return values.reshape(-1, values.shape[-1])


def add_low(keep, came):
    return (keep.astype(jnp.float32) + came.astype(jnp.float32)).astype(BF)


def sum_pair(values, first, second):
    parts = [values, swap(values, (second,)), swap(values, (first,)), swap(values, (first, second))]
    return jnp.stack(parts), lax.axis_index(first) * 2 + lax.axis_index(second)


def add_pair(parts, place):
    return sum(pick(parts, place ^ m) for m in range(4))


def sum_highs(values):
    size, bits = lax.axis_size("h"), 1
    while bits < size:
        values = values + lax.ppermute(values, "h", [(s, s ^ bits) for s in range(size)])
        bits *= 2
    return values


def body(
    hidden_in,
    segments,
    mix_weights,
    ffn_weights,
    norm1_gain,
    norm2_gain,
    head_gain,
    lower_bound,
    out_grad,
):
    core, member = lax.axis_index("tensor"), own_member()
    core_at = jnp.stack([core, member]).astype(jnp.int32)
    rows = mix_weights.shape[0]
    offsets = source_rows(rows)
    quarter, units = lower_bound.shape[0] // 4, ffn_weights.shape[2] // 4
    model = hidden_in.shape[1]
    channels = 4 * quarter
    lanes = -(-3 * units // 128) * 128

    def slices(weights, width):
        split = weights.reshape(rows, weights.shape[1], 4, -1).transpose(2, 0, 1, 3)
        split = split.reshape(4, rows, -1)
        return jnp.pad(split, ((0, 0), (0, 0), (0, width - split.shape[2])))

    length = segments.shape[1]
    labels = jnp.pad(segments.astype(BF), ((0, 15), (0, channels - length)))
    labels = jnp.broadcast_to(labels, (4,) + labels.shape)
    hidden = hidden_in.astype(jnp.float32)
    scale_one = rms_of(hidden)
    normed = (hidden * scale_one * norm1_gain).astype(BF)
    floor = lax.dynamic_slice_in_dim(lower_bound, member * quarter, quarter)
    feed = slices(ffn_weights, 3 * units)
    spare = lanes - 3 * units
    down = jnp.pad(feed[..., 2 * units :], ((0, 0), (0, 0), (0, spare)))
    feed = jnp.concatenate([down, feed[..., : 2 * units]], axis=-1)
    mix = slices(mix_weights, channels)

    mix = trade(jnp.concatenate([slices(mix_weights, channels), labels], axis=1))

    gate = (mix, normed, feed)
    mix, normed, feed = lax.optimization_barrier(gate)
    labels = mix[:, rows, :length].astype(jnp.int32)
    labels = jnp.stack([pick(labels, member ^ m) for m in range(4)])
    mix = mix[:, :rows]
    cuts = [0, 512, 1024, 1152, 1408, 1664, 1920, lanes]
    feed_cut = cuts[4]
    mix_far = far(mix)
    mix_near = over_y(mix)
    feed_one = trade(feed[..., :feed_cut])
    feed_rest = after(feed[..., feed_cut:], gate)
    normed_x, normed_z = over_x(normed), over_z(normed)
    top_x = over_x(after(out_grad, gate))

    columns = jnp.broadcast_to(labels[:, :, None], labels.shape + (1,))
    gate = (mix_far, mix_near, feed_one, feed_rest, normed_x, normed_z, top_x, floor, columns)
    floor = after(floor, gate)
    labels = (after(columns, gate), labels[:, None, :])
    mix_cross = near(after(mix_far, gate))
    ones = [feed_one[..., low:high] for low, high in zip(cuts[:4], cuts[1:5])]
    far_a = far(after(ones[0], gate))
    normed_xz = over_x(after(normed_z, gate))
    normed_three = jnp.stack(after([normed, normed_x, normed_z], gate))
    top_z = over_z(after(out_grad, gate))
    near_a = over_y(after(feed_one[..., :256], gate))

    gate = (mix_cross, far_a, normed_xz, normed_three, top_z, ones, near_a)
    normed_c, normed_cxz = over_c(after(normed_three, gate)), over_c(after(normed_xz, gate))
    normed = [normed, normed_x, normed_z, normed_xz, normed_c, normed_cxz]
    mix_sources = [(0, 0, mix), (1, 0, mix_near)] + pieces(0, mix_far, mix_cross)

    gate = (normed_c, normed_cxz)
    far_b = far(after(ones[1], gate))
    near_b = over_y(after(feed_one[..., 256:768], gate))
    cross_a = near(after(far_a, gate))
    top_xz = over_x(after(top_z, gate))
    feed_two = trade(after(feed_rest, gate))
    projected, mixed, send, send_xz, keep = mixer_forward(
        core_at, offsets, after(normed, gate), mix_sources, labels, floor, head_gain
    )

    gate = (send, far_b, near_b, cross_a, top_xz, feed_two)
    came_xz = over_c(after(send_xz, gate))
    came = over_c(after(send, gate))
    near_c = over_y(after(feed_one[..., 768:1024], gate))
    top_cxz = over_c(after(top_xz, gate))
    top_three = jnp.stack(after([out_grad, top_x, top_z], gate))
    far_c = far(after(ones[2], gate))
    to_xz = add_last(keep, came_xz)

    gate = (to_xz, near_c, far_c, top_cxz, top_three)
    from_x = over_x(after(to_xz, gate))
    far_d = far(after(ones[3], gate))
    cross_b = near(after(far_b, gate))
    own, to_x, to_z = add_cores(keep, after(came, gate))
    top_c = over_c(after(top_three, gate))
    tops = [out_grad, top_x, top_z, top_xz, top_c, top_cxz]

    gate = (from_x, far_d, cross_b, own, top_c)
    to_z = add_low(to_z, after(from_x, gate))
    of_x = over_x(after(to_x, gate))
    of_z = over_z(to_z)
    far_e = far(after(feed_two[..., : cuts[5] - feed_cut], gate))
    near_d = over_y(after(feed_one[..., 1024:], gate))
    near_e = over_y(after(feed_two[..., :384], gate))

    gate = (of_x, of_z, far_e, near_d, near_e)
    far_f = far(after(feed_two[..., cuts[5] - feed_cut : cuts[6] - feed_cut], gate))
    near_f = over_y(after(feed_two[..., 384:], gate))
    cross_cd = [
        over_y(jnp.concatenate([one, two], axis=-1))
        for one, two in zip(after(far_c, gate), after(far_d, gate))
    ]
    middle, normed_two = row_call(
        middle_kernel, "middle", [jnp.float32, BF], *after((own, of_x, of_z), gate), hidden_in,
        norm2_gain[None],
    )
    two_x, two_z = over_x(normed_two), over_z(normed_two)
    down_sources = [(0, 0, feed_one), (1, 0, near_a), (1, 256, near_b)]
    for low, straight, crossed in zip(cuts, [far_a, far_b], [cross_a, cross_b]):
        down_sources += pieces(low, straight, crossed)
    active_grad = tops_product(
        core_at, offsets, after(tops, normed_two), down_sources, lanes - 2 * units
    )

    gate = (far_f, near_f, cross_cd, two_x, two_z, active_grad)
    far_g = far(after(feed_two[..., cuts[6] - feed_cut :], gate))
    cross_e, cross_f = near(after(far_e, gate)), near(after(far_f, gate))
    two_xz = over_x(after(two_z, gate))
    two_three = jnp.stack(after([normed_two, two_x, two_z], gate))

    gate = (far_g, cross_e, cross_f, two_xz, two_three)
    cross_g = near(after(far_g, gate))
    two_c, two_cxz = over_c(after(two_three, gate)), over_c(after(two_xz, gate))
    normed_two = [normed_two, two_x, two_z, two_xz, two_c, two_cxz]
    feed_sources = [(0, 0, feed_one), (0, feed_cut, feed_two)]
    feed_sources += [(1, 0, near_a), (1, 256, near_b), (1, 768, near_c), (1, 1024, near_d)]
    feed_sources += [(1, feed_cut, near_e), (1, feed_cut + 384, near_f)]
    fars = [far_a, far_b, far_c, far_d, far_e, far_f, far_g]
    for low, part in zip(cuts, fars):
        feed_sources += [(2 * k, low, one) for k, one in enumerate(part, 1)]
    crosses = [cross_a, cross_b, cross_cd, cross_e, cross_f, cross_g]
    for low, part in zip(cuts[:3] + cuts[4:], crosses):
        feed_sources += [(2 * k + 1, low, one) for k, one in enumerate(part, 1)]

    widths = [256, 128, 384, 256, 256, 128, 256, 256, lanes - 1920]
    *grads, send, send_xz, keep = ffn(
        core_at, offsets, normed_two, active_grad, feed_sources, units, widths
    )
    gates, downs = grads[:6], grads[6:]
    came_xz, came = over_c(send_xz), over_c(send)
    down_sends = grad_sends(core_at, after(tops, send), downs, LONG)
    to_xz = add_last(keep, after(came_xz, down_sends))

    gate = (to_xz,)
    from_x = over_x(after(to_xz, gate))
    down_one = over_y(after(down_sends[0], gate))
    gate_sends = grad_sends(core_at, after(normed_two, gate), gates, LONG)
    own, to_x, to_z = add_cores(keep, after(came, gate_sends))

    gate = (from_x, down_one, own)
    to_z = add_low(to_z, after(from_x, gate))
    of_x = over_x(after(to_x, gate))
    of_z = over_z(to_z)
    down_two = over_y(after(down_sends[1], gate))
    down_keeps = grad_keeps(core_at, after(tops, gate), downs, LONG)
    down_home, down_away = near_sums([(down_keeps[0], after(down_one, gate))])

    gate = (of_x, of_z, down_two, down_away)
    down_fars = send_far(after(down_away, gate))
    down_three = over_y(after(down_sends[2], gate))
    two_came = over_y(after(gate_sends[1], gate))
    middle_grad, middle_low, gain_two_grad = row_call(
        back_kernel, "middle_grad", [jnp.float32, BF, None], *after((own, of_x, of_z), gate),
        middle, out_grad, norm2_gain[None],
    )
    grad_x, grad_z = over_x(middle_low), over_z(middle_low)
    gate_keeps = grad_keeps(core_at, after(normed_two, middle_low), gates, LONG)
    down_home_two, down_away_two = near_sums(
        [(after(down_keeps[1], gate_keeps), after(down_two, gate))]
    )

    gate = (grad_x, grad_z, down_three, two_came, down_away_two, down_fars)
    down_fars_two = send_far(after(down_away_two, gate))
    one_came = over_y(after(gate_sends[0], gate))
    grad_xz = over_x(after(grad_z, gate))
    grad_three = jnp.stack(after([middle_low, grad_x, grad_z], gate))
    branch = rows_product(
        core_at, offsets, after(downs, gate), down_sources, 0, model, LONG
    )

    gate = early = (grad_xz, grad_three, branch, down_fars_two, one_came)
    grad_c, grad_cxz = over_c(after(grad_three, gate)), over_c(after(grad_xz, gate))
    one_home, one_away = near_sums(
        [
            (down_keeps[2], after(down_three, gate)),
            (gate_keeps[0], after(one_came, gate)),
        ],
        LONG,
    )
    middle_full = [middle_low, grad_x, grad_z, grad_xz, grad_c, grad_cxz]

    gate = (grad_c, grad_cxz, one_away)
    one_fars = send_far(after(one_away, gate))
    three_came, four_came = [over_y(after(part, early)) for part in gate_sends[2:4]]
    branch = lax.psum_scatter(
        after(branch, gate).reshape(-1, model), GROUP + ("tensor",), scatter_dimension=0, tiled=True
    )
    middle_full = after(middle_full, gate)
    *mix_grads, send, send_xz, keep, floor_sums, gain_sums = mixer_backward(
        core_at, offsets, middle_full, mix_sources, projected, labels, floor, head_gain
    )

    gate = (send, one_fars, three_came, four_came)
    came_xz, came = over_c(after(send_xz, gate)), over_c(after(send, gate))
    five_came = over_y(after(gate_sends[4], gate))
    three_home, three_away = near_sums(
        [(gate_keeps[1], after(two_came, gate)), (gate_keeps[2], three_came)], LONG
    )
    to_xz = add_last(keep, after(came_xz, three_away))

    gate = (to_xz,)
    three_fars = send_far(after(three_away, gate))
    from_x = over_x(after(to_xz, gate))
    six_came = over_y(after(gate_sends[5], gate))
    query_send, forget_send, value_send = grad_sends(core_at, after(normed, gate), mix_grads, LONG)
    own, to_x, to_z = add_cores(keep, after(came, value_send))
    four_home, four_away = near_sums(
        [
            (gate_keeps[3], after(four_came, own)),
            (gate_keeps[4], five_came),
            (gate_keeps[5], six_came),
        ]
    )

    gate = (from_x, three_fars, four_away)
    four_fars = send_far(after(four_away, gate))
    to_z = add_low(to_z, after(from_x, gate))
    of_x = over_x(after(to_x, gate))
    of_z = over_z(to_z)
    value_came, query_came = over_y(after(value_send, gate)), over_y(after(query_send, gate))
    query_keep, forget_keep, value_keep = grad_keeps(core_at, after(normed, gate), mix_grads, LONG)
    (last_send,) = grad_sends(core_at, after(middle_full, value_keep), [mixed])
    down_parts = [(down_home, down_fars), (down_home_two, down_fars_two), (one_home, one_fars)]
    down_parts = far_sums(after(down_parts, last_send))
    near_home, near_away = near_sums(
        [(value_keep, after(value_came, down_parts)), (query_keep, query_came)]
    )

    gate = (of_x, of_z, four_fars, near_away)
    near_fars = send_far(after(near_away, gate))
    last_came, forget_came = over_y(after(last_send, gate)), over_y(after(forget_send, gate))
    down_parts = trade(after(down_parts, gate))
    input_grad, _, gain_one_grad = row_call(
        back_kernel, "input_grad", [jnp.float32, BF, None], *after((own, of_x, of_z), gate),
        hidden_in, middle_grad, norm1_gain[None],
    )
    (last_keep,) = grad_keeps(core_at, after(middle_full, input_grad), [mixed])
    head_grad = jnp.sum(after(gain_sums, gate).reshape(-1, HEAD), axis=0)
    lower_grad = jnp.zeros((2, 4, quarter), jnp.float32)
    lower_grad = lax.dynamic_update_slice(
        lower_grad,
        jnp.sum(after(floor_sums, gate), axis=(0, 1)).reshape(1, 1, quarter),
        (core, member, 0),
    )
    sums = [gain_one_grad[0], gain_two_grad[0], head_grad, lower_grad.reshape(-1)]
    sums = jnp.concatenate(sums).reshape(-1, HEAD)
    block_out = (middle + after(branch, last_keep).astype(jnp.float32)).astype(BF)
    gate_parts = [(three_home, three_fars), (four_home, four_fars)]
    gate_parts = far_sums(after(gate_parts, block_out))
    pair_home, pair_away = near_sums(
        [(last_keep, after(last_came, gate_parts)), (forget_keep, forget_came)]
    )

    gate = (near_fars, down_parts, sums, pair_away, gate_parts, block_out)
    pair_fars = send_far(after(pair_away, gate))
    gate_parts = trade(after(gate_parts, gate))
    sums, place = sum_pair(after(sums, gate), "l", "x")

    gate = (pair_fars, gate_parts, sums)
    mix_parts = far_sums(after([(near_home, near_fars), (pair_home, pair_fars)], gate))
    sums, place = sum_pair(add_pair(after(sums, mix_parts), place), "y", "tensor")
    sums = sum_highs(add_pair(sums, place)).reshape(-1)
    mix_parts = trade(mix_parts)
    gain_one, gain_two, head, lower = jnp.split(sums, [model, 2 * model, 2 * model + HEAD])
    ffn_grad = ffn_grad_of(after([down_parts, gate_parts], gate), units)
    mix_grad = mix_grad_of(mix_parts)
    return (block_out, input_grad, mix_grad, ffn_grad, gain_one, gain_two, head, lower)


def solution(mesh):
    total, cores = mesh.shape["dp"], mesh.shape["tensor"]
    fine = Mesh(mesh.devices.reshape(total // 8, 2, 2, 2, cores), ("h", "l", "y", "x", "tensor"))
    dp = ("h", "l", "y", "x")
    rows = P(dp + ("tensor",), None)
    weights = P(dp, None, "tensor")
    return jax.shard_map(
        body,
        mesh=fine,
        in_specs=(rows, P(dp, None), weights, weights, P(), P(), P(), P("tensor"), rows),
        out_specs=(rows, rows, weights, weights, P(), P(), P(), P()),
        check_vma=False,
    )
```
